256 devices in a mesh: cols: 8 (over x, core), rows: 32 (over z, y).
Axes of the slice: x: 4, y: 4, z: 8, core: 2. Of those that a mesh axis runs over, the one named last changes fastest.
Arguments:
- rhs_leaf: bfloat16 [32768, 2048], P('rows', 'cols'), parts along dimension 1, may hold values from -6 to 6
- rhs_sep: bfloat16 [16384, 2048], P('rows', 'cols'), parts along dimension 1, may hold values from -6 to 6
- leaf_inv: bfloat16 [32768, 1024], P('rows'), may hold values from -1.5 to 1.5, as said below
- leaf_cpl: bfloat16 [32, 5, 128, 1024], P('rows'), may hold values from -0.09375 to 0.09375
- leaf_idx: int32 [32, 5, 128], P('rows'), may hold values from 0 to 511, as said below
- sep_inv: bfloat16 [16384, 512], P('rows'), may hold values from -1.5 to 1.5, as said below
- sep_cpl: bfloat16 [32, 4, 128, 512], P('rows'), may hold values from -0.125 to 0.125
- sep_idx: int32 [32, 4, 128], P('rows'), may hold values from 0 to 511, as said below
- stay_dofs: int32 [6, 2048], replicated, may hold values from 0 to 32767, as said below
- stay_coef: float32 [6, 2048], replicated, may hold values from -1 to 1
Outputs:
- disp_leaf: bfloat16 [32768, 2048], P('rows', 'cols'), parts along dimension 1
- disp_sep: bfloat16 [16384, 2048], P('rows', 'cols'), parts along dimension 1
- stretch: float32 [2048, 2048], P('rows', 'cols'), parts along dimension 1
The draws below stay inside these ranges and needn't reach their ends.
There are 8 independent parts, one for each index of `cols`. The reference program is written for one: setup_inputs(seed, part) draws one part's arguments, and reference() takes and returns one part's arrays. A program takes and returns all parts, laid end to end along the dimension named above; an argument that names none is the same for every part. Nothing has to cross between parts.
Inputs may be any that keep to these rules, and one draw needn't show every extreme that they name: `leaf_inv`: each block of 1024 rows is lower triangular with a diagonal between 0.5 and 1.5. `sep_inv`: each block of 512 rows is lower triangular with a diagonal between 0.5 and 1.5. `leaf_idx`: the 128 rows of one subtree and level are distinct. `sep_idx`: the 128 rows of one separator and slot are distinct; slots beyond a separator's ancestors are not read. `stay_dofs`: stay e is collected by device e // 64. Of the 6 * 64 (component, stay) pairs of one device's stays, at most 12 name unknowns of any one subtree, and subtree 0 is named by exactly 12 of them.
All inputs are finite; a program needn't handle non-finite values.
Results may differ from the reference program's by a relative error of at most 0.014.
Values may be sent and summed in bfloat16 or wider, within the bound.
No kernel may reach another device: no remote copies, remote signals or barrier semaphores. Data moves between devices by JAX's collectives and lax.ppermute only.
A program may use at most 128 MiB of HBM per device.

```python
import jax
import jax.numpy as jnp
from jax import lax

LEAF = 1024
P_SIZE = 512
U = 128
NC = 256
S_DEV = 64
K = 6
LEVELS = 5
STAYS = 2048
N_ROWS = 32


def triangle(key, row_count, matrix_order):
    key_off, key_diag = jax.random.split(key)
    row_pos = lax.broadcasted_iota(jnp.int32, (row_count, matrix_order), 0) % matrix_order
    col_pos = lax.broadcasted_iota(jnp.int32, (row_count, matrix_order), 1)
    off_part = jax.random.truncated_normal(key_off, -4.0, 4.0, (row_count, matrix_order), jnp.float32) * 0.6 * (1.0 / matrix_order) ** 0.5
    diag_part = jax.random.uniform(key_diag, (row_count, matrix_order), jnp.float32, 0.7, 1.3)
    lower = jnp.where(col_pos < row_pos, off_part, 0.0)
    return jnp.where(col_pos == row_pos, diag_part, lower)


def chosen_rows(key, row_count):
    keys = jax.random.split(key, row_count)
    picked = jax.vmap(lambda one_key: jax.random.permutation(one_key, P_SIZE)[:U])(keys)
    return picked.astype(jnp.int32)


def draw_leaf_inv(key, part):
    return triangle(jax.random.fold_in(key, 13), N_ROWS * LEAF, LEAF).astype(jnp.bfloat16)


def draw_sep_inv(key, part):
    return triangle(jax.random.fold_in(key, 14), N_ROWS * P_SIZE, P_SIZE).astype(jnp.bfloat16)


def draw_leaf_idx(key, part):
    return chosen_rows(jax.random.fold_in(key, 11), N_ROWS * LEVELS).reshape(N_ROWS, LEVELS, U)


def draw_sep_idx(key, part):
    return chosen_rows(jax.random.fold_in(key, 12), N_ROWS * (LEVELS - 1)).reshape(N_ROWS, LEVELS - 1, U)


def draw_stay_dofs(key, part):
    key_perm, key_row = jax.random.split(jax.random.fold_in(key, 15))
    pair_count = K * S_DEV
    owner_keys = jax.random.split(key_perm, N_ROWS)
    shuffled = jax.vmap(lambda one_key: jax.random.permutation(one_key, pair_count))(owner_keys)
    source = shuffled.astype(jnp.int32) % N_ROWS
    offset = jax.random.randint(key_row, (N_ROWS, pair_count), 0, LEAF, jnp.int32)
    dofs = source * LEAF + offset
    return dofs.reshape(N_ROWS, K, S_DEV).transpose(1, 0, 2).reshape(K, N_ROWS * S_DEV).astype(jnp.int32)


def block_scale(key, shape, cuts, smallest, high):
    factor_of, own = 1.0, jax.random.fold_in(key, 6)
    for dim, parts in cuts:
        steps = jnp.exp(jax.random.uniform(jax.random.fold_in(own, dim), (parts,), jnp.float32, smallest / len(cuts), high / len(cuts)))
        factor_of = factor_of * jnp.repeat(steps, shape[dim] // parts).reshape([-1 if axis == dim else 1 for axis in range(len(shape))])
    return factor_of


def scatter_about(own_key, shape, scale, bound, cuts=(), held_as=jnp.bfloat16):
    factor_of = block_scale(own_key, shape, cuts, -0.22, 0.18) if cuts else 1.0
    drawn = jax.random.normal(own_key, shape, jnp.float32) * scale * factor_of
    return jnp.minimum(jnp.maximum(drawn, -bound), bound).astype(held_as)


def setup_inputs(seed: int = 0, part: int = 0) -> dict:
    splits = jax.random.split(jax.random.key(seed), 11)
    part_splits = jax.random.split(jax.random.fold_in(splits[10], part), 11)
    return {
        "rhs_leaf": scatter_about(part_splits[0], (N_ROWS * LEAF, NC), 1.0, 6.0, ((0, 32),)),
        "rhs_sep": scatter_about(part_splits[1], (N_ROWS * P_SIZE, NC), 1.0, 6.0, ((0, 32),)),
        "leaf_inv": draw_leaf_inv(jax.random.fold_in(splits[10], 71), part),
        "leaf_cpl": scatter_about(splits[3], (N_ROWS, LEVELS, U, LEAF), (4 * LEAF) ** -0.5, 0.09375, ((0, 32),)),
        "leaf_idx": draw_leaf_idx(jax.random.fold_in(splits[10], 71), part),
        "sep_inv": draw_sep_inv(jax.random.fold_in(splits[10], 71), part),
        "sep_cpl": scatter_about(splits[6], (N_ROWS, LEVELS - 1, U, P_SIZE), (4 * P_SIZE) ** -0.5, 0.125, ((0, 32),)),
        "sep_idx": draw_sep_idx(jax.random.fold_in(splits[10], 71), part),
        "stay_dofs": draw_stay_dofs(jax.random.fold_in(splits[10], 71), part),
        "stay_coef": jnp.clip(jax.random.uniform(splits[9], (K, STAYS), jnp.float32, -1.0, 1.0), -1.0, 1.0),
    }


def spread(row_index, values, row_count):
    return jnp.zeros((row_count, values.shape[1]), jnp.float32).at[row_index].add(values)


def lead_dot(left, right):
    return lax.dot_general(left, right, (((0,), (0,)), ((), ())), preferred_element_type=jnp.float32)


def owned_height(device, depth_count):
    for height in range(1, depth_count + 1):
        if (device + 1) % (1 << height) == (1 << (height - 1)):
            return height
    return depth_count + 1


def reference(rhs_leaf, rhs_sep, leaf_inv, leaf_cpl, leaf_idx, sep_inv, sep_cpl, sep_idx, stay_dofs, stay_coef):
    devices = N_ROWS
    columns = rhs_leaf.shape[1]
    heights = [owned_height(device, LEVELS) for device in range(devices)]
    leaf_blocks = [leaf_inv[device * LEAF:(device + 1) * LEAF] for device in range(devices)]
    sep_blocks = [sep_inv[device * P_SIZE:(device + 1) * P_SIZE] for device in range(devices)]
    y_leaf = []
    for device in range(devices):
        solved = jnp.dot(leaf_blocks[device], rhs_leaf[device * LEAF:(device + 1) * LEAF], preferred_element_type=jnp.float32)
        y_leaf.append(solved.astype(jnp.bfloat16))
    y_sep = [jnp.zeros((P_SIZE, columns), jnp.bfloat16) for device in range(devices)]
    for height in range(1, LEVELS + 1):
        for group_pos in range(devices >> height):
            first_leaf = group_pos << height
            holder = first_leaf + (1 << (height - 1)) - 1
            summed = jnp.zeros((P_SIZE, columns), jnp.float32)
            for subtree in range(first_leaf, first_leaf + (1 << height)):
                product = jnp.dot(leaf_cpl[subtree, height - 1], y_leaf[subtree], preferred_element_type=jnp.float32)
                summed = summed + spread(leaf_idx[subtree, height - 1], product, P_SIZE)
                if heights[subtree] < height:
                    slot_pos = height - 1 - heights[subtree]
                    product = jnp.dot(sep_cpl[subtree, slot_pos], y_sep[subtree], preferred_element_type=jnp.float32)
                    summed = summed + spread(sep_idx[subtree, slot_pos], product, P_SIZE)
            residual = (rhs_sep[holder * P_SIZE:(holder + 1) * P_SIZE].astype(jnp.float32) - summed).astype(jnp.bfloat16)
            y_sep[holder] = jnp.dot(sep_blocks[holder], residual, preferred_element_type=jnp.float32).astype(jnp.bfloat16)
    disp_sep = [jnp.zeros((P_SIZE, columns), jnp.bfloat16) for device in range(devices)]
    sub_sep = [jnp.zeros((P_SIZE, columns), jnp.float32) for device in range(devices)]
    sub_leaf = [jnp.zeros((LEAF, columns), jnp.float32) for device in range(devices)]
    for height in range(LEVELS, 0, -1):
        for group_pos in range(devices >> height):
            first_leaf = group_pos << height
            holder = first_leaf + (1 << (height - 1)) - 1
            residual = (y_sep[holder].astype(jnp.float32) - sub_sep[holder]).astype(jnp.bfloat16)
            solved = lead_dot(sep_blocks[holder], residual).astype(jnp.bfloat16)
            disp_sep[holder] = solved
            for subtree in range(first_leaf, first_leaf + (1 << height)):
                sub_leaf[subtree] = sub_leaf[subtree] + lead_dot(leaf_cpl[subtree, height - 1], solved[leaf_idx[subtree, height - 1]])
                if heights[subtree] < height:
                    slot_pos = height - 1 - heights[subtree]
                    sub_sep[subtree] = sub_sep[subtree] + lead_dot(sep_cpl[subtree, slot_pos], solved[sep_idx[subtree, slot_pos]])
    disp_leaf = []
    for device in range(devices):
        residual = (y_leaf[device].astype(jnp.float32) - sub_leaf[device]).astype(jnp.bfloat16)
        disp_leaf.append(lead_dot(leaf_blocks[device], residual).astype(jnp.bfloat16))
    disp_leaf = jnp.concatenate(disp_leaf, axis=0)
    disp_sep = jnp.concatenate(disp_sep, axis=0)
    picked = disp_leaf[stay_dofs].astype(jnp.float32)
    stretch = jnp.sum(stay_coef[:, :, None] * picked, axis=0)
    return (disp_leaf, disp_sep, stretch)
```

```python
import functools

import jax
import jax.numpy as jnp
from jax import lax
from jax.experimental import pallas as pl
from jax.experimental.pallas import tpu as pltpu
from jax.sharding import PartitionSpec as P

BF = jnp.bfloat16
F32 = jnp.float32
LEAF, PANEL, U, NC, LEVELS = 1024, 512, 128, 256, 5
RING = 4
CW = NC // RING
TERM = LEVELS * U
PACK = (TERM + PANEL) // 2
HALF = PANEL // 2
IDX0 = HALF
CPL0 = HALF + 16
WROWS = CPL0 + 4 * (U // 2)
SLOTS = 16
VMEM_LIMIT = 48 * 1024 * 1024


def dot(left, right):
    return jnp.dot(left, right, preferred_element_type=F32)


def lead_dot(left, right):
    return lax.dot_general(left, right, (((0,), (0,)), ((), ())), preferred_element_type=F32)


def call(body, outs, args, scratch=(), specs=None, flops=10**8):
    vmem = pl.BlockSpec(memory_space=pltpu.VMEM)
    return pl.pallas_call(
        body,
        out_shape=outs,
        in_specs=specs or [vmem] * len(args),
        out_specs=[vmem] * len(outs),
        scratch_shapes=list(scratch),
        compiler_params=pltpu.CompilerParams(vmem_limit_bytes=VMEM_LIMIT),
        cost_estimate=pl.CostEstimate(flops=flops, bytes_accessed=4 * 10**6, transcendentals=0),
    )(*args)


def shape(*dims, dtype=BF):
    return jax.ShapeDtypeStruct(dims, dtype)


def hot(row):
    place = lax.broadcasted_iota(jnp.int32, (PANEL, U), 0).astype(F32)
    return jnp.where(place == row, 1.0, 0.0).astype(BF)


def index_rows(block):
    block = block.astype(F32)
    leaf = [block[l : l + 1, 0:U] * 16.0 + block[l : l + 1, U : 2 * U] for l in range(LEVELS)]
    sep = [
        block[s : s + 1, 2 * U : 3 * U] * 16.0 + block[s : s + 1, 3 * U : 4 * U]
        for s in range(LEVELS - 1)
    ]
    return leaf, sep


class Factor:
    def __init__(self, mine, other, first, slots):
        self.mine, self.other, self.first = mine, other, first
        self.rows = index_rows(mine[IDX0 : IDX0 + 16])[1] if slots else []
        self.slots = slots

    def order(self, a, b):
        return jnp.where(self.first, a, b), jnp.where(self.first, b, a)

    def forward(self, resid):
        low, high = self.order(dot(self.mine[0:HALF], resid), dot(self.other[0:HALF], resid))
        return jnp.concatenate([low, high], axis=0).astype(BF)

    def backward(self, back):
        a, b = self.order(back[0:HALF], back[HALF:PANEL])
        return (lead_dot(self.mine[0:HALF], a) + lead_dot(self.other[0:HALF], b)).astype(BF)

    def couple(self, slot):
        start = CPL0 + slot * (U // 2)
        return self.mine[start : start + U // 2], self.other[start : start + U // 2]

    def push(self, slot, y):
        a, b = self.couple(slot)
        low, high = self.order(dot(a, y), dot(b, y))
        value = jnp.concatenate([low, high], axis=0).astype(BF)
        return dot(hot(self.rows[slot]), value)

    def pull(self, slot, x):
        rows = lead_dot(hot(self.rows[slot]), x).astype(BF)
        a, b = self.couple(slot)
        low, high = self.order(rows[0 : U // 2], rows[U // 2 : U])
        return lead_dot(a, low) + lead_dot(b, high)


def pack_rows(ref, start, value):
    ref[start : start + HALF, 0:CW] = value[0:HALF]
    ref[start : start + HALF, CW : 2 * CW] = value[HALF:PANEL]


def unpack_rows(value):
    return jnp.concatenate([value[:, 0:CW], value[:, CW : 2 * CW]], axis=0)


def leaf_forward(inv, rhs, cpl, rsep, y_out, send, stack):
    for i in range(4):
        span = (i + 1) * 256
        y_out[i * 256 : span] = dot(inv[i * 256 : span, 0:span], rhs[0:span]).astype(BF)
    stack[0:TERM] = dot(cpl[...], y_out[...]).astype(BF)
    stack[TERM:] = rsep[...]
    for d in range(RING):
        cols = slice(d * CW, (d + 1) * CW)
        send[d, :, 0:CW] = stack[0:PACK, cols]
        send[d, :, CW : 2 * CW] = stack[PACK : 2 * PACK, cols]


def low_forward(place, recv, gmine, gother, y_out, panels):
    first = place[0] == 0
    z = place[1]
    hold_level = place[2]
    del z
    terms, rhs, rows = [], [], []
    for j in range(RING):
        left, right = recv[j, :, 0:CW], recv[j, :, CW : 2 * CW]
        terms.append(
            [left[l * U : (l + 1) * U] for l in range(4)]
            + [jnp.concatenate([left[4 * U : PACK], right[0 : TERM - PACK]], axis=0)]
        )
        rhs.append(right[TERM - PACK :])
        rows.append(index_rows(gmine[j, IDX0 : IDX0 + 16])[0])

    def gathered(level, leaves):
        total = dot(hot(rows[leaves[0]][level - 1]), terms[leaves[0]][level - 1])
        for j in leaves[1:]:
            total = total + dot(hot(rows[j][level - 1]), terms[j][level - 1])
        return total

    factors = [Factor(gmine.at[j], gother.at[j], first, 4) for j in range(3)]
    ys = {}
    for j, leaves in ((0, (0, 1)), (2, (2, 3))):
        resid = (rhs[j].astype(F32) - gathered(1, leaves)).astype(BF)
        ys[j] = factors[j].forward(resid)
    total = {l: gathered(l, (0, 1, 2, 3)) for l in range(2, LEVELS + 1)}
    for l in range(2, LEVELS + 1):
        total[l] = total[l] + factors[0].push(l - 2, ys[0]) + factors[2].push(l - 2, ys[2])
    ys[1] = factors[1].forward((rhs[1].astype(F32) - total[2]).astype(BF))
    for l in range(3, LEVELS + 1):
        held = jnp.where(hold_level == l, rhs[3].astype(F32), 0.0)
        value = total[l] + factors[1].push(l - 3, ys[1]) - held
        pack_rows(panels, (l - 3) * HALF, value.astype(BF))
    for j in range(3):
        y_out[j] = ys[j]


def top_forward(level, place, mine, recv, wa, wb, wa_other, wb_other, y_out, panels, w, w_other):
    first = place[0] == 0
    pick = place[3 + level - 3] == 1
    count = LEVELS - level
    rows = CPL0 + count * (U // 2)
    w[0:rows] = jnp.where(pick, wa[0:rows], wb[0:rows])
    w_other[0:rows] = jnp.where(pick, wa_other[0:rows], wb_other[0:rows])
    factor = Factor(w, w_other, first, count)
    value = mine[...].astype(F32) + recv[...].astype(F32)
    y = factor.forward((-unpack_rows(value[0:HALF])).astype(BF))
    y_out[...] = y
    for k in range(count):
        total = unpack_rows(value[(k + 1) * HALF : (k + 2) * HALF]) + factor.push(k, y)
        pack_rows(panels, k * HALF, total.astype(BF))


def backward(
    place, mine, recv, y_low, y3_ref, y4_ref, gmine, gother, w3, w3o, w4, w4o, w5a, w5b, w5ao, w5bo,
    send, stack, w5, w5o,
):
    first = place[0] == 0
    hold_level = place[2]
    pick = place[5] == 1
    w5[...] = jnp.where(pick, w5a[0:HALF], w5b[0:HALF])
    w5o[...] = jnp.where(pick, w5ao[0:HALF], w5bo[0:HALF])
    top = Factor(w5, w5o, first, 0)
    total = mine[...].astype(F32) + recv[...].astype(F32)
    x5 = top.backward(top.forward((-unpack_rows(total)).astype(BF)))

    def solve(factor, y, above):
        sub = factor.pull(0, above[0])
        for k in range(1, len(above)):
            sub = sub + factor.pull(k, above[k])
        return factor.backward((y.astype(F32) - sub).astype(BF))

    x4 = solve(Factor(w4, w4o, first, 1), y4_ref[...], [x5])
    x3 = solve(Factor(w3, w3o, first, 2), y3_ref[...], [x4, x5])
    low = [Factor(gmine.at[j], gother.at[j], first, 4) for j in range(3)]
    x2 = solve(low[1], y_low[1], [x3, x4, x5])
    x1 = {j: solve(low[j], y_low[j], [x2, x3, x4, x5]) for j in (0, 2)}
    held = jnp.where(hold_level == 3, x3, jnp.where(hold_level == 4, x4, x5))
    held = jnp.where(hold_level == 0, jnp.zeros_like(held), held)
    own = [x1[0], x2, x1[2], held]
    for j in range(RING):
        rows = index_rows(gmine[j, IDX0 : IDX0 + 16])[0]
        above = [x1[0] if j < 2 else x1[2], x2, x3, x4, x5]
        for l in range(LEVELS):
            stack[l * U : (l + 1) * U] = lead_dot(hot(rows[l]), above[l]).astype(BF)
        stack[TERM:] = own[j]
        send[j, :, 0:CW] = stack[0:PACK]
        send[j, :, CW : 2 * CW] = stack[PACK : 2 * PACK]


def leaf_backward(recv, inv, cpl, y, sel, x_leaf, x_sep, picks, rows, sub):
    for d in range(RING):
        cols = slice(d * CW, (d + 1) * CW)
        rows[0:PACK, cols] = recv[d, :, 0:CW]
        rows[PACK:TERM, cols] = recv[d, 0 : TERM - PACK, CW : 2 * CW]
        x_sep[:, cols] = recv[d, TERM - PACK :, CW : 2 * CW]
    sub[...] = (y[...].astype(F32) - lead_dot(cpl[...], rows[...])).astype(BF)
    for i in range(4):
        start = i * 256
        x_leaf[start : start + 256] = lead_dot(inv[start:, start : start + 256], sub[start:]).astype(BF)
    place = lax.broadcasted_iota(jnp.int32, (32 * SLOTS, LEAF), 1)
    chosen = jnp.where(place == sel[...] - 1, 1.0, 0.0).astype(BF)
    picks[...] = dot(chosen, x_leaf[...]).astype(BF)


def stretch_sum(weight, recv, out):
    value = weight[...]
    high = value.astype(BF)
    low = (value - high.astype(F32)).astype(BF)
    out[...] = dot(high, recv[...]) + dot(low, recv[...])


def stay_plan(me, stay_dofs, stay_coef):
    k, stays = stay_dofs.shape
    per = stays // 32
    pairs = k * per
    dofs = stay_dofs.reshape(k, 32, per).transpose(1, 0, 2).reshape(32, pairs)
    before = jnp.arange(pairs)[:, None] < jnp.arange(pairs)[None, :]
    match = (dofs // LEAF) == me
    rank = dot(match.astype(BF), before.astype(BF))
    at = match[:, None, :] & (rank[:, None, :] == jnp.arange(SLOTS, dtype=F32)[None, :, None])
    sel = jnp.sum(jnp.where(at, (dofs % LEAF + 1)[:, None, :], 0), axis=2).reshape(32 * SLOTS, 1)
    mine = lax.dynamic_index_in_dim(dofs, me, 0, keepdims=False) // LEAF
    earlier = jnp.sum(jnp.where(before & (mine[:, None] == mine[None, :]), 1, 0), axis=0)
    slot = (mine * SLOTS + earlier).reshape(k, per)
    coef = lax.dynamic_slice_in_dim(stay_coef, me * per, per, 1)
    hit = slot[:, :, None] == jnp.arange(32 * SLOTS)[None, None, :]
    weight = jnp.sum(jnp.where(hit, coef[:, :, None], 0.0), axis=0)
    return sel.astype(jnp.int32), weight


def on_device(
    rhs_leaf, rhs_sep, leaf_inv, leaf_cpl, leaf_idx, sep_inv, sep_cpl, sep_idx, stay_dofs, stay_coef
):
    rows_axis, cols_axis = "rows", "cols"
    me = lax.axis_index(rows_axis)
    core = lax.axis_index(cols_axis) % 2
    y, z = me % RING, me // RING
    ring = [[zz * RING + yy for yy in range(RING)] for zz in range(8)]

    def swap_core(value):
        return lax.ppermute(value, cols_axis, [(i, i ^ 1) for i in range(lax.axis_size(cols_axis))])

    def swap_z(value, bit):
        return lax.ppermute(value, rows_axis, [(i, i ^ (bit * RING)) for i in range(32)])

    top_level = jnp.where(
        z % 2 == 0, 3, jnp.where(z % 4 == 1, 4, jnp.where(z % 8 == 3, 5, 0))
    )
    place = jnp.stack(
        [
            core,
            z,
            top_level,
            (z % 2 == 0).astype(jnp.int32),
            (z % 4 < 2).astype(jnp.int32),
            (z < 4).astype(jnp.int32),
        ]
    ).astype(jnp.int32)
    vmem = pl.BlockSpec(memory_space=pltpu.VMEM)
    smem = pl.BlockSpec(memory_space=pltpu.SMEM)

    def split(idx):
        return jnp.concatenate([idx // 16, idx % 16], axis=-1).astype(BF)

    codes = jnp.concatenate(
        [
            jnp.pad(split(leaf_idx[0]), ((0, 16 - LEVELS), (0, 0))),
            jnp.pad(split(sep_idx[0]), ((0, 16 - LEVELS + 1), (0, 0))),
        ],
        axis=1,
    )
    half_inv = lax.dynamic_slice_in_dim(sep_inv, core * HALF, HALF, 0)
    half_cpl = lax.dynamic_slice_in_dim(sep_cpl[0], core * (U // 2), U // 2, 1)
    packed = jnp.concatenate([half_inv, codes, half_cpl.reshape(4 * (U // 2), PANEL)], axis=0)
    gmine = lax.all_gather(packed, rows_axis, axis=0, axis_index_groups=ring, tiled=False)

    cpl = leaf_cpl[0].reshape(TERM, LEAF)
    y_leaf, send = call(
        leaf_forward,
        [shape(LEAF, NC), shape(RING, PACK, 2 * CW)],
        [leaf_inv, rhs_leaf, cpl, rhs_sep],
        [pltpu.VMEM((TERM + PANEL, NC), BF)],
    )
    sel, weight = stay_plan(me, stay_dofs, stay_coef)
    send, sel, weight = lax.optimization_barrier((send, sel, weight))
    recv = lax.all_to_all(send, rows_axis, 0, 0, axis_index_groups=ring, tiled=True)

    gother = swap_core(gmine)
    top_mine, top_other = gmine[3], gother[3]
    far_a = swap_z(top_mine[0 : CPL0 + U], 1)
    y_low, panels = call(
        low_forward,
        [shape(3, PANEL, CW), shape(3 * HALF, 2 * CW)],
        [place, recv, gmine, gother],
        specs=[smem, vmem, vmem, vmem],
    )
    far_ao = swap_core(far_a)
    rows_b = CPL0 + U // 2
    next_mine = jnp.where(z % 2 == 1, top_mine[0:rows_b], far_a[0:rows_b])
    far_b = swap_z(next_mine, 2)
    next_other = swap_core(next_mine)
    far_bo = swap_core(far_b)
    last_mine = jnp.where(z % 4 >= 2, next_mine[0:HALF], far_b[0:HALF])
    last_other = swap_core(last_mine)
    far_c = swap_z(last_mine, 4)
    far_co = swap_core(far_c)

    def rise(level, panels, wa, wb, wao, wbo):
        count = LEVELS - level
        rows = CPL0 + count * (U // 2)
        far = swap_z(panels, 1 << (level - 3))
        return call(
            functools.partial(top_forward, level),
            [shape(PANEL, CW), shape(count * HALF, 2 * CW), shape(rows, PANEL), shape(rows, PANEL)],
            [place, panels, far, wa, wb, wao, wbo],
            specs=[smem] + [vmem] * 6,
        )

    y3, panels, w3, w3o = rise(3, panels, top_mine, far_a, top_other, far_ao)
    y4, panels, w4, w4o = rise(4, panels, next_mine, far_b, next_other, far_bo)
    far = swap_z(panels, 4)
    (send,) = call(
        backward,
        [shape(RING, PACK, 2 * CW)],
        [
            place, panels, far, y_low, y3, y4, gmine, gother, w3, w3o, w4, w4o,
            last_mine, far_c, last_other, far_co,
        ],
        [
            pltpu.VMEM((TERM + PANEL, CW), BF),
            pltpu.VMEM((HALF, PANEL), BF),
            pltpu.VMEM((HALF, PANEL), BF),
        ],
        specs=[smem] + [vmem] * 15,
    )
    recv = lax.all_to_all(send, rows_axis, 0, 0, axis_index_groups=ring, tiled=True)
    x_leaf, x_sep, picks = call(
        leaf_backward,
        [shape(LEAF, NC), shape(PANEL, NC), shape(32 * SLOTS, NC)],
        [recv, leaf_inv, cpl, y_leaf, sel],
        [pltpu.VMEM((TERM, NC), BF), pltpu.VMEM((LEAF, NC), BF)],
    )
    got = lax.all_to_all(
        picks.reshape(32, SLOTS, NC), rows_axis, 0, 0, tiled=True
    ).reshape(32 * SLOTS, NC)
    (stretch,) = call(stretch_sum, [shape(64, NC, dtype=F32)], [weight, got])
    return (x_leaf, x_sep, stretch)


def solution(mesh):
    return jax.shard_map(
        on_device,
        mesh=mesh,
        in_specs=(
            P("rows", "cols"),
            P("rows", "cols"),
            P("rows", None),
            P("rows", None, None, None),
            P("rows", None, None),
            P("rows", None),
            P("rows", None, None, None),
            P("rows", None, None),
            P(),
            P(),
        ),
        out_specs=(P("rows", "cols"), P("rows", "cols"), P("rows", "cols")),
        check_vma=False,
    )
```

```python
import functools

import jax
import jax.numpy as jnp
from jax import lax
from jax.experimental import pallas as pl
from jax.experimental.pallas import tpu as pltpu
from jax.sharding import PartitionSpec as P

BF = jnp.bfloat16
F32 = jnp.float32
LEAF, PANEL, U, NC, LEVELS = 1024, 512, 128, 256, 5
RING, DEPTH = 4, 8
TERM = LEVELS * U
SLOTS = 16
VMEM_LIMIT = 16 * 1024 * 1024

CPL0 = PANEL + 16


def factor_rows(slots):
    return CPL0 + slots * U


def dot(left, right):
    return jnp.dot(left, right, preferred_element_type=F32)


def dot_t(left, right):
    return lax.dot_general(left, right, (((1,), (1,)), ((), ())), preferred_element_type=F32)


VMEM = pl.BlockSpec(memory_space=pltpu.VMEM)
VMEM_FREE = pl.BlockSpec(memory_space=pltpu.VMEM)
SMEM = pl.BlockSpec(memory_space=pltpu.SMEM)
HBM = pl.BlockSpec(memory_space=pltpu.HBM)
ANY = pl.BlockSpec(memory_space=pl.ANY)


def call(body, outs, args, specs, scratch=(), out_specs=None, flops=10**8, moved=10**6):
    args = [in_vmem(arg) if spec is VMEM else arg for arg, spec in zip(args, specs)]
    return pl.pallas_call(
        body,
        out_shape=outs,
        in_specs=specs,
        out_specs=out_specs or [VMEM] * len(outs),
        scratch_shapes=list(scratch),
        compiler_params=pltpu.CompilerParams(vmem_limit_bytes=VMEM_LIMIT),
        cost_estimate=pl.CostEstimate(flops=flops, bytes_accessed=moved, transcendentals=0),
    )(*args)


def dma(n):
    return pltpu.SemaphoreType.DMA((n,))


def pinned(*dims, dtype=BF):
    return pltpu.VMEM(dims, dtype)


def plain(*dims, dtype=BF):
    return jax.ShapeDtypeStruct(dims, dtype)


def in_vmem(value):
    return pltpu.with_memory_space_constraint(value, pltpu.VMEM)


def in_hbm(value):
    return pltpu.with_memory_space_constraint(value, pltpu.HBM)


def hot(rows):
    place = lax.broadcasted_iota(jnp.int32, (PANEL, rows.shape[1]), 0).astype(F32)
    return jnp.where(place == rows, 1.0, 0.0).astype(BF)


def leaf_rows(block):
    block = block.astype(F32)
    return [block[l : l + 1, 0:U] * 16.0 + block[l : l + 1, U : 2 * U] for l in range(LEVELS)]


def sep_rows(block):
    block = block.astype(F32)
    return [
        block[s : s + 1, 2 * U : 3 * U] * 16.0 + block[s : s + 1, 3 * U : 4 * U]
        for s in range(LEVELS - 1)
    ]


def push_values(factor, y, slots):
    return dot_t(y, factor[CPL0 : CPL0 + slots * U]).astype(BF)


def solve_back(factor, hots, y, above):
    back = y
    slots = len(above)
    if slots:
        taken = [dot(above[k], hots[k]).astype(BF) for k in range(slots)]
        taken = taken[0] if slots == 1 else jnp.concatenate(taken, axis=1)
        sub = dot(taken, factor[CPL0 : CPL0 + slots * U])
        back = (y.astype(F32) - sub).astype(BF)
    return dot(back, factor[0:PANEL]).astype(BF)


def pack_factor(inv, cpl, leaf_idx, sep_idx, out, codes, sems):
    copies = [
        pltpu.make_async_copy(inv, out.at[0:PANEL], sems.at[0]),
        pltpu.make_async_copy(cpl, out.at[CPL0:], sems.at[1]),
    ]
    for copy in copies:
        copy.start()
    codes[...] = jnp.zeros_like(codes)
    for ref, count, at in ((leaf_idx, LEVELS, 0), (sep_idx, LEVELS - 1, 2 * U)):
        value = ref[0]
        codes[0:count, at : at + U] = (value >> 4).astype(F32)
        codes[0:count, at + U : at + 2 * U] = (value & 15).astype(F32)
    out[PANEL:CPL0] = codes[...].astype(BF)
    for copy in copies:
        copy.wait()


def leaf_forward(
    place, inv, rhs, cpl, rsep, yt_out, keep, send, inv_v, cpl_v, rhs_v, rsep_v, y, stack, sems
):
    loads = [pltpu.make_async_copy(rhs, rhs_v, sems.at[0])]
    for i in range(4):
        rows = pl.ds(i * 256, 256)
        loads.append(pltpu.make_async_copy(inv.at[rows], inv_v.at[rows], sems.at[1 + i]))
    loads.append(pltpu.make_async_copy(cpl.at[0], cpl_v, sems.at[5]))
    loads.append(pltpu.make_async_copy(rsep, rsep_v, sems.at[6]))
    for load in loads:
        load.start()
    loads[0].wait()
    for i in range(4):
        loads[1 + i].wait()
        span = (i + 1) * 256
        y[i * 256 : span] = dot(inv_v[i * 256 : span, 0:span], rhs_v[0:span])
    yt_out[...] = y[...].T.astype(BF)
    loads[5].wait()
    for l in range(LEVELS):
        stack[:, l * U : (l + 1) * U] = dot_t(yt_out[...], cpl_v[l]).astype(BF)
    loads[6].wait()
    stack[:, TERM:] = rsep_v[...].astype(F32).T.astype(BF)
    side = place[3]
    keep[...] = stack[pl.ds(pl.multiple_of(side * 128, 128), 128)]
    send[...] = stack[pl.ds(pl.multiple_of((1 - side) * 128, 128), 128)]


ONE = 2 * U
ONE_HOTS = ONE + 4 * 3 * U


def start_chosen(cases, sources, copy_of):
    for i, source in enumerate(sources):

        @pl.when(cases[i] == 1)
        def _(source=source):
            copy_of(source).start()

    return copy_of(sources[0])


def stage(slots, count, cases, *refs):
    sources = refs[:count]
    factor, hots, sems = refs[count:]
    rows = factor_rows(slots)
    copy = start_chosen(
        cases, sources, lambda source: pltpu.make_async_copy(source.at[0:rows], factor, sems.at[0])
    )
    copy.wait()
    if slots:
        taken = sep_rows(factor[PANEL:CPL0])
        for k in range(slots):
            hots[:, k * U : (k + 1) * U] = hot(taken[k])


def stage_last(count, cases, *refs):
    factor, done, sems = refs[count:]
    copy = start_chosen(
        cases,
        refs[:count],
        lambda source: pltpu.make_async_copy(source.at[0:PANEL], factor, sems.at[0]),
    )
    done[...] = jnp.zeros_like(done)
    copy.wait()


def stage_one(cases, own, a, b, factor, hots, theirs_v, sems):
    copies = [
        start_chosen(cases, [own, a, b], lambda source: pltpu.make_async_copy(source, factor, sems.at[0]))
    ]
    rows = pl.ds(PANEL, 16)
    far = [
        pltpu.make_async_copy(a.at[rows], theirs_v.at[0], sems.at[1]),
        pltpu.make_async_copy(b.at[rows], theirs_v.at[1], sems.at[2]),
    ]
    for copy in far:
        copy.start()
    mine = leaf_rows(own[PANEL:CPL0])
    for copy in far:
        copy.wait()
    other = jnp.where(cases[3] == 0, theirs_v[0], theirs_v[1])
    theirs = leaf_rows(other)
    ours, others = sep_rows(own[PANEL:CPL0]), sep_rows(other)
    hots[:, 0:ONE] = hot(jnp.concatenate([mine[0], theirs[0]], axis=1))
    for k in range(4):
        up = jnp.where(cases[0] == 1, ours[k], others[k])
        at = ONE + k * 3 * U
        hots[:, at : at + 3 * U] = hot(jnp.concatenate([mine[k + 1], theirs[k + 1], up], axis=1))
    for copy in copies:
        copy.wait()


def level_one(place, keep, recv, factor, hots, y_out, panel_keep, panel_send, panels):
    ring, even = place[1], place[2] == 0
    total = dot_t(jnp.concatenate([keep[:, 0:U], recv[:, 0:U]], axis=1), hots[:, 0:ONE])
    rhs_keep, rhs_recv = keep[:, TERM:].astype(F32), recv[:, TERM:].astype(F32)
    resid = (jnp.where(even, rhs_keep, rhs_recv) - total).astype(BF)
    y = dot_t(resid, factor[0:PANEL]).astype(BF)
    y_out[...] = y
    values = push_values(factor, y, 4)
    held = jnp.where(even, rhs_recv, rhs_keep)
    level = jnp.where(ring < 2, 2, place[4])
    for l in range(2, LEVELS + 1):
        at = slice((l - 1) * U, l * U)
        start = ONE + (l - 2) * 3 * U
        parts = [keep[:, at], recv[:, at], values[:, (l - 2) * U : (l - 1) * U]]
        total = dot_t(jnp.concatenate(parts, axis=1), hots[:, start : start + 3 * U])
        total = total - jnp.where(level == l, held, 0.0)
        panels[:, (l - 2) * PANEL : (l - 1) * PANEL] = total.astype(BF)
    side = place[5]
    panel_keep[...] = panels[pl.ds(pl.multiple_of(side * 64, 64), 64)]
    panel_send[...] = panels[pl.ds(pl.multiple_of((1 - side) * 64, 64), 64)]


def level_up(level, mine, recv, factor, hots, y_out, panels):
    slots = LEVELS - level
    total = mine[...].astype(F32) + recv[...].astype(F32)
    y = dot_t((-total[:, 0:PANEL]).astype(BF), factor[0:PANEL]).astype(BF)
    y_out[...] = y
    values = push_values(factor, y, slots)
    for k in range(slots):
        at = slice((k + 1) * PANEL, (k + 2) * PANEL)
        term = dot_t(values[:, k * U : (k + 1) * U], hots[:, k * U : (k + 1) * U])
        panels[:, k * PANEL : (k + 1) * PANEL] = (total[:, at] + term).astype(BF)


def turn(mine, recv, f3, f4, f5, h3, h4, y3, y4, x_out):
    total = mine[...].astype(F32) + recv[...].astype(F32)
    y5 = dot_t((-total).astype(BF), f5[0:PANEL]).astype(BF)
    x5 = solve_back(f5, [], y5, [])
    x4 = solve_back(f4, [h4[...]], y4[...], [x5])
    x3 = solve_back(f3, [h3[:, 0:U], h3[:, U : 2 * U]], y3[...], [x4, x5])
    for k, x in enumerate((x3, x4, x5)):
        x_out[:, k * PANEL : (k + 1) * PANEL] = x


def level_two_back(place, mine, recv, f2, h2, y2, x_out):
    x = jnp.where(place[6] == 0, mine[...], recv[...])
    above = [x[:, k * PANEL : (k + 1) * PANEL] for k in range(3)]
    x_out[:, 0:PANEL] = solve_back(f2, [h2[:, k * U : (k + 1) * U] for k in range(3)], y2[...], above)
    x_out[:, PANEL:] = x


def level_one_back(place, mine, recv, y1, factor, hots, rows_keep, rows_send, sep_keep, sep_send, x):
    side = place[5]
    even = place[2] == 0
    x[pl.ds(pl.multiple_of(side * 64, 64), 64)] = mine[...]
    x[pl.ds(pl.multiple_of((1 - side) * 64, 64), 64)] = recv[...]
    above = [x[:, k * PANEL : (k + 1) * PANEL] for k in range(4)]
    ups = [hots[:, ONE + k * 3 * U + 2 * U : ONE + (k + 1) * 3 * U] for k in range(4)]
    x1 = solve_back(factor, ups, y1[...], above)
    for l, value in enumerate([x1] + above):
        start = 0 if l == 0 else ONE + (l - 1) * 3 * U
        both = dot(value, hots[:, start : start + 2 * U]).astype(BF)
        rows_keep[:, l * U : (l + 1) * U] = both[:, 0:U]
        rows_send[:, l * U : (l + 1) * U] = both[:, U : 2 * U]
    level = jnp.where(place[1] < 2, 2, place[4])
    held = jnp.where(level == 0, jnp.zeros_like(x1), above[0])
    for k in (1, 2, 3):
        held = jnp.where(level == k + 2, above[k], held)
    sep_keep[...] = jnp.where(even, x1, held)
    sep_send[...] = jnp.where(even, held, x1)


def stage_leaf(sel, chosen):
    place = lax.broadcasted_iota(jnp.int32, (32 * SLOTS, LEAF), 1)
    chosen[...] = jnp.where(place == sel[...] - 1, 1.0, 0.0).astype(BF)


def leaf_backward(place, keep, recv, inv, cpl, yt, chosen, x_leaf, picks, rows, sub):
    side = place[3]
    rows[pl.ds(pl.multiple_of(side * 128, 128), 128)] = keep[...]
    rows[pl.ds(pl.multiple_of((1 - side) * 128, 128), 128)] = recv[...]
    total = yt[...].astype(F32)
    for l in range(LEVELS):
        total = total - dot(rows[:, l * U : (l + 1) * U], cpl[l])
    sub[...] = total.astype(BF)
    for i in range(4):
        start = i * 256
        part = dot(sub[:, start:], inv[start:, start : start + 256])
        x_leaf[start : start + 256] = part.T.astype(BF)
    picks[...] = dot(chosen[...], x_leaf[...]).astype(BF)


def finish(place, weight, got, keep, recv, out, x_sep, xt):
    side = place[3]
    xt[pl.ds(pl.multiple_of(side * 128, 128), 128)] = keep[...].astype(F32)
    xt[pl.ds(pl.multiple_of((1 - side) * 128, 128), 128)] = recv[...].astype(F32)
    x_sep[...] = xt[...].T.astype(BF)
    value = weight[...]
    high = value.astype(BF)
    low = (value - high.astype(F32)).astype(BF)
    out[...] = dot(high, got[...]) + dot(low, got[...])


def stay_plan(me, stay_dofs, stay_coef):
    k, stays = stay_dofs.shape
    per = stays // 32
    pairs = k * per
    dofs = stay_dofs.reshape(k, 32, per).transpose(1, 0, 2).reshape(32, pairs)
    before = jnp.arange(pairs)[:, None] < jnp.arange(pairs)[None, :]
    match = (dofs // LEAF) == me
    rank = dot(match.astype(BF), before.astype(BF))
    at = match[:, None, :] & (rank[:, None, :] == jnp.arange(SLOTS, dtype=F32)[None, :, None])
    sel = jnp.sum(jnp.where(at, (dofs % LEAF + 1)[:, None, :], 0), axis=2).reshape(32 * SLOTS, 1)
    mine = lax.dynamic_index_in_dim(dofs, me, 0, keepdims=False) // LEAF
    earlier = jnp.sum(jnp.where(before & (mine[:, None] == mine[None, :]), 1, 0), axis=0)
    slot = (mine * SLOTS + earlier).reshape(k, per)
    coef = lax.dynamic_slice_in_dim(stay_coef, me * per, per, 1)
    hit = slot[:, :, None] == jnp.arange(32 * SLOTS)[None, None, :]
    weight = jnp.sum(jnp.where(hit, coef[:, :, None], 0.0), axis=0)
    return sel.astype(jnp.int32), weight


def after(value, *others):
    return lax.optimization_barrier((value, *others))[0]


def on_device(
    rhs_leaf, rhs_sep, leaf_inv, leaf_cpl, leaf_idx, sep_inv, sep_cpl, sep_idx, stay_dofs, stay_coef
):
    rows_axis, cols_axis = "rows", "cols"
    columns, rows = lax.axis_size(cols_axis), lax.axis_size(rows_axis)
    me = lax.axis_index(rows_axis)
    core = lax.axis_index(cols_axis) % 2
    y, z = me % RING, me // RING

    def swap_core(value):
        return lax.ppermute(value, cols_axis, [(i, i ^ 1) for i in range(columns)])

    def swap(value, flip):
        return lax.ppermute(value, rows_axis, [(i, i ^ flip) for i in range(rows)])

    def route(value, target):
        pairs = []
        for c in range(columns):
            for r in range(rows):
                to = target(c % 2, r % RING, r // RING)
                if to is not None:
                    pairs.append((c * rows + r, c * rows + to[1] * RING + to[0]))
        return lax.ppermute(value, (cols_axis, rows_axis), pairs)

    def cases(*values):
        return jnp.stack(values).astype(jnp.int32)

    top_level = jnp.where(z % 2 == 0, 3, jnp.where(z % 4 == 1, 4, jnp.where(z == 3, 5, 0)))
    place = cases(core, y, y % 2, (y % 2) ^ (y // 2), top_level, y // 2, z % 2)

    (own,) = call(
        pack_factor,
        [pinned(factor_rows(4), PANEL)],
        [in_hbm(sep_inv), in_hbm(sep_cpl.reshape(4 * U, PANEL)), leaf_idx, sep_idx],
        [HBM, HBM, VMEM, VMEM],
        [pltpu.VMEM((16, PANEL), F32), dma(2)],
    )
    with jax.named_scope("factors_to_neighbours"):
        near = route(own, lambda c, y, z: (y ^ (3 if c else 1), z))

    yt, keep, send, inv_v, cpl_v = call(
        leaf_forward,
        [
            pinned(NC, LEAF),
            pinned(128, TERM + PANEL),
            pinned(128, TERM + PANEL),
            pinned(LEAF, LEAF),
            pinned(LEVELS, U, LEAF),
        ],
        [after(place, own), in_hbm(leaf_inv), in_hbm(rhs_leaf), in_hbm(leaf_cpl), in_hbm(rhs_sep)],
        [SMEM, HBM, HBM, HBM, HBM],
        [
            pltpu.VMEM((LEAF, NC), BF),
            pltpu.VMEM((PANEL, NC), BF),
            pltpu.VMEM((LEAF, NC), F32),
            pltpu.VMEM((NC, TERM + PANEL), BF),
            dma(7),
        ],
    )
    with jax.named_scope("leaf_terms"):
        recv = swap(send, 1)
    sel, weight = stay_plan(me, *after((stay_dofs, stay_coef), send))
    recv, sel, weight = lax.optimization_barrier((recv, sel, weight))
    near = after(near, recv)
    with jax.named_scope("near_to_core"):
        near_o = swap_core(near)
    with jax.named_scope("factors_across"):
        far = route(
            near, lambda c, y, z: (y ^ (1 if c else 3), z) if y % 2 == 0 else None
        )
    first = core == 0
    one = (y % 2 == 1) & first, (y % 2 == 1) & ~first
    f1, h1 = call(
        stage_one,
        [pinned(factor_rows(4), PANEL), pinned(PANEL, ONE_HOTS)],
        [cases(y % 2 == 0, *one, core), own, near, near_o],
        [SMEM, VMEM, ANY, ANY],
        [pltpu.VMEM((2, 16, PANEL), BF), dma(3)],
    )
    y1, panel, send = call(
        level_one,
        [pinned(128, PANEL), pinned(64, 4 * PANEL), pinned(64, 4 * PANEL)],
        [place, keep, recv, f1, h1],
        [SMEM] + [VMEM] * 4,
        [pltpu.VMEM((128, 4 * PANEL), BF)],
    )
    with jax.named_scope("panels_ring"):
        recv = swap(send, 3)

    def ready(slots, which, sources):
        return call(
            functools.partial(stage, slots, len(sources)),
            [pinned(factor_rows(slots), PANEL), pinned(PANEL, max(slots, 1) * U)],
            [which, *sources],
            [SMEM] + [ANY] * len(sources),
            [dma(1)],
        )

    def rise(level, panel, recv, factor, hots):
        slots = LEVELS - level
        return call(
            functools.partial(level_up, level),
            [pinned(64, PANEL), pinned(64, slots * PANEL)],
            [panel, recv, factor, hots],
            [VMEM] * 4,
        )

    far = after(far, recv)
    at = [own, near, near_o, far]
    f2, h2 = ready(
        3,
        cases(
            y == 1,
            ((y == 0) & first) | ((y == 2) & ~first),
            ((y == 0) & ~first) | ((y == 2) & first),
            y == 3,
        ),
        at,
    )
    f3, h3 = ready(
        2,
        cases(
            y == 3,
            ((y == 2) & first) | ((y == 0) & ~first),
            ((y == 2) & ~first) | ((y == 0) & first),
            y == 1,
        ),
        at,
    )
    with jax.named_scope("factors_up"):
        up = route(
            f3[0 : factor_rows(1)],
            lambda c, y, z: (y, (z + (1 if c else -1)) % DEPTH) if z % 2 else None,
        )
    recv = after(recv, f2, h2)
    y2, panel = rise(2, panel, recv, f2, h2)
    with jax.named_scope("panels_z1"):
        recv = lax.ppermute(
            panel, rows_axis, [(r, r - RING) for r in range(rows) if r // RING % 2]
        )
    up = after(up, recv)
    with jax.named_scope("up_to_core"):
        up_o = swap_core(up)
    with jax.named_scope("factor_top"):
        last = route(
            up,
            lambda c, y, z: (y, 0) if (c, z) == (0, 2) else (y, 6) if (c, z) == (1, 4) else None,
        )
    y3, panel = rise(3, panel, recv, f3, h3)
    with jax.named_scope("panels_z2"):
        recv = lax.ppermute(
            panel, rows_axis, [(r, r ^ (2 * RING)) for r in range(rows) if r // RING % 2 == 0]
        )
    f4, h4 = ready(
        1, cases((z % 4 == 0) == first, (z % 4 == 0) != first), after((up, up_o), panel)
    )
    recv = after(recv, f4, h4)
    y4, panel = rise(4, panel, recv, f4, h4)
    with jax.named_scope("panels_z3"):
        recv = lax.ppermute(
            panel,
            rows_axis,
            [(r, (6 - r // RING) * RING + r % RING) for r in range(rows) if r // RING % 2 == 0],
        )
    last = after(last, panel)
    with jax.named_scope("last_to_core"):
        last_o = swap_core(last)
    inner = (z == 2) | (z == 4)
    same = (z == 2) == first
    f5, _ = call(
        functools.partial(stage_last, 4),
        [pinned(PANEL, PANEL), pinned(16, 128)],
        [cases(
            inner & same,
            inner & ~same,
            ~inner & ((z == 0) == first),
            ~inner & ((z == 0) != first),
        ), up, up_o, last, last_o],
        [SMEM] + [ANY] * 4,
        [dma(1)],
    )
    recv = after(recv, f5)
    (x,) = call(
        turn,
        [pinned(64, 3 * PANEL)],
        [panel, recv, f3, f4, f5, h3, h4, y3, y4],
        [VMEM] * 9,
    )
    with jax.named_scope("down_z1"):
        recv = lax.ppermute(
            x, rows_axis, [(r, r + RING) for r in range(rows) if r // RING % 2 == 0]
        )
    (x,) = call(
        level_two_back,
        [pinned(64, 4 * PANEL)],
        [place, x, recv, f2, h2, y2],
        [SMEM] + [VMEM] * 5,
    )
    with jax.named_scope("down_ring"):
        recv = swap(x, 3)
    rows_keep, rows_send, sep_keep, sep_send = call(
        level_one_back,
        [pinned(128, TERM), pinned(128, TERM), pinned(128, PANEL), pinned(128, PANEL)],
        [place, x, recv, y1, f1, h1],
        [SMEM] + [VMEM] * 5,
        [pltpu.VMEM((128, 4 * PANEL), BF)],
    )
    with jax.named_scope("rows_back"):
        recv = swap(rows_send, 1)
    (picked,) = call(stage_leaf, [pinned(32 * SLOTS, LEAF)], [after(sel, rows_send)], [VMEM_FREE])
    recv = after(recv, picked)
    x_leaf, picks = call(
        leaf_backward,
        [plain(LEAF, NC), pinned(32 * SLOTS, NC)],
        [place, rows_keep, recv, inv_v, cpl_v, yt, picked],
        [SMEM] + [VMEM] * 6,
        [pltpu.VMEM((NC, TERM), BF), pltpu.VMEM((NC, LEAF), BF)],
    )
    with jax.named_scope("sep_back"):
        sep_recv = swap(after(sep_send, recv), 1)
    got = lax.all_to_all(
        picks.reshape(32, SLOTS, NC), rows_axis, 0, 0, tiled=True
    ).reshape(32 * SLOTS, NC)
    stretch, x_sep = call(
        finish,
        [plain(64, NC, dtype=F32), plain(PANEL, NC)],
        [place, weight, got, sep_keep, sep_recv],
        [SMEM] + [VMEM] * 4,
        [pltpu.VMEM((NC, PANEL), F32)],
    )
    return (x_leaf, x_sep, stretch)


def solution(mesh):
    return jax.shard_map(
        on_device,
        mesh=mesh,
        in_specs=(
            P("rows", "cols"),
            P("rows", "cols"),
            P("rows", None),
            P("rows", None, None, None),
            P("rows", None, None),
            P("rows", None),
            P("rows", None, None, None),
            P("rows", None, None),
            P(),
            P(),
        ),
        out_specs=(P("rows", "cols"), P("rows", "cols"), P("rows", "cols")),
        check_vma=False,
    )
```

```python
import functools

import jax
import jax.numpy as jnp
from jax import lax
from jax.experimental import pallas as pl
from jax.experimental.pallas import tpu as pltpu
from jax.sharding import PartitionSpec as P

BF = jnp.bfloat16
F32 = jnp.float32
LEAF, PANEL, U, NC, LEVELS = 1024, 512, 128, 256, 5
RING, DEPTH = 4, 8
TERM = LEVELS * U
SLOTS = 16
VMEM_LIMIT = 16 * 1024 * 1024

TRI = 320
IDX = slice(TRI, TRI + 16)
CPL0 = TRI + 16


def packed_rows(slots):
    return CPL0 + slots * U


def factor_rows(slots):
    return PANEL + slots * U


def triangle_blocks():
    return [
        (slice(384, 512), slice(0, 512), slice(0, 128), slice(0, 512)),
        (slice(256, 384), slice(0, 384), slice(128, 256), slice(0, 384)),
        (slice(0, 128), slice(0, 128), slice(128, 256), slice(384, 512)),
        (slice(128, 192), slice(0, 256), slice(256, 320), slice(0, 256)),
        (slice(192, 256), slice(0, 256), slice(256, 320), slice(256, 512)),
    ]


def dot(left, right):
    return jnp.dot(left, right, preferred_element_type=F32)


def dot_t(left, right):
    return lax.dot_general(left, right, (((1,), (1,)), ((), ())), preferred_element_type=F32)


VMEM = pl.BlockSpec(memory_space=pltpu.VMEM)
SMEM = pl.BlockSpec(memory_space=pltpu.SMEM)
HBM = pl.BlockSpec(memory_space=pltpu.HBM)
ANY = pl.BlockSpec(memory_space=pl.ANY)


def call(body, outs, args, specs, scratch=(), out_specs=None, flops=10**8, moved=10**6):
    args = [
        in_vmem(arg) if spec is VMEM else in_hbm(arg) if spec is HBM else arg
        for arg, spec in zip(args, specs)
    ]
    return pl.pallas_call(
        body,
        out_shape=outs,
        in_specs=specs,
        out_specs=out_specs or [VMEM] * len(outs),
        scratch_shapes=list(scratch),
        compiler_params=pltpu.CompilerParams(vmem_limit_bytes=VMEM_LIMIT),
        cost_estimate=pl.CostEstimate(flops=flops, bytes_accessed=moved, transcendentals=0),
    )(*args)


def dma(n):
    return pltpu.SemaphoreType.DMA((n,))


def pinned(*dims, dtype=BF):
    return pltpu.VMEM(dims, dtype)


def plain(*dims, dtype=BF):
    return jax.ShapeDtypeStruct(dims, dtype)


def stored(*dims, dtype=BF):
    return pltpu.HBM(dims, dtype)


def in_vmem(value):
    return pltpu.with_memory_space_constraint(value, pltpu.VMEM)


def in_hbm(value):
    return pltpu.with_memory_space_constraint(value, pltpu.HBM)


def hot(rows):
    place = lax.broadcasted_iota(jnp.int32, (PANEL, rows.shape[1]), 0).astype(F32)
    return jnp.where(place == rows, 1.0, 0.0).astype(BF)


def leaf_rows(block):
    block = block.astype(F32)
    return [block[l : l + 1, 0:U] * 16.0 + block[l : l + 1, U : 2 * U] for l in range(LEVELS)]


def sep_rows(block):
    block = block.astype(F32)
    return [
        block[s : s + 1, 2 * U : 3 * U] * 16.0 + block[s : s + 1, 3 * U : 4 * U]
        for s in range(LEVELS - 1)
    ]


def push_values(factor, y, slots):
    return dot_t(y, factor[PANEL : PANEL + slots * U]).astype(BF)


def solve_back(factor, hots, y, above):
    back = y
    slots = len(above)
    if slots:
        taken = [dot(above[k], hots[k]).astype(BF) for k in range(slots)]
        taken = taken[0] if slots == 1 else jnp.concatenate(taken, axis=1)
        sub = dot(taken, factor[PANEL : PANEL + slots * U])
        back = (y.astype(F32) - sub).astype(BF)
    return dot(back, factor[0:PANEL]).astype(BF)


def pack_factor(place, inv, cpl, leaf_idx, sep_idx, out, up, codes_out, codes, leaf_v, sep_v, sems):
    loads = [
        pltpu.make_async_copy(leaf_idx.at[0], leaf_v, sems.at[0]),
        pltpu.make_async_copy(sep_idx.at[0], sep_v, sems.at[1]),
    ]
    copies = []
    for n, (dst, slots) in enumerate(((up, 3), (out, 4))):
        for i, (r, c, pr, pc) in enumerate(triangle_blocks()):
            copies.append(pltpu.make_async_copy(inv.at[r, c], dst.at[pr, pc], sems.at[2 + 6 * n + i]))
        copies.append(
            pltpu.make_async_copy(cpl.at[0 : slots * U], dst.at[CPL0 : packed_rows(slots)], sems.at[7 + 6 * n])
        )
    for copy in loads + copies:
        copy.start()
    codes[...] = jnp.zeros_like(codes)
    for ref, load, count, at in ((leaf_v, loads[0], LEVELS, 0), (sep_v, loads[1], LEVELS - 1, 2 * U)):
        load.wait()
        value = ref[...]
        codes[0:count, at : at + U] = (value >> 4).astype(F32)
        codes[0:count, at + U : at + 2 * U] = (value & 15).astype(F32)
    coded = codes[...].astype(BF)
    out[IDX] = coded
    up[IDX] = coded
    for q in range(4):
        codes_out[16 * q : 16 * (q + 1)] = coded[:, q * U : (q + 1) * U]
    for copy in copies:
        copy.wait()


def leaf_forward(
    place, inv, rhs, cpl, rsep, codes, yt_out, terms, rhs_out, one_out, inv_v, cpl_v, rhs_v, rsep_v, y, sems
):
    loads = [pltpu.make_async_copy(rhs, rhs_v, sems.at[0])]
    for i in range(4):
        rows = pl.ds(i * 256, 256)
        loads.append(pltpu.make_async_copy(inv.at[rows], inv_v.at[rows], sems.at[1 + i]))
    loads.append(pltpu.make_async_copy(cpl.at[0], cpl_v, sems.at[5]))
    loads.append(pltpu.make_async_copy(rsep, rsep_v, sems.at[6]))
    for load in loads:
        load.start()
    loads[0].wait()
    for i in range(4):
        loads[1 + i].wait()
        span = (i + 1) * 256
        y[i * 256 : span] = dot(inv_v[i * 256 : span, 0:span], rhs_v[0:span])
    yt_out[...] = y[...].T.astype(BF)
    loads[5].wait()
    one_out[0:NC] = dot_t(yt_out[...], cpl_v[0]).astype(BF)
    one_out[NC:] = codes[...]
    for l in range(1, LEVELS):
        terms[:, (l - 1) * U : l * U] = dot_t(yt_out[...], cpl_v[l]).astype(BF)
    loads[6].wait()
    rhs_out[...] = rsep_v[...].astype(F32).T.astype(BF)


def which(place):
    return place[0], place[1], place[2]


def pick_two(core, y, z):
    return (
        y == 1,
        ((y == 0) & (core == 0)) | ((y == 2) & (core == 1)),
        ((y == 0) & (core == 1)) | ((y == 2) & (core == 0)),
        y == 3,
    )


def pick_top(core, y, z):
    return (
        y == 3,
        ((y == 2) & (core == 0)) | ((y == 0) & (core == 1)),
        ((y == 2) & (core == 1)) | ((y == 0) & (core == 0)),
        y == 1,
    )


def pick_four(core, y, z):
    after_me = (z == 0) | (z == 4)
    first = core == 0
    return (after_me & first) | (~after_me & ~first), (after_me & ~first) | (~after_me & first)


def pick_five(core, y, z):
    inner = (z == 2) | (z == 4)
    first = core == 0
    low = (z == 2) | (z == 0)
    same = (low & first) | (~low & ~first)
    return inner & same, inner & ~same, ~inner & same, ~inner & ~same


def pick_one(core, y, z):
    even = (y == 0) | (y == 2)
    return even, ~even


def stage(slots, pick, split, count, place, *refs):
    if split:
        sources = [(refs[2 * i], refs[2 * i + 1], 0) for i in range(count)]
    else:
        sources = [(refs[i], refs[i], TRI) for i in range(count)]
    factor, hots, idx, sems = refs[(2 if split else 1) * count :]
    cases = pick(*which(place))

    def copies_of(triangle, rest, at):
        copies = [
            pltpu.make_async_copy(triangle.at[pr, pc], factor.at[r, c], sems.at[i])
            for i, (r, c, pr, pc) in enumerate(triangle_blocks())
        ]
        if slots:
            coupling = rest.at[at + 16 : at + 16 + slots * U]
            copies.append(pltpu.make_async_copy(coupling, factor.at[PANEL:], sems.at[5]))
            copies.append(pltpu.make_async_copy(rest.at[at : at + 16], idx, sems.at[6]))
        return copies

    for case, source in zip(cases, sources):

        @pl.when(case)
        def _(source=source):
            for copy in copies_of(*source):
                copy.start()

    for rows, cols in (
        (slice(0, 128), slice(128, 512)),
        (slice(128, 256), slice(256, 512)),
        (slice(256, 384), slice(384, 512)),
    ):
        factor[rows, cols] = jnp.zeros((rows.stop - rows.start, cols.stop - cols.start), BF)
    copies = copies_of(*sources[0])
    if slots:
        copies[-1].wait()
        taken = sep_rows(idx[...])
        for k in range(slots):
            hots[:, k * U : (k + 1) * U] = hot(taken[k])
        copies = copies[:-1]
    else:
        hots[...] = jnp.zeros_like(hots)
    for copy in copies:
        copy.wait()


def stage_and_pass(place, own, near, near_o, far, factor, hots, triangle, rest, idx, sems):
    sources = (own, near, near_o, far)

    def copies_of(source):
        return [
            pltpu.make_async_copy(source.at[0:TRI], triangle, sems.at[7]),
            pltpu.make_async_copy(source.at[TRI : packed_rows(1)], rest, sems.at[8]),
        ]

    for case, source in zip(pick_top(*which(place)), sources):

        @pl.when(case)
        def _(source=source):
            for copy in copies_of(source):
                copy.start()

    stage(2, pick_top, False, 4, place, *sources, factor, hots, idx, sems)
    for copy in copies_of(own):
        copy.wait()


ONE = 2 * U
ONE_HOTS = ONE + 4 * 3 * U


def stage_pair(place, one, other, hots):
    even = place[1] % 2 == 0
    mine, far = one[NC:], other[NC:]

    def rows(block, at, count):
        block = block.astype(F32)
        return [
            block[at + i : at + i + 1] * 16.0 + block[at + 16 + i : at + 17 + i] for i in range(count)
        ]

    left, right = jnp.where(even, mine, far), jnp.where(even, far, mine)
    a, b, up = rows(left, 0, LEVELS), rows(right, 0, LEVELS), rows(left, 32, LEVELS - 1)
    hots[:, 0:ONE] = hot(jnp.concatenate([a[0], b[0]], axis=1))
    for k in range(4):
        at = ONE + k * 3 * U
        hots[:, at : at + 3 * U] = hot(jnp.concatenate([a[k + 1], b[k + 1], up[k]], axis=1))


def half_of(place):
    y = place[1]
    return jnp.where((y == 1) | (y == 2), 1, 0)


def level_one(place, one, recv, terms, rhs, factor, hots, y_keep, y_send, keep, send, y_all):
    even = place[1] % 2 == 0
    total = dot_t(jnp.concatenate([one[0:NC], recv[0:NC]], axis=1), hots[:, 0:ONE])
    resid = (rhs[...].astype(F32) - total).astype(BF)
    y = dot_t(resid, factor[0:PANEL]).astype(BF)
    y_all[:, 0:PANEL] = y
    y_all[:, PANEL:] = jnp.where(even, push_values(factor, y, 4), rhs[...])
    side = half_of(place)
    mine = pl.ds(pl.multiple_of(side * 128, 128), 128)
    theirs = pl.ds(pl.multiple_of((1 - side) * 128, 128), 128)
    send[:, 0:PANEL] = terms[theirs]
    send[:, PANEL:] = y_all[theirs, PANEL:]
    keep[:, 0:PANEL] = terms[mine]
    keep[:, PANEL:] = y_all[mine, PANEL:]
    y_keep[...] = y_all[mine, 0:PANEL]
    y_send[...] = y_all[theirs, 0:PANEL]


def join_pair(place, keep, recv, hots, panel_keep, panel_send, panels):
    ring, even = place[1], place[1] % 2 == 0
    a, b = keep[...], recv[...]
    left, right = jnp.where(even, a, b), jnp.where(even, b, a)
    held = right[:, PANEL:].astype(F32)
    level = jnp.where(ring < 2, 2, place[3])
    for k in range(4):
        at = slice(k * U, (k + 1) * U)
        start = ONE + k * 3 * U
        parts = [left[:, at], right[:, at], left[:, PANEL + k * U : PANEL + (k + 1) * U]]
        total = dot_t(jnp.concatenate(parts, axis=1), hots[:, start : start + 3 * U])
        total = total - jnp.where(level == k + 2, held, 0.0)
        panels[:, k * PANEL : (k + 1) * PANEL] = total.astype(BF)
    side = ring // 2
    panel_keep[...] = panels[pl.ds(pl.multiple_of(side * 64, 64), 64)]
    panel_send[...] = panels[pl.ds(pl.multiple_of((1 - side) * 64, 64), 64)]


def level_up(level, mine, recv, factor, hots, y_out, panels):
    slots = LEVELS - level
    total = mine[...].astype(F32) + recv[...].astype(F32)
    y = dot_t((-total[:, 0:PANEL]).astype(BF), factor[0:PANEL]).astype(BF)
    y_out[...] = y
    values = push_values(factor, y, slots)
    for k in range(slots):
        at = slice((k + 1) * PANEL, (k + 2) * PANEL)
        term = dot_t(values[:, k * U : (k + 1) * U], hots[:, k * U : (k + 1) * U])
        panels[:, k * PANEL : (k + 1) * PANEL] = (total[:, at] + term).astype(BF)


def turn(mine, recv, f3, f4, f5, h3, h4, y3, y4, x_out):
    total = mine[...].astype(F32) + recv[...].astype(F32)
    y5 = dot_t((-total).astype(BF), f5[0:PANEL]).astype(BF)
    x5 = solve_back(f5, [], y5, [])
    x4 = solve_back(f4, [h4[...]], y4[...], [x5])
    x3 = solve_back(f3, [h3[:, 0:U], h3[:, U : 2 * U]], y3[...], [x4, x5])
    for k, x in enumerate((x3, x4, x5)):
        x_out[:, k * PANEL : (k + 1) * PANEL] = x


def level_two_back(place, mine, recv, f2, h2, y2, x_out):
    x = jnp.where(place[2] % 2 == 0, mine[...], recv[...])
    above = [x[:, k * PANEL : (k + 1) * PANEL] for k in range(3)]
    x_out[:, 0:PANEL] = solve_back(f2, [h2[:, k * U : (k + 1) * U] for k in range(3)], y2[...], above)
    x_out[:, PANEL:] = x


def level_one_back(
    place, mine, recv, y_mine, y_recv, factor, hots, rows_keep, rows_send, sep_keep, sep_send, x, sep_a, sep_b, sems
):
    side = place[1] // 2
    even = place[1] % 2 == 0
    x[pl.ds(pl.multiple_of(side * 64, 64), 64)] = mine[...]
    x[pl.ds(pl.multiple_of((1 - side) * 64, 64), 64)] = recv[...]
    above = [x[:, k * PANEL : (k + 1) * PANEL] for k in range(4)]
    ups = [hots[:, ONE + k * 3 * U + 2 * U : ONE + (k + 1) * 3 * U] for k in range(4)]
    x1 = solve_back(factor, ups, jnp.where(even, y_mine[...], y_recv[...]), above)
    level = jnp.where(place[1] < 2, 2, place[3])
    held = jnp.where(level == 0, jnp.zeros_like(x1), above[0])
    for k in (1, 2, 3):
        held = jnp.where(level == k + 2, above[k], held)
    sep_a[...] = jnp.where(even, x1, held)
    sep_b[...] = jnp.where(even, held, x1)
    stores = [
        pltpu.make_async_copy(sep_a, sep_keep, sems.at[0]),
        pltpu.make_async_copy(sep_b, sep_send, sems.at[1]),
    ]
    for store in stores:
        store.start()
    for l, value in enumerate([x1] + above):
        start = 0 if l == 0 else ONE + (l - 1) * 3 * U
        both = dot(value, hots[:, start : start + 2 * U]).astype(BF)
        left, right = both[:, 0:U], both[:, U : 2 * U]
        rows_keep[:, l * U : (l + 1) * U] = jnp.where(even, left, right)
        rows_send[:, l * U : (l + 1) * U] = jnp.where(even, right, left)
    for store in stores:
        store.wait()


def leaf_backward(place, keep, recv, inv, cpl, yt, chosen, x_leaf, picks_out, rows, sub, picks, sems):
    side = half_of(place)
    rows[pl.ds(pl.multiple_of(side * 128, 128), 128)] = keep[...]
    rows[pl.ds(pl.multiple_of((1 - side) * 128, 128), 128)] = recv[...]
    total = yt[...].astype(F32)
    for l in range(LEVELS):
        total = total - dot(rows[:, l * U : (l + 1) * U], cpl[l])
    sub[...] = total.astype(BF)
    for i in range(4):
        start = i * 256
        part = dot(sub[:, start:], inv[start:, start : start + 256])
        x_leaf[start : start + 256] = part.T.astype(BF)
    stores = []
    for i in range(2):
        part = slice(i * 256, (i + 1) * 256)
        picks[part] = dot(chosen[part], x_leaf[...]).astype(BF)
        stores.append(pltpu.make_async_copy(picks.at[part], picks_out.at[part], sems.at[i]))
        stores[-1].start()
    for store in stores:
        store.wait()


def sep_out(place, keep, recv, x_sep, keep_v, recv_v, xt, sems):
    loads = [
        pltpu.make_async_copy(keep, keep_v, sems.at[0]),
        pltpu.make_async_copy(recv, recv_v, sems.at[1]),
    ]
    for load in loads:
        load.start()
    for load in loads:
        load.wait()
    side = half_of(place)
    xt[pl.ds(pl.multiple_of(side * 128, 128), 128)] = keep_v[...].astype(F32)
    xt[pl.ds(pl.multiple_of((1 - side) * 128, 128), 128)] = recv_v[...].astype(F32)
    x_sep[...] = xt[...].T.astype(BF)


def stretch_sum(weight, got, out, weight_v, sems):
    load = pltpu.make_async_copy(weight, weight_v, sems.at[0])
    load.start()
    load.wait()
    out[...] = dot(weight_v[0], got[...]) + dot(weight_v[1], got[...])


def iota(rows, cols, axis):
    return lax.broadcasted_iota(jnp.int32, (rows, cols), axis)


def ones_where(mask):
    return jnp.where(mask, 1.0, 0.0)


def stay_plan(place, dofs, coef, chosen, weight_out, grid, turned, dof_t, coef_t, weight, sems):
    me = place[2] * RING + place[1]
    grid[...] = jnp.full((128, 128), -1, jnp.int32)
    for r in range(16):
        grid[8 * r : 8 * r + 6] = dofs[:, 128 * r : 128 * (r + 1)]
    dof = grid[...]
    match = ones_where((dof >> 10) == me)
    row, col = iota(128, 128, 0), iota(128, 128, 1)
    same = (row >> 3) == (col >> 3)
    earlier = ((row >> 6) == (col >> 6)) & (row < col)
    match_b = match.astype(BF)
    count = dot(ones_where(same).astype(BF), match_b).astype(BF)
    rank = dot(count, ones_where(earlier).astype(BF))
    rank = rank + dot(ones_where(same & (col < row)).astype(BF), match_b)
    high = ((dof >> 5) & 31).astype(F32) + 1.0
    low = (dof & 31).astype(F32)
    rank = jnp.where(match > 0.0, rank, -1.0)
    parts = []
    for value in (high, low):
        for s in range(SLOTS):
            parts.append(jnp.where(rank == float(s), value, 0.0).astype(BF))
    block = ones_where(iota(16, 128, 0) == (iota(16, 128, 1) >> 3)).astype(BF)
    flat = dot(block, jnp.concatenate(parts, axis=1)).astype(BF)
    width = SLOTS * 128
    lane, q = iota(width, 32, 0), iota(width, 32, 1)
    gather = ones_where(q == ((lane >> 6) & 1) * SLOTS + (lane >> 7)).astype(BF)
    table_high = dot(flat[:, 0:width], gather).astype(BF)
    table_low = dot(flat[:, width:], gather).astype(BF)
    spread = ones_where((iota(512, 16, 0) >> 5) == iota(512, 16, 1)).astype(BF)
    here = ones_where((iota(512, 32, 0) & 31) == iota(512, 32, 1))
    sel_high = jnp.sum(dot(spread, table_high) * here, axis=1, keepdims=True)
    sel_low = jnp.sum(dot(spread, table_low) * here, axis=1, keepdims=True)
    sel = (sel_high - 1.0) * 32.0 + sel_low
    for part in range(4):
        at = slice(part * 128, (part + 1) * 128)
        chosen[at] = ones_where(iota(128, LEAF, 1).astype(F32) == sel[at]).astype(BF)

    block_row = pl.multiple_of((me >> 1) * 8, 8)
    block_col = pl.multiple_of((me >> 1) * 128, 128)
    half = pl.ds(pl.multiple_of((me & 1) * 64, 64), 64)
    turned[...] = jnp.zeros_like(turned)
    turned[0:8] = grid[pl.ds(block_row, 8)].astype(F32)
    dof_t[...] = turned[...].T
    turned[0:6] = coef[:, pl.ds(block_col, 128)]
    coef_t[...] = turned[...].T
    my_dof, my_coef = dof_t[half], coef_t[half]
    lanes = iota(64, 32, 1)
    source = [my_dof[:, k : k + 1].astype(jnp.int32) >> 10 for k in range(6)]
    named = [ones_where(source[k] == lanes) for k in range(6)]
    every = named[0]
    for k in range(1, 6):
        every = every + named[k]
    lower = ones_where(iota(64, 64, 1) < iota(64, 64, 0)).astype(BF)
    running = dot(lower, every.astype(BF))
    total = jnp.zeros((64, 512), F32)
    slots = iota(64, 512, 1).astype(F32)
    for k in range(6):
        at = jnp.sum(named[k] * running, axis=1, keepdims=True)
        slot = source[k].astype(F32) * float(SLOTS) + at
        total = total + jnp.where(slots == slot, my_coef[:, k : k + 1], 0.0)
        running = running + named[k]
    first = total.astype(BF)
    weight[0] = first
    weight[1] = (total - first.astype(F32)).astype(BF)
    store = pltpu.make_async_copy(weight, weight_out, sems.at[0])
    store.start()
    store.wait()


def after(value, *others):
    return lax.optimization_barrier((value, *others))[0]


def on_device(
    rhs_leaf, rhs_sep, leaf_inv, leaf_cpl, leaf_idx, sep_inv, sep_cpl, sep_idx, stay_dofs, stay_coef
):
    rows_axis, cols_axis = "rows", "cols"
    columns, rows = lax.axis_size(cols_axis), lax.axis_size(rows_axis)
    me = lax.axis_index(rows_axis)
    core = lax.axis_index(cols_axis) % 2
    y, z = me % RING, me // RING
    top_level = jnp.where(z % 2 == 0, 3, jnp.where(z % 4 == 1, 4, jnp.where(z == 3, 5, 0)))
    place = jnp.stack([core, y, z, top_level]).astype(jnp.int32)

    def route(value, target):
        pairs = []
        for c in range(columns):
            for r in range(rows):
                to = target(c % 2, r % RING, r // RING)
                if to is not None:
                    pairs.append((c * rows + r, (c - c % 2 + to[0]) * rows + to[2] * RING + to[1]))
        return lax.ppermute(value, (cols_axis, rows_axis), pairs)

    def swap_core(value):
        return route(value, lambda c, y, z: (1 - c, y, z))

    def swap(value, flip):
        return route(value, lambda c, y, z: (c, y ^ flip, z))

    def to_odd(value):
        return route(value, lambda c, y, z: (c, y + 1, z) if y % 2 == 0 else None)

    own, own_up, codes = call(
        pack_factor,
        [pinned(packed_rows(4), PANEL), pinned(packed_rows(3), PANEL), pinned(4 * 16, U)],
        [place, sep_inv, sep_cpl.reshape(4 * U, PANEL), leaf_idx, sep_idx],
        [SMEM, HBM, HBM, HBM, HBM],
        [
            pltpu.VMEM((16, PANEL), F32),
            pltpu.VMEM((LEVELS, U), jnp.int32),
            pltpu.VMEM((LEVELS - 1, U), jnp.int32),
            dma(14),
        ],
    )
    with jax.named_scope("factors_to_neighbours"):
        near = route(own_up, lambda c, y, z: (c, y ^ (3 if c else 1), z) if y % 2 else None)
    yt, terms, rhs, one, inv_v, cpl_v = call(
        leaf_forward,
        [
            pinned(NC, LEAF),
            pinned(NC, PANEL),
            pinned(NC, PANEL),
            pinned(NC + 4 * 16, U),
            pinned(LEAF, LEAF),
            pinned(LEVELS, U, LEAF),
        ],
        [after(place, own), leaf_inv, rhs_leaf, leaf_cpl, rhs_sep, codes],
        [SMEM, HBM, HBM, HBM, HBM, VMEM],
        [pltpu.VMEM((LEAF, NC), BF), pltpu.VMEM((PANEL, NC), BF), pltpu.VMEM((LEAF, NC), F32), dma(7)],
    )
    with jax.named_scope("first_terms"):
        recv = swap(one, 1)

    def ready(slots, pick, sources, split=False):
        return call(
            functools.partial(stage, slots, pick, split, len(sources) // (2 if split else 1)),
            [pinned(factor_rows(slots), PANEL), pinned(PANEL, max(slots, 1) * U)],
            [place, *sources],
            [SMEM] + [ANY] * len(sources),
            [pltpu.VMEM((16, PANEL), BF), dma(7)],
        )

    def rise(level, panel, recv, factor, hots):
        slots = LEVELS - level
        return call(
            functools.partial(level_up, level),
            [pinned(64, PANEL), pinned(64, slots * PANEL)],
            [panel, recv, factor, hots],
            [VMEM] * 4,
        )

    f1, _ = ready(4, lambda core, y, z: (core >= 0,), [after(own, one)])
    (h1,) = call(
        stage_pair,
        [pinned(PANEL, ONE_HOTS)],
        [place, one, recv],
        [SMEM, VMEM, VMEM],
    )
    recv = after(recv, f1)
    y1, y1_send, keep, send = call(
        level_one,
        [pinned(128, PANEL), pinned(128, PANEL), pinned(128, 2 * PANEL), pinned(128, 2 * PANEL)],
        [place, one, recv, terms, rhs, f1, h1],
        [SMEM] + [VMEM] * 6,
        [pltpu.VMEM((NC, 2 * PANEL), BF)],
    )
    with jax.named_scope("terms_pair"):
        recv = swap(send, 1)
    chosen, weight = call(
        stay_plan,
        [pinned(32 * SLOTS, LEAF), stored(2, 64, 512)],
        [place, stay_dofs, after(stay_coef, send)],
        [SMEM, VMEM, VMEM],
        [
            pltpu.VMEM((128, 128), jnp.int32),
            pltpu.VMEM((128, 128), F32),
            pltpu.VMEM((128, 128), F32),
            pltpu.VMEM((128, 128), F32),
            pltpu.VMEM((2, 64, 512), BF),
            dma(1),
        ],
        [VMEM, HBM],
    )
    recv = after(recv, chosen)
    panel, send = call(
        join_pair,
        [pinned(64, 4 * PANEL), pinned(64, 4 * PANEL)],
        [place, keep, recv, h1],
        [SMEM] + [VMEM] * 3,
        [pltpu.VMEM((128, 4 * PANEL), BF)],
    )
    with jax.named_scope("panels_ring"):
        recv = swap(send, 3)
    near = after(near, keep)
    with jax.named_scope("near_to_core"):
        near_o = swap_core(near)
    with jax.named_scope("factors_across"):
        far = route(near, lambda c, y, z: (c, y ^ (1 if c else 3), z) if y % 2 == 0 else None)
    far = after(far, send)
    at = [own_up, near, near_o, far]
    f2, h2 = ready(3, pick_two, at)
    f3, h3, top, top_rest = call(
        stage_and_pass,
        [
            pinned(factor_rows(2), PANEL),
            pinned(PANEL, 2 * U),
            pinned(TRI, PANEL),
            pinned(16 + U, PANEL),
        ],
        [place, *at],
        [SMEM] + [ANY] * 4,
        [pltpu.VMEM((16, PANEL), BF), dma(9)],
    )

    def next_up(value):
        return route(value, lambda c, y, z: (c, y, (z + (1 if c else -1)) % DEPTH) if z % 2 else None)

    with jax.named_scope("factors_up"):
        up = next_up(top)
    with jax.named_scope("factors_up_rest"):
        rest = next_up(top_rest)
    recv = after(recv, f2, h2, f3, h3)
    y2, panel = rise(2, panel, recv, f2, h2)
    with jax.named_scope("panels_z1"):
        recv = route(panel, lambda c, y, z: (c, y, z - 1) if z % 2 else None)
    own_far, y1_far = after((own, y1_send), panel)
    with jax.named_scope("first_factor_to_odd"):
        own_far = to_odd(own_far)
    with jax.named_scope("first_solution_to_odd"):
        y1_far = to_odd(y1_far)
    y3, panel = rise(3, panel, recv, f3, h3)
    with jax.named_scope("panels_z2"):
        recv = route(panel, lambda c, y, z: (c, y, z ^ 2) if z % 2 == 0 else None)
    up, rest = after((up, rest), panel)
    with jax.named_scope("up_to_core"):
        up_o = swap_core(up)
    with jax.named_scope("rest_to_core"):
        rest_o = swap_core(rest)
    with jax.named_scope("factor_top"):
        last = route(
            up,
            lambda c, y, z: (c, y, 0) if (c, z) == (0, 2) else (c, y, 6) if (c, z) == (1, 4) else None,
        )
    f4, h4 = ready(1, pick_four, [up, rest, up_o, rest_o], True)
    recv = after(recv, f4, h4)
    y4, panel = rise(4, panel, recv, f4, h4)
    with jax.named_scope("panels_z3"):
        recv = route(panel, lambda c, y, z: (c, y, 6 - z) if z % 2 == 0 else None)
    last = after(last, panel)
    with jax.named_scope("last_to_core"):
        last_o = swap_core(last)
    f5, _ = ready(0, pick_five, [up, up_o, last, last_o])
    recv = after(recv, f5)
    (x,) = call(
        turn,
        [pinned(64, 3 * PANEL)],
        [panel, recv, f3, f4, f5, h3, h4, y3, y4],
        [VMEM] * 9,
    )
    with jax.named_scope("down_z1"):
        recv = route(x, lambda c, y, z: (c, y, z + 1) if z % 2 == 0 else None)
    (x,) = call(
        level_two_back,
        [pinned(64, 4 * PANEL)],
        [place, x, recv, f2, h2, y2],
        [SMEM] + [VMEM] * 5,
    )
    with jax.named_scope("down_ring"):
        recv = swap(x, 3)
    f1, _ = ready(4, pick_one, [own, after(own_far, x)])
    recv = after(recv, f1)
    rows_keep, rows_send, sep_keep, sep_send = call(
        level_one_back,
        [pinned(128, TERM), pinned(128, TERM), stored(128, PANEL), stored(128, PANEL)],
        [place, x, recv, y1, y1_far, f1, h1],
        [SMEM] + [VMEM] * 6,
        [
            pltpu.VMEM((128, 4 * PANEL), BF),
            pltpu.VMEM((128, PANEL), BF),
            pltpu.VMEM((128, PANEL), BF),
            dma(2),
        ],
        [VMEM, VMEM, HBM, HBM],
    )
    with jax.named_scope("rows_back"):
        recv = swap(rows_send, 1)
    with jax.named_scope("sep_back"):
        sep_recv = swap(sep_send, 1)
    x_leaf, picks = call(
        leaf_backward,
        [plain(LEAF, NC), stored(32 * SLOTS, NC)],
        [place, rows_keep, recv, inv_v, cpl_v, yt, chosen],
        [SMEM] + [VMEM] * 6,
        [
            pltpu.VMEM((NC, TERM), BF),
            pltpu.VMEM((NC, LEAF), BF),
            pltpu.VMEM((32 * SLOTS, NC), BF),
            dma(2),
        ],
        [VMEM, HBM],
    )
    got = lax.all_to_all(
        picks.reshape(32, SLOTS, NC), rows_axis, 0, 0, tiled=True
    ).reshape(32 * SLOTS, NC)
    (x_sep,) = call(
        sep_out,
        [plain(PANEL, NC)],
        [place, sep_keep, after(sep_recv, picks)],
        [SMEM, HBM, HBM],
        [pltpu.VMEM((128, PANEL), BF), pltpu.VMEM((128, PANEL), BF), pltpu.VMEM((NC, PANEL), F32), dma(2)],
    )
    (stretch,) = call(
        stretch_sum,
        [plain(64, NC, dtype=F32)],
        [weight, got],
        [HBM, VMEM],
        [pltpu.VMEM((2, 64, 512), BF), dma(1)],
    )
    return (x_leaf, x_sep, stretch)


def solution(mesh):
    return jax.shard_map(
        on_device,
        mesh=mesh,
        in_specs=(
            P("rows", "cols"),
            P("rows", "cols"),
            P("rows", None),
            P("rows", None, None, None),
            P("rows", None, None),
            P("rows", None),
            P("rows", None, None, None),
            P("rows", None, None),
            P(),
            P(),
        ),
        out_specs=(P("rows", "cols"), P("rows", "cols"), P("rows", "cols")),
        check_vma=False,
    )
```

```python
import functools

import jax
import jax.numpy as jnp
from jax import lax
from jax.experimental import pallas as pl
from jax.experimental.pallas import tpu as pltpu
from jax.sharding import PartitionSpec as P

BF = jnp.bfloat16
F32 = jnp.float32
LEAF, PANEL, U, NC, LEVELS = 1024, 512, 128, 256, 5
RING, DEPTH = 4, 8
TERM = LEVELS * U
SLOTS = 16
VMEM_LIMIT = 16 * 1024 * 1024

TRI = 320
IDX = slice(TRI, TRI + 16)
CPL0 = TRI + 16


def packed_rows(slots):
    return CPL0 + slots * U


def factor_rows(slots):
    return PANEL + slots * U


def triangle_blocks():
    return [
        (slice(384, 512), slice(0, 512), slice(0, 128), slice(0, 512)),
        (slice(256, 384), slice(0, 384), slice(128, 256), slice(0, 384)),
        (slice(0, 128), slice(0, 128), slice(128, 256), slice(384, 512)),
        (slice(128, 192), slice(0, 256), slice(256, 320), slice(0, 256)),
        (slice(192, 256), slice(0, 256), slice(256, 320), slice(256, 512)),
    ]


def dot(left, right):
    return jnp.dot(left, right, preferred_element_type=F32)


def dot_t(left, right):
    return lax.dot_general(left, right, (((1,), (1,)), ((), ())), preferred_element_type=F32)


VMEM = pl.BlockSpec(memory_space=pltpu.VMEM)
SMEM = pl.BlockSpec(memory_space=pltpu.SMEM)
HBM = pl.BlockSpec(memory_space=pltpu.HBM)
ANY = pl.BlockSpec(memory_space=pl.ANY)


def call(body, outs, args, specs, scratch=(), out_specs=None, aliases=None, flops=10**8, moved=10**6):
    args = [
        in_vmem(arg) if spec is VMEM else in_hbm(arg) if spec is HBM else arg
        for arg, spec in zip(args, specs)
    ]
    return pl.pallas_call(
        body,
        out_shape=outs,
        in_specs=specs,
        out_specs=out_specs or [VMEM] * len(outs),
        scratch_shapes=list(scratch),
        input_output_aliases=aliases or {},
        compiler_params=pltpu.CompilerParams(vmem_limit_bytes=VMEM_LIMIT),
        cost_estimate=pl.CostEstimate(flops=flops, bytes_accessed=moved, transcendentals=0),
    )(*args)


def dma(n):
    return pltpu.SemaphoreType.DMA((n,))


def pinned(*dims, dtype=BF):
    return pltpu.VMEM(dims, dtype)


def plain(*dims, dtype=BF):
    return jax.ShapeDtypeStruct(dims, dtype)


def stored(*dims, dtype=BF):
    return pltpu.HBM(dims, dtype)


def in_vmem(value):
    return pltpu.with_memory_space_constraint(value, pltpu.VMEM)


def in_hbm(value):
    return pltpu.with_memory_space_constraint(value, pltpu.HBM)


def hot(rows):
    place = lax.broadcasted_iota(jnp.int32, (PANEL, rows.shape[1]), 0).astype(F32)
    return jnp.where(place == rows, 1.0, 0.0).astype(BF)


def sep_rows(block):
    block = block.astype(F32)
    return [block[s : s + 1, 0:U] * 16.0 + block[s : s + 1, U : 2 * U] for s in range(LEVELS - 1)]


def push_values(factor, y, slots):
    return dot_t(y, factor[PANEL : PANEL + slots * U]).astype(BF)


def solve_back(factor, hots, y, above):
    back = y
    slots = len(above)
    if slots:
        taken = [dot(above[k], hots[k]).astype(BF) for k in range(slots)]
        taken = taken[0] if slots == 1 else jnp.concatenate(taken, axis=1)
        sub = dot(taken, factor[PANEL : PANEL + slots * U])
        back = (y.astype(F32) - sub).astype(BF)
    return dot(back, factor[0:PANEL]).astype(BF)


def pack_factor(place, inv, cpl, sep_idx, out, up, codes, sep_v, sems):
    load = pltpu.make_async_copy(sep_idx.at[0], sep_v, sems.at[0])
    copies = []
    for n, (dst, slots) in enumerate(((up, 3), (out, 4))):
        for i, (r, c, pr, pc) in enumerate(triangle_blocks()):
            copies.append(pltpu.make_async_copy(inv.at[r, c], dst.at[pr, pc], sems.at[1 + 6 * n + i]))
        copies.append(
            pltpu.make_async_copy(cpl.at[0 : slots * U], dst.at[CPL0 : packed_rows(slots)], sems.at[6 + 6 * n])
        )
    load.start()
    for copy in copies:
        copy.start()
    codes[...] = jnp.zeros_like(codes)
    out[packed_rows(4) :] = jnp.zeros((128, PANEL), BF)
    load.wait()
    value = sep_v[...]
    codes[0 : LEVELS - 1, 0:U] = (value >> 4).astype(F32)
    codes[0 : LEVELS - 1, U : 2 * U] = (value & 15).astype(F32)
    coded = codes[...].astype(BF)
    out[IDX] = coded
    up[IDX] = coded
    for copy in copies:
        copy.wait()


def leaf_first(
    place, inv, rhs, cpl, rsep, leaf_idx, sep_idx, yt, rhs_out, one, inv_v, cpl_v,
    rhs_v, rsep_v, leaf_v, sep_v, codes, sems
):
    loads = [
        pltpu.make_async_copy(leaf_idx.at[0], leaf_v, sems.at[0]),
        pltpu.make_async_copy(sep_idx.at[0], sep_v, sems.at[1]),
        pltpu.make_async_copy(rhs, rhs_v, sems.at[2]),
    ]
    for i in range(4):
        rows = pl.ds(i * 256, 256)
        loads.append(pltpu.make_async_copy(inv.at[rows], inv_v.at[rows], sems.at[3 + i]))
    loads.append(pltpu.make_async_copy(cpl.at[0], cpl_v, sems.at[7]))
    loads.append(pltpu.make_async_copy(rsep, rsep_v, sems.at[8]))
    for load in loads:
        load.start()
    codes[...] = jnp.zeros_like(codes)
    for ref, load, count, at in ((leaf_v, loads[0], LEVELS, 0), (sep_v, loads[1], LEVELS - 1, 32)):
        load.wait()
        value = ref[...]
        codes[at : at + count] = (value >> 4).astype(F32)
        codes[at + 16 : at + 16 + count] = (value & 15).astype(F32)
    one[NC:] = codes[...].astype(BF)
    loads[2].wait()
    rhs_t = rhs_v[...].astype(F32).T.astype(BF)
    for i in range(4):
        loads[3 + i].wait()
        span = (i + 1) * 256
        yt[:, i * 256 : span] = dot_t(rhs_t[:, 0:span], inv_v[i * 256 : span, 0:span]).astype(BF)
    loads[7].wait()
    one[0:NC] = dot_t(yt[...], cpl_v[0]).astype(BF)
    loads[8].wait()
    rhs_out[...] = rsep_v[...].astype(F32).T.astype(BF)


def leaf_second(yt, cpl_v, terms):
    for l in range(1, LEVELS):
        terms[:, (l - 1) * U : l * U] = dot_t(yt[...], cpl_v[l]).astype(BF)


def which(place):
    return place[0], place[1], place[2]


def pick_two(core, y, z):
    return (
        y == 1,
        ((y == 0) & (core == 0)) | ((y == 2) & (core == 1)),
        ((y == 0) & (core == 1)) | ((y == 2) & (core == 0)),
        y == 3,
    )


def pick_top(core, y, z):
    return (
        y == 3,
        ((y == 2) & (core == 0)) | ((y == 0) & (core == 1)),
        ((y == 2) & (core == 1)) | ((y == 0) & (core == 0)),
        y == 1,
    )


def pick_four(core, y, z):
    after_me = (z == 0) | (z == 4)
    first = core == 0
    return (after_me & first) | (~after_me & ~first), (after_me & ~first) | (~after_me & first)


def pick_five(core, y, z):
    inner = (z == 2) | (z == 4)
    first = core == 0
    low = (z == 2) | (z == 0)
    same = (low & first) | (~low & ~first)
    return inner & same, inner & ~same, ~inner & same, ~inner & ~same


def pick_one(core, y, z):
    even = (y == 0) | (y == 2)
    return even, ~even


def stage(slots, pick, split, count, place, *refs):
    if split:
        sources = [(refs[2 * i], refs[2 * i + 1], 0) for i in range(count)]
    else:
        sources = [(refs[i], refs[i], TRI) for i in range(count)]
    factor, hots, idx, sems = refs[(2 if split else 1) * count :]
    cases = pick(*which(place))

    def copies_of(triangle, rest, at):
        copies = [
            pltpu.make_async_copy(triangle.at[pr, pc], factor.at[r, c], sems.at[i])
            for i, (r, c, pr, pc) in enumerate(triangle_blocks())
        ]
        if slots:
            coupling = rest.at[at + 16 : at + 16 + slots * U]
            copies.append(pltpu.make_async_copy(coupling, factor.at[PANEL:], sems.at[5]))
            copies.append(pltpu.make_async_copy(rest.at[at : at + 16], idx, sems.at[6]))
        return copies

    for case, source in zip(cases, sources):

        @pl.when(case)
        def _(source=source):
            for copy in copies_of(*source):
                copy.start()

    for rows, cols in (
        (slice(0, 128), slice(128, 512)),
        (slice(128, 256), slice(256, 512)),
        (slice(256, 384), slice(384, 512)),
    ):
        factor[rows, cols] = jnp.zeros((rows.stop - rows.start, cols.stop - cols.start), BF)
    copies = copies_of(*sources[0])
    if slots:
        copies[-1].wait()
        taken = sep_rows(idx[...])
        for k in range(slots):
            hots[:, k * U : (k + 1) * U] = hot(taken[k])
        copies = copies[:-1]
    else:
        hots[...] = jnp.zeros_like(hots)
    for copy in copies:
        copy.wait()


def stage_and_pass(place, own, near, near_o, far, factor, hots, triangle, rest, idx, sems):
    sources = (own, near, near_o, far)

    def copies_of(source):
        return [
            pltpu.make_async_copy(source.at[0:TRI], triangle, sems.at[7]),
            pltpu.make_async_copy(source.at[TRI : packed_rows(1)], rest, sems.at[8]),
        ]

    for case, source in zip(pick_top(*which(place)), sources):

        @pl.when(case)
        def _(source=source):
            for copy in copies_of(source):
                copy.start()

    stage(2, pick_top, False, 4, place, *sources, factor, hots, idx, sems)
    for copy in copies_of(own):
        copy.wait()


ONE = 2 * U
PAIR_HOTS = 4 * 3 * U


def pair_rows(place, one, other):
    even = place[1] % 2 == 0
    mine, far = one[NC:], other[NC:]

    def rows(block, at, count):
        block = block.astype(F32)
        return [
            block[at + i : at + i + 1] * 16.0 + block[at + 16 + i : at + 17 + i] for i in range(count)
        ]

    left, right = jnp.where(even, mine, far), jnp.where(even, far, mine)
    return rows(left, 0, LEVELS), rows(right, 0, LEVELS), rows(left, 32, LEVELS - 1)


def stage_pair(place, one, other, hots):
    a, b, up = pair_rows(place, one, other)
    for k in range(4):
        at = k * 3 * U
        hots[:, at : at + 3 * U] = hot(jnp.concatenate([a[k + 1], b[k + 1], up[k]], axis=1))


def half_of(place):
    y = place[1]
    return jnp.where((y == 1) | (y == 2), 1, 0)


def level_one(place, one, recv, terms, rhs, factor, own, hots, y_keep, passed, keep, send, y_all):
    even = place[1] % 2 == 0
    a, b, _ = pair_rows(place, one, recv)
    hots[...] = hot(jnp.concatenate([a[0], b[0]], axis=1))
    total = dot_t(jnp.concatenate([one[0:NC], recv[0:NC]], axis=1), hots[...])
    resid = (rhs[...].astype(F32) - total).astype(BF)
    y = dot_t(resid, factor[0:PANEL]).astype(BF)
    y_all[:, 0:PANEL] = y
    y_all[:, PANEL:] = jnp.where(even, push_values(factor, y, 4), rhs[...])
    side = half_of(place)
    mine = pl.ds(pl.multiple_of(side * 128, 128), 128)
    theirs = pl.ds(pl.multiple_of((1 - side) * 128, 128), 128)
    send[:, 0:PANEL] = terms[theirs]
    send[:, PANEL:] = y_all[theirs, PANEL:]
    keep[:, 0:PANEL] = terms[mine]
    keep[:, PANEL:] = y_all[mine, PANEL:]
    y_keep[...] = y_all[mine, 0:PANEL]
    passed[packed_rows(4) :] = y_all[theirs, 0:PANEL]


def join_pair(place, keep, recv, hots, panel_keep, panel_send, panels):
    ring, even = place[1], place[1] % 2 == 0
    a, b = keep[...], recv[...]
    left, right = jnp.where(even, a, b), jnp.where(even, b, a)
    held = right[:, PANEL:].astype(F32)
    level = jnp.where(ring < 2, 2, place[3])
    for k in range(4):
        at = slice(k * U, (k + 1) * U)
        start = k * 3 * U
        parts = [left[:, at], right[:, at], left[:, PANEL + k * U : PANEL + (k + 1) * U]]
        total = dot_t(jnp.concatenate(parts, axis=1), hots[:, start : start + 3 * U])
        total = total - jnp.where(level == k + 2, held, 0.0)
        panels[:, k * PANEL : (k + 1) * PANEL] = total.astype(BF)
    side = ring // 2
    panel_keep[...] = panels[pl.ds(pl.multiple_of(side * 64, 64), 64)]
    panel_send[...] = panels[pl.ds(pl.multiple_of((1 - side) * 64, 64), 64)]


def level_up(level, mine, recv, factor, hots, y_out, panels):
    slots = LEVELS - level
    total = mine[...].astype(F32) + recv[...].astype(F32)
    y = dot_t((-total[:, 0:PANEL]).astype(BF), factor[0:PANEL]).astype(BF)
    y_out[...] = y
    values = push_values(factor, y, slots)
    for k in range(slots):
        at = slice((k + 1) * PANEL, (k + 2) * PANEL)
        term = dot_t(values[:, k * U : (k + 1) * U], hots[:, k * U : (k + 1) * U])
        panels[:, k * PANEL : (k + 1) * PANEL] = (total[:, at] + term).astype(BF)


def turn(mine, recv, f3, f4, f5, h3, h4, y3, y4, x_out):
    total = mine[...].astype(F32) + recv[...].astype(F32)
    y5 = dot_t((-total).astype(BF), f5[0:PANEL]).astype(BF)
    x5 = solve_back(f5, [], y5, [])
    x4 = solve_back(f4, [h4[...]], y4[...], [x5])
    x3 = solve_back(f3, [h3[:, 0:U], h3[:, U : 2 * U]], y3[...], [x4, x5])
    for k, x in enumerate((x3, x4, x5)):
        x_out[:, k * PANEL : (k + 1) * PANEL] = x


def level_two_back(place, mine, recv, f2, h2, y2, x_out):
    x = jnp.where(place[2] % 2 == 0, mine[...], recv[...])
    above = [x[:, k * PANEL : (k + 1) * PANEL] for k in range(3)]
    x_out[:, 0:PANEL] = solve_back(f2, [h2[:, k * U : (k + 1) * U] for k in range(3)], y2[...], above)
    x_out[:, PANEL:] = x


def level_one_back(
    place, mine, recv, y_mine, passed, factor, first_hots, hots, rows_keep, rows_send, sep_keep, sep_send, x, sep_a, sep_b, sems
):
    side = place[1] // 2
    even = place[1] % 2 == 0
    x[pl.ds(pl.multiple_of(side * 64, 64), 64)] = mine[...]
    x[pl.ds(pl.multiple_of((1 - side) * 64, 64), 64)] = recv[...]
    above = [x[:, k * PANEL : (k + 1) * PANEL] for k in range(4)]
    ups = [hots[:, k * 3 * U + 2 * U : (k + 1) * 3 * U] for k in range(4)]
    x1 = solve_back(factor, ups, jnp.where(even, y_mine[...], passed[packed_rows(4) :]), above)
    level = jnp.where(place[1] < 2, 2, place[3])
    held = jnp.where(level == 0, jnp.zeros_like(x1), above[0])
    for k in (1, 2, 3):
        held = jnp.where(level == k + 2, above[k], held)
    sep_a[...] = jnp.where(even, x1, held)
    sep_b[...] = jnp.where(even, held, x1)
    stores = [
        pltpu.make_async_copy(sep_a, sep_keep, sems.at[0]),
        pltpu.make_async_copy(sep_b, sep_send, sems.at[1]),
    ]
    for store in stores:
        store.start()
    for l, value in enumerate([x1] + above):
        pair = first_hots[...] if l == 0 else hots[:, (l - 1) * 3 * U : (l - 1) * 3 * U + 2 * U]
        both = dot(value, pair).astype(BF)
        left, right = both[:, 0:U], both[:, U : 2 * U]
        rows_keep[:, l * U : (l + 1) * U] = jnp.where(even, left, right)
        rows_send[:, l * U : (l + 1) * U] = jnp.where(even, right, left)
    for store in stores:
        store.wait()


def leaf_backward(place, keep, recv, inv, cpl, yt, chosen, xt_out, picks_out, rows, sub, xt, picks, sems):
    side = half_of(place)
    rows[pl.ds(pl.multiple_of(side * 128, 128), 128)] = keep[...]
    rows[pl.ds(pl.multiple_of((1 - side) * 128, 128), 128)] = recv[...]
    total = yt[...].astype(F32)
    for l in range(LEVELS):
        total = total - dot(rows[:, l * U : (l + 1) * U], cpl[l])
    sub[...] = total.astype(BF)
    for i in range(4):
        start = i * 256
        xt[:, start : start + 256] = dot(sub[:, start:], inv[start:, start : start + 256]).astype(BF)
    stores = [pltpu.make_async_copy(xt, xt_out, sems.at[2])]
    stores[0].start()
    for i in range(2):
        part = slice(i * 256, (i + 1) * 256)
        picks[part] = dot_t(chosen[part], xt[...]).astype(BF)
        stores.append(pltpu.make_async_copy(picks.at[part], picks_out.at[part], sems.at[i]))
        stores[-1].start()
    for store in stores:
        store.wait()


def turn_back(place, keep, recv, xt, x_sep, x_leaf, keep_v, recv_v, xt_v, both, sems):
    loads = [
        pltpu.make_async_copy(keep, keep_v, sems.at[0]),
        pltpu.make_async_copy(recv, recv_v, sems.at[1]),
        pltpu.make_async_copy(xt, xt_v, sems.at[2]),
    ]
    for load in loads:
        load.start()
    loads[2].wait()
    for i in range(4):
        part = slice(i * 256, (i + 1) * 256)
        x_leaf[part] = xt_v[:, part].astype(F32).T.astype(BF)
    for load in loads[:2]:
        load.wait()
    side = half_of(place)
    both[pl.ds(pl.multiple_of(side * 128, 128), 128)] = keep_v[...].astype(F32)
    both[pl.ds(pl.multiple_of((1 - side) * 128, 128), 128)] = recv_v[...].astype(F32)
    x_sep[...] = both[...].T.astype(BF)


def stretch_sum(weight, got, out, weight_v, sems):
    load = pltpu.make_async_copy(weight, weight_v, sems.at[0])
    load.start()
    load.wait()
    out[...] = dot(weight_v[0], got[...]) + dot(weight_v[1], got[...])


def iota(rows, cols, axis):
    return lax.broadcasted_iota(jnp.int32, (rows, cols), axis)


def ones_where(mask):
    return jnp.where(mask, 1.0, 0.0)


def stay_plan(place, dofs, coef, chosen, weight_out, grid, turned, dof_t, coef_t, weight, sems):
    me = place[2] * RING + place[1]
    grid[...] = jnp.full((128, 128), -1, jnp.int32)
    for r in range(16):
        grid[8 * r : 8 * r + 6] = dofs[:, 128 * r : 128 * (r + 1)]
    dof = grid[...]
    match = ones_where((dof >> 10) == me)
    row, col = iota(128, 128, 0), iota(128, 128, 1)
    same = (row >> 3) == (col >> 3)
    earlier = ((row >> 6) == (col >> 6)) & (row < col)
    match_b = match.astype(BF)
    count = dot(ones_where(same).astype(BF), match_b).astype(BF)
    rank = dot(count, ones_where(earlier).astype(BF))
    rank = rank + dot(ones_where(same & (col < row)).astype(BF), match_b)
    high = ((dof >> 5) & 31).astype(F32) + 1.0
    low = (dof & 31).astype(F32)
    rank = jnp.where(match > 0.0, rank, -1.0)
    parts = []
    for value in (high, low):
        for s in range(SLOTS):
            parts.append(jnp.where(rank == float(s), value, 0.0).astype(BF))
    block = ones_where(iota(16, 128, 0) == (iota(16, 128, 1) >> 3)).astype(BF)
    flat = dot(block, jnp.concatenate(parts, axis=1)).astype(BF)
    width = SLOTS * 128
    lane, q = iota(width, 32, 0), iota(width, 32, 1)
    gather = ones_where(q == ((lane >> 6) & 1) * SLOTS + (lane >> 7)).astype(BF)
    table_high = dot(flat[:, 0:width], gather).astype(BF)
    table_low = dot(flat[:, width:], gather).astype(BF)
    spread = ones_where((iota(512, 16, 0) >> 5) == iota(512, 16, 1)).astype(BF)
    here = ones_where((iota(512, 32, 0) & 31) == iota(512, 32, 1))
    sel_high = jnp.sum(dot(spread, table_high) * here, axis=1, keepdims=True)
    sel_low = jnp.sum(dot(spread, table_low) * here, axis=1, keepdims=True)
    sel = (sel_high - 1.0) * 32.0 + sel_low
    for part in range(4):
        at = slice(part * 128, (part + 1) * 128)
        chosen[at] = ones_where(iota(128, LEAF, 1).astype(F32) == sel[at]).astype(BF)

    block_row = pl.multiple_of((me >> 1) * 8, 8)
    block_col = pl.multiple_of((me >> 1) * 128, 128)
    half = pl.ds(pl.multiple_of((me & 1) * 64, 64), 64)
    turned[...] = jnp.zeros_like(turned)
    turned[0:8] = grid[pl.ds(block_row, 8)].astype(F32)
    dof_t[...] = turned[...].T
    turned[0:6] = coef[:, pl.ds(block_col, 128)]
    coef_t[...] = turned[...].T
    my_dof, my_coef = dof_t[half], coef_t[half]
    lanes = iota(64, 32, 1)
    source = [my_dof[:, k : k + 1].astype(jnp.int32) >> 10 for k in range(6)]
    named = [ones_where(source[k] == lanes) for k in range(6)]
    every = named[0]
    for k in range(1, 6):
        every = every + named[k]
    lower = ones_where(iota(64, 64, 1) < iota(64, 64, 0)).astype(BF)
    running = dot(lower, every.astype(BF))
    total = jnp.zeros((64, 512), F32)
    slots = iota(64, 512, 1).astype(F32)
    for k in range(6):
        at = jnp.sum(named[k] * running, axis=1, keepdims=True)
        slot = source[k].astype(F32) * float(SLOTS) + at
        total = total + jnp.where(slots == slot, my_coef[:, k : k + 1], 0.0)
        running = running + named[k]
    first = total.astype(BF)
    weight[0] = first
    weight[1] = (total - first.astype(F32)).astype(BF)
    store = pltpu.make_async_copy(weight, weight_out, sems.at[0])
    store.start()
    store.wait()


def after(value, *others):
    return lax.optimization_barrier((value, *others))[0]


def on_device(
    rhs_leaf, rhs_sep, leaf_inv, leaf_cpl, leaf_idx, sep_inv, sep_cpl, sep_idx, stay_dofs, stay_coef
):
    rows_axis, cols_axis = "rows", "cols"
    columns, rows = lax.axis_size(cols_axis), lax.axis_size(rows_axis)
    me = lax.axis_index(rows_axis)
    core = lax.axis_index(cols_axis) % 2
    y, z = me % RING, me // RING
    top_level = jnp.where(z % 2 == 0, 3, jnp.where(z % 4 == 1, 4, jnp.where(z == 3, 5, 0)))
    place = jnp.stack([core, y, z, top_level]).astype(jnp.int32)

    def route(value, target):
        pairs = []
        for c in range(columns):
            for r in range(rows):
                to = target(c % 2, r % RING, r // RING)
                if to is not None:
                    pairs.append((c * rows + r, (c - c % 2 + to[0]) * rows + to[2] * RING + to[1]))
        return lax.ppermute(value, (cols_axis, rows_axis), pairs)

    def swap_core(value):
        return route(value, lambda c, y, z: (1 - c, y, z))

    def swap(value, flip):
        return route(value, lambda c, y, z: (c, y ^ flip, z))

    def to_odd(value):
        return route(value, lambda c, y, z: (c, y + 1, z) if y % 2 == 0 else None)

    own, own_up = call(
        pack_factor,
        [pinned(packed_rows(4) + 128, PANEL), pinned(packed_rows(3), PANEL)],
        [place, sep_inv, sep_cpl.reshape(4 * U, PANEL), sep_idx],
        [SMEM, HBM, HBM, HBM],
        [pltpu.VMEM((16, PANEL), F32), pltpu.VMEM((LEVELS - 1, U), jnp.int32), dma(13)],
    )
    with jax.named_scope("factors_to_neighbours"):
        near = route(own_up, lambda c, y, z: (c, y ^ (3 if c else 1), z) if y % 2 else None)
    yt, rhs, one, inv_v, cpl_v = call(
        leaf_first,
        [
            pinned(NC, LEAF),
            pinned(NC, PANEL),
            pinned(NC + 4 * 16, U),
            pinned(LEAF, LEAF),
            pinned(LEVELS, U, LEAF),
        ],
        [place, leaf_inv, rhs_leaf, leaf_cpl, rhs_sep, after(leaf_idx, own), sep_idx],
        [SMEM] + [HBM] * 6,
        [
            pltpu.VMEM((LEAF, NC), BF),
            pltpu.VMEM((PANEL, NC), BF),
            pltpu.VMEM((LEVELS, U), jnp.int32),
            pltpu.VMEM((LEVELS - 1, U), jnp.int32),
            pltpu.VMEM((64, U), F32),
            dma(9),
        ],
    )
    with jax.named_scope("first_terms"):
        recv = swap(one, 1)
    (terms,) = call(
        leaf_second, [pinned(NC, PANEL)], [yt, cpl_v], [VMEM, VMEM]
    )

    def ready(slots, pick, sources, split=False):
        return call(
            functools.partial(stage, slots, pick, split, len(sources) // (2 if split else 1)),
            [pinned(factor_rows(slots), PANEL), pinned(PANEL, max(slots, 1) * U)],
            [place, *sources],
            [SMEM] + [ANY] * len(sources),
            [pltpu.VMEM((16, PANEL), BF), dma(7)],
        )

    def rise(level, panel, recv, factor, hots):
        slots = LEVELS - level
        return call(
            functools.partial(level_up, level),
            [pinned(64, PANEL), pinned(64, slots * PANEL)],
            [panel, recv, factor, hots],
            [VMEM] * 4,
        )

    f1, _ = ready(4, lambda core, y, z: (core >= 0,), [after(own, one)])
    near = after(near, recv, f1, terms)
    with jax.named_scope("factors_across"):
        far = route(near, lambda c, y, z: (c, y ^ (1 if c else 3), z) if y % 2 == 0 else None)
    with jax.named_scope("near_to_core"):
        near_o = swap_core(near)
    first = after(recv, f1)
    first_hots, y1, passed, keep, send = call(
        level_one,
        [
            pinned(PANEL, ONE),
            pinned(128, PANEL),
            pinned(packed_rows(4) + 128, PANEL),
            pinned(128, 2 * PANEL),
            pinned(128, 2 * PANEL),
        ],
        [place, one, first, terms, rhs, f1, own],
        [SMEM] + [VMEM] * 6,
        [pltpu.VMEM((NC, 2 * PANEL), BF)],
        aliases={6: 2},
    )
    with jax.named_scope("terms_pair"):
        recv = swap(send, 1)
    chosen, weight = call(
        stay_plan,
        [pinned(32 * SLOTS, LEAF), stored(2, 64, 512)],
        [place, stay_dofs, after(stay_coef, send)],
        [SMEM, VMEM, VMEM],
        [
            pltpu.VMEM((128, 128), jnp.int32),
            pltpu.VMEM((128, 128), F32),
            pltpu.VMEM((128, 128), F32),
            pltpu.VMEM((128, 128), F32),
            pltpu.VMEM((2, 64, 512), BF),
            dma(1),
        ],
        [VMEM, HBM],
    )
    (h1,) = call(
        stage_pair, [pinned(PANEL, PAIR_HOTS)], [place, one, after(first, send)], [SMEM, VMEM, VMEM]
    )
    recv = after(recv, chosen, h1)
    panel, send = call(
        join_pair,
        [pinned(64, 4 * PANEL), pinned(64, 4 * PANEL)],
        [place, keep, recv, h1],
        [SMEM] + [VMEM] * 3,
        [pltpu.VMEM((128, 4 * PANEL), BF)],
    )
    with jax.named_scope("panels_ring"):
        recv = swap(send, 3)
    far = after(far, send)
    at = [own_up, near, near_o, far]
    f2, h2 = ready(3, pick_two, at)
    f3, h3, top, top_rest = call(
        stage_and_pass,
        [
            pinned(factor_rows(2), PANEL),
            pinned(PANEL, 2 * U),
            pinned(TRI, PANEL),
            pinned(16 + U, PANEL),
        ],
        [place, *at],
        [SMEM] + [ANY] * 4,
        [pltpu.VMEM((16, PANEL), BF), dma(9)],
    )

    def next_up(value):
        return route(value, lambda c, y, z: (c, y, (z + (1 if c else -1)) % DEPTH) if z % 2 else None)

    with jax.named_scope("factors_up"):
        up = next_up(top)
    with jax.named_scope("factor_top"):
        last = route(
            top,
            lambda c, y, z: (0, y, 0) if (c, z) == (0, 3) else (1, y, 6) if (c, z) == (1, 3) else None,
        )
    with jax.named_scope("factors_up_rest"):
        rest = next_up(top_rest)
    with jax.named_scope("first_factor_to_odd"):
        passed_far = to_odd(after(passed, f2))
    recv = after(recv, f2, h2, f3, h3)
    y2, panel = rise(2, panel, recv, f2, h2)
    with jax.named_scope("panels_z1"):
        recv = route(panel, lambda c, y, z: (c, y, z - 1) if z % 2 else None)
    up, rest, last = after((up, rest, last), recv)
    with jax.named_scope("up_to_core"):
        up_o = swap_core(up)
    with jax.named_scope("rest_to_core"):
        rest_o = swap_core(rest)
    with jax.named_scope("last_to_core"):
        last_o = swap_core(last)
    y3, panel = rise(3, panel, recv, f3, h3)
    with jax.named_scope("panels_z2"):
        recv = route(panel, lambda c, y, z: (c, y, z ^ 2) if z % 2 == 0 else None)
    up, rest, last, up_o, rest_o, last_o = after((up, rest, last, up_o, rest_o, last_o), panel)
    f4, h4 = ready(1, pick_four, [up, rest, up_o, rest_o], True)
    f5, _ = ready(0, pick_five, [up, up_o, last, last_o])
    recv = after(recv, f4, h4, f5)
    y4, panel = rise(4, panel, recv, f4, h4)
    with jax.named_scope("panels_z3"):
        recv = route(panel, lambda c, y, z: (c, y, 6 - z) if z % 2 == 0 else None)
    (x,) = call(
        turn,
        [pinned(64, 3 * PANEL)],
        [panel, recv, f3, f4, f5, h3, h4, y3, y4],
        [VMEM] * 9,
    )
    with jax.named_scope("down_z1"):
        recv = route(x, lambda c, y, z: (c, y, z + 1) if z % 2 == 0 else None)
    (x,) = call(
        level_two_back,
        [pinned(64, 4 * PANEL)],
        [place, x, recv, f2, h2, y2],
        [SMEM] + [VMEM] * 5,
    )
    with jax.named_scope("down_ring"):
        recv = swap(x, 3)
    passed_far = after(passed_far, x)
    f1, _ = ready(4, pick_one, [passed, passed_far])
    recv = after(recv, f1)
    rows_keep, rows_send, sep_keep, sep_send = call(
        level_one_back,
        [pinned(128, TERM), pinned(128, TERM), stored(128, PANEL), stored(128, PANEL)],
        [place, x, recv, y1, passed_far, f1, first_hots, h1],
        [SMEM] + [VMEM] * 7,
        [
            pltpu.VMEM((128, 4 * PANEL), BF),
            pltpu.VMEM((128, PANEL), BF),
            pltpu.VMEM((128, PANEL), BF),
            dma(2),
        ],
        [VMEM, VMEM, HBM, HBM],
    )
    with jax.named_scope("rows_back"):
        recv = swap(rows_send, 1)
    with jax.named_scope("sep_back"):
        sep_recv = swap(after(sep_send, recv), 1)
    xt, picks = call(
        leaf_backward,
        [stored(NC, LEAF), stored(32 * SLOTS, NC)],
        [place, rows_keep, recv, inv_v, cpl_v, yt, chosen],
        [SMEM] + [VMEM] * 6,
        [
            pltpu.VMEM((NC, TERM), BF),
            pltpu.VMEM((NC, LEAF), BF),
            pltpu.VMEM((NC, LEAF), BF),
            pltpu.VMEM((32 * SLOTS, NC), BF),
            dma(3),
        ],
        [HBM, HBM],
        moved=14 * 10**6,
    )
    sep_recv = after(sep_recv, picks)
    got = lax.all_to_all(
        picks.reshape(32, SLOTS, NC), rows_axis, 0, 0, tiled=True
    ).reshape(32 * SLOTS, NC)
    x_sep, x_leaf = call(
        turn_back,
        [plain(PANEL, NC), plain(LEAF, NC)],
        [place, sep_keep, sep_recv, xt],
        [SMEM, HBM, HBM, HBM],
        [
            pltpu.VMEM((128, PANEL), BF),
            pltpu.VMEM((128, PANEL), BF),
            pltpu.VMEM((NC, LEAF), BF),
            pltpu.VMEM((NC, PANEL), F32),
            dma(3),
        ],
    )
    (stretch,) = call(
        stretch_sum,
        [plain(64, NC, dtype=F32)],
        [weight, got],
        [HBM, VMEM],
        [pltpu.VMEM((2, 64, 512), BF), dma(1)],
    )
    return (x_leaf, x_sep, stretch)


def solution(mesh):
    return jax.shard_map(
        on_device,
        mesh=mesh,
        in_specs=(
            P("rows", "cols"),
            P("rows", "cols"),
            P("rows", None),
            P("rows", None, None, None),
            P("rows", None, None),
            P("rows", None),
            P("rows", None, None, None),
            P("rows", None, None),
            P(),
            P(),
        ),
        out_specs=(P("rows", "cols"), P("rows", "cols"), P("rows", "cols")),
        check_vma=False,
    )
```

```python
import functools

import jax
import jax.numpy as jnp
from jax import lax
from jax.experimental import pallas as pl
from jax.experimental.pallas import tpu as pltpu
from jax.sharding import PartitionSpec as P

BF = jnp.bfloat16
F32 = jnp.float32
LEAF, PANEL, U, NC, LEVELS = 1024, 512, 128, 256, 5
RING, DEPTH = 4, 8
TERM = LEVELS * U
SLOTS = 16
VMEM_LIMIT = 16 * 1024 * 1024

TRI = 320
IDX = slice(TRI, TRI + 16)
CPL0 = TRI + 16


def packed_rows(slots):
    return CPL0 + slots * U


def factor_rows(slots):
    return PANEL + slots * U


def triangle_blocks():
    return [
        (slice(384, 512), slice(0, 512), slice(0, 128), slice(0, 512)),
        (slice(256, 384), slice(0, 384), slice(128, 256), slice(0, 384)),
        (slice(0, 128), slice(0, 128), slice(128, 256), slice(384, 512)),
        (slice(128, 192), slice(0, 256), slice(256, 320), slice(0, 256)),
        (slice(192, 256), slice(0, 256), slice(256, 320), slice(256, 512)),
    ]


def dot(left, right):
    return jnp.dot(left, right, preferred_element_type=F32)


def dot_t(left, right):
    return lax.dot_general(left, right, (((1,), (1,)), ((), ())), preferred_element_type=F32)


VMEM = pl.BlockSpec(memory_space=pltpu.VMEM)
SMEM = pl.BlockSpec(memory_space=pltpu.SMEM)
HBM = pl.BlockSpec(memory_space=pltpu.HBM)
ANY = pl.BlockSpec(memory_space=pl.ANY)


def call(body, outs, args, specs, scratch=(), out_specs=None, aliases=None, flops=10**8, moved=10**6):
    args = [
        in_vmem(arg) if spec is VMEM else in_hbm(arg) if spec is HBM else arg
        for arg, spec in zip(args, specs)
    ]
    return pl.pallas_call(
        body,
        out_shape=outs,
        in_specs=specs,
        out_specs=out_specs or [VMEM] * len(outs),
        scratch_shapes=list(scratch),
        input_output_aliases=aliases or {},
        compiler_params=pltpu.CompilerParams(vmem_limit_bytes=VMEM_LIMIT),
        cost_estimate=pl.CostEstimate(flops=flops, bytes_accessed=moved, transcendentals=0),
    )(*args)


def dma(n):
    return pltpu.SemaphoreType.DMA((n,))


def pinned(*dims, dtype=BF):
    return pltpu.VMEM(dims, dtype)


def plain(*dims, dtype=BF):
    return jax.ShapeDtypeStruct(dims, dtype)


def stored(*dims, dtype=BF):
    return pltpu.HBM(dims, dtype)


def in_vmem(value):
    return pltpu.with_memory_space_constraint(value, pltpu.VMEM)


def in_hbm(value):
    return pltpu.with_memory_space_constraint(value, pltpu.HBM)


def hot(rows):
    place = lax.broadcasted_iota(jnp.int32, (PANEL, rows.shape[1]), 0).astype(F32)
    return jnp.where(place == rows, 1.0, 0.0).astype(BF)


def sep_rows(block):
    block = block.astype(F32)
    return [block[s : s + 1, 0:U] * 16.0 + block[s : s + 1, U : 2 * U] for s in range(LEVELS - 1)]


def push_values(factor, y, slots):
    return dot_t(y, factor[PANEL : PANEL + slots * U]).astype(BF)


def solve_back(factor, hots, y, above):
    back = y
    slots = len(above)
    if slots:
        taken = [dot(above[k], hots[k]).astype(BF) for k in range(slots)]
        taken = taken[0] if slots == 1 else jnp.concatenate(taken, axis=1)
        sub = dot(taken, factor[PANEL : PANEL + slots * U])
        back = (y.astype(F32) - sub).astype(BF)
    return dot(back, factor[0:PANEL]).astype(BF)


def pack_factor(place, inv, cpl, sep_idx, up, codes, sep_v, sems):
    load = pltpu.make_async_copy(sep_idx.at[0], sep_v, sems.at[0])
    copies = [
        pltpu.make_async_copy(inv.at[r, c], up.at[pr, pc], sems.at[1 + i])
        for i, (r, c, pr, pc) in enumerate(triangle_blocks())
    ]
    copies.append(pltpu.make_async_copy(cpl.at[0 : 3 * U], up.at[CPL0 : packed_rows(3)], sems.at[6]))
    load.start()
    for copy in copies:
        copy.start()
    codes[...] = jnp.zeros_like(codes)
    load.wait()
    value = sep_v[...]
    codes[0 : LEVELS - 1, 0:U] = (value >> 4).astype(F32)
    codes[0 : LEVELS - 1, U : 2 * U] = (value & 15).astype(F32)
    up[IDX] = codes[...].astype(BF)
    for copy in copies:
        copy.wait()


def load_first(inv, cpl, out, sems):
    copies = [
        pltpu.make_async_copy(inv, out.at[0:PANEL], sems.at[0]),
        pltpu.make_async_copy(cpl, out.at[PANEL : 2 * PANEL], sems.at[1]),
    ]
    for copy in copies:
        copy.start()
    out[2 * PANEL :] = jnp.zeros((128, PANEL), BF)
    for copy in copies:
        copy.wait()


def pick_first(place, own, far, factor, sems):
    even = place[1] % 2 == 0
    copies = [
        pltpu.make_async_copy(source, factor, sems.at[0]) for source in (own, far)
    ]

    @pl.when(even)
    def _():
        copies[0].start()

    @pl.when(jnp.logical_not(even))
    def _():
        copies[1].start()

    copies[0].wait()


def leaf_first(
    place, inv, rhs, cpl, rsep, leaf_idx, sep_idx, yt, rhs_out, one, inv_v, cpl_v,
    rhs_v, rsep_v, leaf_v, sep_v, codes, sems
):
    loads = [
        pltpu.make_async_copy(leaf_idx, leaf_v, sems.at[0]),
        pltpu.make_async_copy(sep_idx.at[0], sep_v, sems.at[1]),
        pltpu.make_async_copy(rhs, rhs_v, sems.at[2]),
    ]
    for i in range(4):
        rows = pl.ds(i * 256, 256)
        loads.append(pltpu.make_async_copy(inv.at[rows], inv_v.at[rows], sems.at[3 + i]))
    loads.append(pltpu.make_async_copy(cpl.at[0], cpl_v, sems.at[7]))
    loads.append(pltpu.make_async_copy(rsep, rsep_v, sems.at[8]))
    for load in loads:
        load.start()
    codes[...] = jnp.zeros_like(codes)
    loads[0].wait()
    for l in range(LEVELS):
        value = leaf_v[l]
        codes[l : l + 1] = (value >> 4).astype(F32)
        codes[16 + l : 17 + l] = (value & 15).astype(F32)
    loads[1].wait()
    value = sep_v[...]
    codes[32 : 32 + LEVELS - 1] = (value >> 4).astype(F32)
    codes[48 : 48 + LEVELS - 1] = (value & 15).astype(F32)
    one[NC:] = codes[...].astype(BF)
    loads[2].wait()
    rhs_t = rhs_v[...].astype(F32).T.astype(BF)
    for i in range(4):
        loads[3 + i].wait()
        span = (i + 1) * 256
        yt[:, i * 256 : span] = dot_t(rhs_t[:, 0:span], inv_v[i * 256 : span, 0:span]).astype(BF)
    loads[7].wait()
    one[0:NC] = dot_t(yt[...], cpl_v[0]).astype(BF)
    loads[8].wait()
    rhs_out[...] = rsep_v[...].astype(F32).T.astype(BF)


def leaf_second(yt, cpl_v, terms):
    for l in range(1, LEVELS):
        terms[:, (l - 1) * U : l * U] = dot_t(yt[...], cpl_v[l]).astype(BF)


def which(place):
    return place[0], place[1], place[2]


def pick_two(core, y, z):
    return (
        y == 1,
        ((y == 0) & (core == 0)) | ((y == 2) & (core == 1)),
        ((y == 0) & (core == 1)) | ((y == 2) & (core == 0)),
        y == 3,
    )


def pick_top(core, y, z):
    return (
        y == 3,
        ((y == 2) & (core == 0)) | ((y == 0) & (core == 1)),
        ((y == 2) & (core == 1)) | ((y == 0) & (core == 0)),
        y == 1,
    )


def pick_four(core, y, z):
    after_me = (z == 0) | (z == 4)
    first = core == 0
    return (after_me & first) | (~after_me & ~first), (after_me & ~first) | (~after_me & first)


def pick_five(core, y, z):
    inner = (z == 2) | (z == 4)
    first = core == 0
    low = (z == 2) | (z == 0)
    same = (low & first) | (~low & ~first)
    return inner & same, inner & ~same, ~inner & same, ~inner & ~same


def pick_one(core, y, z):
    even = (y == 0) | (y == 2)
    return even, ~even


def stage(slots, pick, split, count, place, *refs):
    if split:
        sources = [(refs[2 * i], refs[2 * i + 1], 0) for i in range(count)]
    else:
        sources = [(refs[i], refs[i], TRI) for i in range(count)]
    factor, hots, idx, sems = refs[(2 if split else 1) * count :]
    cases = pick(*which(place))

    def copies_of(triangle, rest, at):
        copies = [
            pltpu.make_async_copy(triangle.at[pr, pc], factor.at[r, c], sems.at[i])
            for i, (r, c, pr, pc) in enumerate(triangle_blocks())
        ]
        if slots:
            coupling = rest.at[at + 16 : at + 16 + slots * U]
            copies.append(pltpu.make_async_copy(coupling, factor.at[PANEL:], sems.at[5]))
            copies.append(pltpu.make_async_copy(rest.at[at : at + 16], idx, sems.at[6]))
        return copies

    for case, source in zip(cases, sources):

        @pl.when(case)
        def _(source=source):
            for copy in copies_of(*source):
                copy.start()

    for rows, cols in (
        (slice(0, 128), slice(128, 512)),
        (slice(128, 256), slice(256, 512)),
        (slice(256, 384), slice(384, 512)),
    ):
        factor[rows, cols] = jnp.zeros((rows.stop - rows.start, cols.stop - cols.start), BF)
    copies = copies_of(*sources[0])
    if slots:
        copies[-1].wait()
        taken = sep_rows(idx[...])
        for k in range(slots):
            hots[:, k * U : (k + 1) * U] = hot(taken[k])
        copies = copies[:-1]
    else:
        hots[...] = jnp.zeros_like(hots)
    for copy in copies:
        copy.wait()


def stage_and_pass(place, own, near, near_o, far, factor, hots, triangle, rest, idx, sems):
    sources = (own, near, near_o, far)

    def copies_of(source):
        return [
            pltpu.make_async_copy(source.at[0:TRI], triangle, sems.at[7]),
            pltpu.make_async_copy(source.at[TRI : packed_rows(1)], rest, sems.at[8]),
        ]

    for case, source in zip(pick_top(*which(place)), sources):

        @pl.when(case)
        def _(source=source):
            for copy in copies_of(source):
                copy.start()

    stage(2, pick_top, False, 4, place, *sources, factor, hots, idx, sems)
    for copy in copies_of(own):
        copy.wait()


ONE = 2 * U
PAIR_HOTS = 4 * 3 * U


def pair_rows(place, one, other):
    even = place[1] % 2 == 0
    mine, far = one[NC:], other[NC:]

    def rows(block, at, count):
        block = block.astype(F32)
        return [
            block[at + i : at + i + 1] * 16.0 + block[at + 16 + i : at + 17 + i] for i in range(count)
        ]

    left, right = jnp.where(even, mine, far), jnp.where(even, far, mine)
    return rows(left, 0, LEVELS), rows(right, 0, LEVELS), rows(left, 32, LEVELS - 1)


def stage_pair(place, one, other, hots):
    a, b, up = pair_rows(place, one, other)
    for k in range(4):
        at = k * 3 * U
        hots[:, at : at + 3 * U] = hot(jnp.concatenate([a[k + 1], b[k + 1], up[k]], axis=1))


def half_of(place):
    y = place[1]
    return jnp.where((y == 1) | (y == 2), 1, 0)


def level_one(place, one, recv, terms, rhs, factor, hots, y_keep, passed, keep, send, y_all):
    even = place[1] % 2 == 0
    a, b, _ = pair_rows(place, one, recv)
    hots[...] = hot(jnp.concatenate([a[0], b[0]], axis=1))
    total = dot_t(jnp.concatenate([one[0:NC], recv[0:NC]], axis=1), hots[...])
    resid = (rhs[...].astype(F32) - total).astype(BF)
    y = dot_t(resid, factor[0:PANEL]).astype(BF)
    y_all[:, 0:PANEL] = y
    y_all[:, PANEL:] = jnp.where(even, push_values(factor, y, 4), rhs[...])
    side = half_of(place)
    mine = pl.ds(pl.multiple_of(side * 128, 128), 128)
    theirs = pl.ds(pl.multiple_of((1 - side) * 128, 128), 128)
    send[:, 0:PANEL] = terms[theirs]
    send[:, PANEL:] = y_all[theirs, PANEL:]
    keep[:, 0:PANEL] = terms[mine]
    keep[:, PANEL:] = y_all[mine, PANEL:]
    y_keep[...] = y_all[mine, 0:PANEL]
    passed[2 * PANEL :] = y_all[theirs, 0:PANEL]


def join_pair(place, keep, recv, hots, panel_keep, panel_send, panels):
    ring, even = place[1], place[1] % 2 == 0
    a, b = keep[...], recv[...]
    left, right = jnp.where(even, a, b), jnp.where(even, b, a)
    held = right[:, PANEL:].astype(F32)
    level = jnp.where(ring < 2, 2, place[3])
    for k in range(4):
        at = slice(k * U, (k + 1) * U)
        start = k * 3 * U
        parts = [left[:, at], right[:, at], left[:, PANEL + k * U : PANEL + (k + 1) * U]]
        total = dot_t(jnp.concatenate(parts, axis=1), hots[:, start : start + 3 * U])
        total = total - jnp.where(level == k + 2, held, 0.0)
        panels[:, k * PANEL : (k + 1) * PANEL] = total.astype(BF)
    side = ring // 2
    panel_keep[...] = panels[pl.ds(pl.multiple_of(side * 64, 64), 64)]
    panel_send[...] = panels[pl.ds(pl.multiple_of((1 - side) * 64, 64), 64)]


def level_up(level, mine, recv, factor, hots, y_out, panels):
    slots = LEVELS - level
    total = mine[...].astype(F32) + recv[...].astype(F32)
    y = dot_t((-total[:, 0:PANEL]).astype(BF), factor[0:PANEL]).astype(BF)
    y_out[...] = y
    values = push_values(factor, y, slots)
    for k in range(slots):
        at = slice((k + 1) * PANEL, (k + 2) * PANEL)
        term = dot_t(values[:, k * U : (k + 1) * U], hots[:, k * U : (k + 1) * U])
        panels[:, k * PANEL : (k + 1) * PANEL] = (total[:, at] + term).astype(BF)


def turn(mine, recv, f3, f4, f5, h3, h4, y3, y4, x_out):
    total = mine[...].astype(F32) + recv[...].astype(F32)
    y5 = dot_t((-total).astype(BF), f5[0:PANEL]).astype(BF)
    x5 = solve_back(f5, [], y5, [])
    x4 = solve_back(f4, [h4[...]], y4[...], [x5])
    x3 = solve_back(f3, [h3[:, 0:U], h3[:, U : 2 * U]], y3[...], [x4, x5])
    for k, x in enumerate((x3, x4, x5)):
        x_out[:, k * PANEL : (k + 1) * PANEL] = x


def level_two_back(place, mine, recv, f2, h2, y2, x_out):
    x = jnp.where(place[2] % 2 == 0, mine[...], recv[...])
    above = [x[:, k * PANEL : (k + 1) * PANEL] for k in range(3)]
    x_out[:, 0:PANEL] = solve_back(f2, [h2[:, k * U : (k + 1) * U] for k in range(3)], y2[...], above)
    x_out[:, PANEL:] = x


def level_one_back(place, mine, recv, y_mine, factor, first_hots, hots, x1_out, x, rows_send):
    side = place[1] // 2
    even = place[1] % 2 == 0
    x[pl.ds(pl.multiple_of(side * 64, 64), 64)] = mine[...]
    x[pl.ds(pl.multiple_of((1 - side) * 64, 64), 64)] = recv[...]
    above = [x[:, k * PANEL : (k + 1) * PANEL] for k in range(4)]
    ups = [hots[:, k * 3 * U + 2 * U : (k + 1) * 3 * U] for k in range(4)]
    x1 = solve_back(factor, ups, jnp.where(even, y_mine[...], factor[2 * PANEL :]), above)
    x1_out[...] = x1
    for l, value in enumerate([x1] + above):
        pair = first_hots[...] if l == 0 else hots[:, (l - 1) * 3 * U : (l - 1) * 3 * U + 2 * U]
        pair = jnp.where(even, pair[:, U:], pair[:, 0:U])
        rows_send[:, l * U : (l + 1) * U] = dot(value, pair).astype(BF)


def level_one_rest(place, x1_ref, x, first_hots, hots, rows_keep, sep_keep, sep_send, sep_a, sep_b, sems):
    even = place[1] % 2 == 0
    x1 = x1_ref[...]
    above = [x[:, k * PANEL : (k + 1) * PANEL] for k in range(4)]
    level = jnp.where(place[1] < 2, 2, place[3])
    held = jnp.where(level == 0, jnp.zeros_like(x1), above[0])
    for k in (1, 2, 3):
        held = jnp.where(level == k + 2, above[k], held)
    sep_a[...] = jnp.where(even, x1, held)
    sep_b[...] = jnp.where(even, held, x1)
    stores = [
        pltpu.make_async_copy(sep_a, sep_keep, sems.at[0]),
        pltpu.make_async_copy(sep_b, sep_send, sems.at[1]),
    ]
    for store in stores:
        store.start()
    for l, value in enumerate([x1] + above):
        pair = first_hots[...] if l == 0 else hots[:, (l - 1) * 3 * U : (l - 1) * 3 * U + 2 * U]
        pair = jnp.where(even, pair[:, 0:U], pair[:, U:])
        rows_keep[:, l * U : (l + 1) * U] = dot(value, pair).astype(BF)
    for store in stores:
        store.wait()


def leaf_half(rows, inv, cpl, yt, chosen):
    total = yt.astype(F32)
    for l in range(LEVELS):
        total = total - dot(rows[:, l * U : (l + 1) * U], cpl[l])
    back = total.astype(BF)
    parts = []
    for i in range(4):
        start = i * 256
        parts.append(dot(back[:, start:], inv[start:, start : start + 256]).astype(BF))
    xt = jnp.concatenate(parts, axis=1)
    return xt, dot_t(chosen[...], xt).astype(BF)


def leaf_mine(place, keep, inv, cpl, yt, chosen, xt_out, picks_out):
    side = half_of(place)
    xt, picks = leaf_half(keep, inv, cpl, yt[pl.ds(pl.multiple_of(side * 128, 128), 128)], chosen)
    xt_out[...] = xt
    picks_out[...] = picks


def leaf_other(place, recv, inv, cpl, yt, chosen, xt_mine, picks_mine, xt_out, picks_out, xt, picks, sems):
    side = half_of(place)
    mine = pl.ds(pl.multiple_of(side * 128, 128), 128)
    other = pl.ds(pl.multiple_of((1 - side) * 128, 128), 128)
    picks[:, mine] = picks_mine[...]
    xt[mine] = xt_mine[...]
    far, far_picks = leaf_half(recv, inv, cpl, yt[other], chosen)
    picks[:, other] = far_picks
    stores = [pltpu.make_async_copy(picks, picks_out, sems.at[0])]
    stores[0].start()
    xt[other] = far
    stores.append(pltpu.make_async_copy(xt, xt_out, sems.at[1]))
    stores[1].start()
    for store in stores:
        store.wait()


def turn_back(place, keep, recv, xt, x_sep, x_leaf, keep_v, recv_v, xt_v, both, sems):
    loads = [
        pltpu.make_async_copy(keep, keep_v, sems.at[0]),
        pltpu.make_async_copy(recv, recv_v, sems.at[1]),
        pltpu.make_async_copy(xt, xt_v, sems.at[2]),
    ]
    for load in loads:
        load.start()
    loads[2].wait()
    for i in range(4):
        part = slice(i * 256, (i + 1) * 256)
        x_leaf[part] = xt_v[:, part].astype(F32).T.astype(BF)
    for load in loads[:2]:
        load.wait()
    side = half_of(place)
    both[pl.ds(pl.multiple_of(side * 128, 128), 128)] = keep_v[...].astype(F32)
    both[pl.ds(pl.multiple_of((1 - side) * 128, 128), 128)] = recv_v[...].astype(F32)
    x_sep[...] = both[...].T.astype(BF)


def stretch_sum(weight, got, out, weight_v, sems):
    load = pltpu.make_async_copy(weight, weight_v, sems.at[0])
    load.start()
    load.wait()
    out[...] = dot(weight_v[0], got[...]) + dot(weight_v[1], got[...])


def iota(rows, cols, axis):
    return lax.broadcasted_iota(jnp.int32, (rows, cols), axis)


def ones_where(mask):
    return jnp.where(mask, 1.0, 0.0)


def stay_plan(place, dofs, coef, chosen, weight_out, grid, turned, dof_t, coef_t, weight, sems):
    me = place[2] * RING + place[1]
    grid[...] = jnp.full((128, 128), -1, jnp.int32)
    for r in range(16):
        grid[8 * r : 8 * r + 6] = dofs[:, 128 * r : 128 * (r + 1)]
    dof = grid[...]
    match = ones_where((dof >> 10) == me)
    row, col = iota(128, 128, 0), iota(128, 128, 1)
    same = (row >> 3) == (col >> 3)
    earlier = ((row >> 6) == (col >> 6)) & (row < col)
    match_b = match.astype(BF)
    count = dot(ones_where(same).astype(BF), match_b).astype(BF)
    rank = dot(count, ones_where(earlier).astype(BF))
    rank = rank + dot(ones_where(same & (col < row)).astype(BF), match_b)
    high = ((dof >> 5) & 31).astype(F32) + 1.0
    low = (dof & 31).astype(F32)
    rank = jnp.where(match > 0.0, rank, -1.0)
    parts = []
    for value in (high, low):
        for s in range(SLOTS):
            parts.append(jnp.where(rank == float(s), value, 0.0).astype(BF))
    block = ones_where(iota(16, 128, 0) == (iota(16, 128, 1) >> 3)).astype(BF)
    flat = dot(block, jnp.concatenate(parts, axis=1)).astype(BF)
    width = SLOTS * 128
    lane, q = iota(width, 32, 0), iota(width, 32, 1)
    gather = ones_where(q == ((lane >> 6) & 1) * SLOTS + (lane >> 7)).astype(BF)
    table_high = dot(flat[:, 0:width], gather).astype(BF)
    table_low = dot(flat[:, width:], gather).astype(BF)
    spread = ones_where((iota(512, 16, 0) >> 5) == iota(512, 16, 1)).astype(BF)
    here = ones_where((iota(512, 32, 0) & 31) == iota(512, 32, 1))
    sel_high = jnp.sum(dot(spread, table_high) * here, axis=1, keepdims=True)
    sel_low = jnp.sum(dot(spread, table_low) * here, axis=1, keepdims=True)
    sel = (sel_high - 1.0) * 32.0 + sel_low
    for part in range(4):
        at = slice(part * 128, (part + 1) * 128)
        chosen[at] = ones_where(iota(128, LEAF, 1).astype(F32) == sel[at]).astype(BF)

    block_row = pl.multiple_of((me >> 1) * 8, 8)
    block_col = pl.multiple_of((me >> 1) * 128, 128)
    half = pl.ds(pl.multiple_of((me & 1) * 64, 64), 64)
    turned[...] = jnp.zeros_like(turned)
    turned[0:8] = grid[pl.ds(block_row, 8)].astype(F32)
    dof_t[...] = turned[...].T
    turned[0:6] = coef[:, pl.ds(block_col, 128)]
    coef_t[...] = turned[...].T
    my_dof, my_coef = dof_t[half], coef_t[half]
    lanes = iota(64, 32, 1)
    source = [my_dof[:, k : k + 1].astype(jnp.int32) >> 10 for k in range(6)]
    named = [ones_where(source[k] == lanes) for k in range(6)]
    every = named[0]
    for k in range(1, 6):
        every = every + named[k]
    lower = ones_where(iota(64, 64, 1) < iota(64, 64, 0)).astype(BF)
    running = dot(lower, every.astype(BF))
    total = jnp.zeros((64, 512), F32)
    slots = iota(64, 512, 1).astype(F32)
    for k in range(6):
        at = jnp.sum(named[k] * running, axis=1, keepdims=True)
        slot = source[k].astype(F32) * float(SLOTS) + at
        total = total + jnp.where(slots == slot, my_coef[:, k : k + 1], 0.0)
        running = running + named[k]
    first = total.astype(BF)
    weight[0] = first
    weight[1] = (total - first.astype(F32)).astype(BF)
    store = pltpu.make_async_copy(weight, weight_out, sems.at[0])
    store.start()
    store.wait()


def after(value, *others):
    return lax.optimization_barrier((value, *others))[0]


def on_device(
    rhs_leaf, rhs_sep, leaf_inv, leaf_cpl, leaf_idx, sep_inv, sep_cpl, sep_idx, stay_dofs, stay_coef
):
    rows_axis, cols_axis = "rows", "cols"
    columns, rows = lax.axis_size(cols_axis), lax.axis_size(rows_axis)
    me = lax.axis_index(rows_axis)
    core = lax.axis_index(cols_axis) % 2
    y, z = me % RING, me // RING
    top_level = jnp.where(z % 2 == 0, 3, jnp.where(z % 4 == 1, 4, jnp.where(z == 3, 5, 0)))
    place = jnp.stack([core, y, z, top_level]).astype(jnp.int32)

    def route(value, target):
        pairs = []
        for c in range(columns):
            for r in range(rows):
                to = target(c % 2, r % RING, r // RING)
                if to is not None:
                    pairs.append((c * rows + r, (c - c % 2 + to[0]) * rows + to[2] * RING + to[1]))
        return lax.ppermute(value, (cols_axis, rows_axis), pairs)

    def swap_core(value):
        return route(value, lambda c, y, z: (1 - c, y, z))

    def swap(value, flip):
        return route(value, lambda c, y, z: (c, y ^ flip, z))

    def to_odd(value):
        return route(value, lambda c, y, z: (c, y + 1, z) if y % 2 == 0 else None)

    sep_rows_flat = sep_cpl.reshape(4 * U, PANEL)
    (own_up,) = call(
        pack_factor,
        [pinned(packed_rows(3), PANEL)],
        [place, sep_inv, sep_rows_flat, sep_idx],
        [SMEM, HBM, HBM, HBM],
        [pltpu.VMEM((16, PANEL), F32), pltpu.VMEM((LEVELS - 1, U), jnp.int32), dma(7)],
    )
    with jax.named_scope("factors_to_neighbours"):
        near = route(own_up, lambda c, y, z: (c, y ^ (3 if c else 1), z) if y % 2 else None)
    yt, rhs, one, inv_v, cpl_v = call(
        leaf_first,
        [
            pinned(NC, LEAF),
            pinned(NC, PANEL),
            pinned(NC + 4 * 16, U),
            pinned(LEAF, LEAF),
            pinned(LEVELS, U, LEAF),
        ],
        [after(place, own_up), leaf_inv, rhs_leaf, leaf_cpl, rhs_sep, leaf_idx.transpose(1, 0, 2), sep_idx],
        [SMEM] + [HBM] * 6,
        [
            pltpu.VMEM((LEAF, NC), BF),
            pltpu.VMEM((PANEL, NC), BF),
            pltpu.VMEM((LEVELS, 1, U), jnp.int32),
            pltpu.VMEM((LEVELS - 1, U), jnp.int32),
            pltpu.VMEM((64, U), F32),
            dma(9),
        ],
    )
    with jax.named_scope("first_terms"):
        recv = swap(one, 1)
    (terms,) = call(
        leaf_second, [pinned(NC, PANEL)], [yt, cpl_v], [VMEM, VMEM]
    )

    def ready(slots, pick, sources, split=False):
        return call(
            functools.partial(stage, slots, pick, split, len(sources) // (2 if split else 1)),
            [pinned(factor_rows(slots), PANEL), pinned(PANEL, max(slots, 1) * U)],
            [place, *sources],
            [SMEM] + [ANY] * len(sources),
            [pltpu.VMEM((16, PANEL), BF), dma(7)],
        )

    def rise(level, panel, recv, factor, hots):
        slots = LEVELS - level
        return call(
            functools.partial(level_up, level),
            [pinned(64, PANEL), pinned(64, slots * PANEL)],
            [panel, recv, factor, hots],
            [VMEM] * 4,
        )

    (f1,) = call(
        load_first,
        [pinned(2 * PANEL + 128, PANEL)],
        [after(sep_inv, one), sep_rows_flat],
        [HBM, HBM],
        [dma(2)],
    )
    near = after(near, recv, f1, terms)
    with jax.named_scope("factors_across"):
        far = route(near, lambda c, y, z: (c, y ^ (1 if c else 3), z) if y % 2 == 0 else None)
    first = after(recv, f1)
    first_hots, y1, passed, keep, send = call(
        level_one,
        [
            pinned(PANEL, ONE),
            pinned(128, PANEL),
            pinned(2 * PANEL + 128, PANEL),
            pinned(128, 2 * PANEL),
            pinned(128, 2 * PANEL),
        ],
        [place, one, first, terms, rhs, f1],
        [SMEM] + [VMEM] * 5,
        [pltpu.VMEM((NC, 2 * PANEL), BF)],
        aliases={5: 2},
    )
    with jax.named_scope("terms_pair"):
        recv = swap(send, 1)
    near = after(near, send)
    with jax.named_scope("near_to_core"):
        near_o = swap_core(near)
    chosen, weight = call(
        stay_plan,
        [pinned(32 * SLOTS, LEAF), stored(2, 64, 512)],
        [place, stay_dofs, after(stay_coef, send)],
        [SMEM, VMEM, VMEM],
        [
            pltpu.VMEM((128, 128), jnp.int32),
            pltpu.VMEM((128, 128), F32),
            pltpu.VMEM((128, 128), F32),
            pltpu.VMEM((128, 128), F32),
            pltpu.VMEM((2, 64, 512), BF),
            dma(1),
        ],
        [VMEM, HBM],
    )
    (h1,) = call(
        stage_pair, [pinned(PANEL, PAIR_HOTS)], [place, one, after(first, send)], [SMEM, VMEM, VMEM]
    )
    recv = after(recv, chosen, h1)
    panel, send = call(
        join_pair,
        [pinned(64, 4 * PANEL), pinned(64, 4 * PANEL)],
        [place, keep, recv, h1],
        [SMEM] + [VMEM] * 3,
        [pltpu.VMEM((128, 4 * PANEL), BF)],
    )
    with jax.named_scope("panels_ring"):
        recv = swap(send, 3)
    far = after(far, send)
    at = [own_up, near, near_o, far]
    f2, h2 = ready(3, pick_two, at)
    f3, h3, top, top_rest = call(
        stage_and_pass,
        [
            pinned(factor_rows(2), PANEL),
            pinned(PANEL, 2 * U),
            pinned(TRI, PANEL),
            pinned(16 + U, PANEL),
        ],
        [place, *at],
        [SMEM] + [ANY] * 4,
        [pltpu.VMEM((16, PANEL), BF), dma(9)],
    )

    def next_up(value, senders):
        return route(value, lambda c, y, z: (c, y, z + (1 if c else -1)) if z in senders else None)

    with jax.named_scope("factors_up"):
        up = next_up(top, (1, 3, 5))
    with jax.named_scope("factor_top"):
        last = route(
            top,
            lambda c, y, z: (0, y, 0) if (c, z) == (0, 3) else (1, y, 6) if (c, z) == (1, 3) else None,
        )
    with jax.named_scope("factors_up_rest"):
        rest = next_up(top_rest, (1, 5))
    with jax.named_scope("first_factor_to_odd"):
        passed_far = to_odd(after(passed, f2))
    recv = after(recv, f2, h2, f3, h3)
    y2, panel = rise(2, panel, recv, f2, h2)
    with jax.named_scope("panels_z1"):
        recv = route(panel, lambda c, y, z: (c, y, z - 1) if z % 2 else None)
    up, rest, last = after((up, rest, last), recv)
    with jax.named_scope("up_to_core"):
        up_o = swap_core(up)
    with jax.named_scope("rest_to_core"):
        rest_o = swap_core(rest)
    with jax.named_scope("last_to_core"):
        last_o = swap_core(last)
    y3, panel = rise(3, panel, recv, f3, h3)
    with jax.named_scope("panels_z2"):
        recv = route(panel, lambda c, y, z: (c, y, z ^ 2) if z % 2 == 0 else None)
    up, rest, last, up_o, rest_o, last_o = after((up, rest, last, up_o, rest_o, last_o), panel)
    f4, h4 = ready(1, pick_four, [up, rest, up_o, rest_o], True)
    f5, _ = ready(0, pick_five, [up, up_o, last, last_o])
    recv = after(recv, f4, h4, f5)
    y4, panel = rise(4, panel, recv, f4, h4)
    with jax.named_scope("panels_z3"):
        recv = route(panel, lambda c, y, z: (c, y, 6 - z) if z % 2 == 0 else None)
    (x,) = call(
        turn,
        [pinned(64, 3 * PANEL)],
        [panel, recv, f3, f4, f5, h3, h4, y3, y4],
        [VMEM] * 9,
    )
    with jax.named_scope("down_z1"):
        recv = route(x, lambda c, y, z: (c, y, z + 1) if z % 2 == 0 else None)
    (x,) = call(
        level_two_back,
        [pinned(64, 4 * PANEL)],
        [place, x, recv, f2, h2, y2],
        [SMEM] + [VMEM] * 5,
    )
    with jax.named_scope("down_ring"):
        recv = swap(x, 3)
    passed_far = after(passed_far, x)
    (f1,) = call(
        pick_first,
        [pinned(2 * PANEL + 128, PANEL)],
        [place, passed, passed_far],
        [SMEM, ANY, ANY],
        [dma(1)],
    )
    recv = after(recv, f1)
    x1, x, rows_send = call(
        level_one_back,
        [pinned(128, PANEL), pinned(128, 4 * PANEL), pinned(128, TERM)],
        [place, x, recv, y1, f1, first_hots, h1],
        [SMEM] + [VMEM] * 6,
    )
    with jax.named_scope("rows_back"):
        recv = swap(rows_send, 1)
    rows_keep, sep_keep, sep_send = call(
        level_one_rest,
        [pinned(128, TERM), stored(128, PANEL), stored(128, PANEL)],
        [place, x1, x, first_hots, h1],
        [SMEM] + [VMEM] * 4,
        [pltpu.VMEM((128, PANEL), BF), pltpu.VMEM((128, PANEL), BF), dma(2)],
        [VMEM, HBM, HBM],
    )
    xt_mine, picks_mine = call(
        leaf_mine,
        [pinned(128, LEAF), pinned(32 * SLOTS, 128)],
        [place, rows_keep, inv_v, cpl_v, yt, chosen],
        [SMEM] + [VMEM] * 5,
    )
    recv = after(recv, xt_mine)
    with jax.named_scope("sep_back"):
        sep_recv = swap(sep_send, 1)
    xt, picks = call(
        leaf_other,
        [stored(NC, LEAF), stored(32 * SLOTS, NC)],
        [place, recv, inv_v, cpl_v, yt, chosen, xt_mine, picks_mine],
        [SMEM] + [VMEM] * 7,
        [pltpu.VMEM((NC, LEAF), BF), pltpu.VMEM((32 * SLOTS, NC), BF), dma(2)],
        [HBM, HBM],
        moved=14 * 10**6,
    )
    picks, sep_recv = lax.optimization_barrier((picks, sep_recv))
    got = lax.all_to_all(
        picks.reshape(32, SLOTS, NC), rows_axis, 0, 0, tiled=True
    ).reshape(32 * SLOTS, NC)
    x_sep, x_leaf = call(
        turn_back,
        [plain(PANEL, NC), plain(LEAF, NC)],
        [place, sep_keep, sep_recv, xt],
        [SMEM, HBM, HBM, HBM],
        [
            pltpu.VMEM((128, PANEL), BF),
            pltpu.VMEM((128, PANEL), BF),
            pltpu.VMEM((NC, LEAF), BF),
            pltpu.VMEM((NC, PANEL), F32),
            dma(3),
        ],
    )
    (stretch,) = call(
        stretch_sum,
        [plain(64, NC, dtype=F32)],
        [weight, got],
        [HBM, VMEM],
        [pltpu.VMEM((2, 64, 512), BF), dma(1)],
    )
    return (x_leaf, x_sep, stretch)


def solution(mesh):
    return jax.shard_map(
        on_device,
        mesh=mesh,
        in_specs=(
            P("rows", "cols"),
            P("rows", "cols"),
            P("rows", None),
            P("rows", None, None, None),
            P("rows", None, None),
            P("rows", None),
            P("rows", None, None, None),
            P("rows", None, None),
            P(),
            P(),
        ),
        out_specs=(P("rows", "cols"), P("rows", "cols"), P("rows", "cols")),
        check_vma=False,
    )
```

```python
import functools

import jax
import jax.numpy as jnp
from jax import lax
from jax.experimental import pallas as pl
from jax.experimental.pallas import tpu as pltpu
from jax.sharding import PartitionSpec as P

BF = jnp.bfloat16
F32 = jnp.float32
LEAF, PANEL, U, NC, LEVELS = 1024, 512, 128, 256, 5
RING, DEPTH = 4, 8
TERM = LEVELS * U
SLOTS = 16
VMEM_LIMIT = 16 * 1024 * 1024

TRI = 320
IDX = slice(TRI, TRI + 16)
CUT, WINDOW = 352, 368
CPL0 = TRI + 16


def packed_rows(slots):
    return CPL0 + slots * U


def factor_rows(slots):
    return PANEL + slots * U


def triangle_blocks():
    return [
        (slice(384, 512), slice(0, 512), slice(0, 128), slice(0, 512)),
        (slice(256, 384), slice(0, 384), slice(128, 256), slice(0, 384)),
        (slice(0, 128), slice(0, 128), slice(128, 256), slice(384, 512)),
        (slice(128, 192), slice(0, 256), slice(256, 320), slice(0, 256)),
        (slice(192, 256), slice(0, 256), slice(256, 320), slice(256, 512)),
    ]


def dot(left, right):
    return jnp.dot(left, right, preferred_element_type=F32)


def dot_t(left, right):
    return lax.dot_general(left, right, (((1,), (1,)), ((), ())), preferred_element_type=F32)


VMEM = pl.BlockSpec(memory_space=pltpu.VMEM)
SMEM = pl.BlockSpec(memory_space=pltpu.SMEM)
HBM = pl.BlockSpec(memory_space=pltpu.HBM)
ANY = pl.BlockSpec(memory_space=pl.ANY)


def call(body, outs, args, specs, scratch=(), out_specs=None, aliases=None, flops=10**8, moved=10**6):
    args = [
        in_vmem(arg) if spec is VMEM else in_hbm(arg) if spec is HBM else arg
        for arg, spec in zip(args, specs)
    ]
    return pl.pallas_call(
        body,
        out_shape=outs,
        in_specs=specs,
        out_specs=out_specs or [VMEM] * len(outs),
        scratch_shapes=list(scratch),
        input_output_aliases=aliases or {},
        compiler_params=pltpu.CompilerParams(vmem_limit_bytes=VMEM_LIMIT),
        cost_estimate=pl.CostEstimate(flops=flops, bytes_accessed=moved, transcendentals=0),
    )(*args)


def dma(n):
    return pltpu.SemaphoreType.DMA((n,))


def pinned(*dims, dtype=BF):
    return pltpu.VMEM(dims, dtype)


def plain(*dims, dtype=BF):
    return jax.ShapeDtypeStruct(dims, dtype)


def stored(*dims, dtype=BF):
    return pltpu.HBM(dims, dtype)


def in_vmem(value):
    return pltpu.with_memory_space_constraint(value, pltpu.VMEM)


def in_hbm(value):
    return pltpu.with_memory_space_constraint(value, pltpu.HBM)


def hot(rows):
    place = lax.broadcasted_iota(jnp.int32, (PANEL, rows.shape[1]), 0).astype(F32)
    return jnp.where(place == rows, 1.0, 0.0).astype(BF)


def sep_rows(block):
    block = block.astype(F32)
    return [block[s : s + 1, 0:U] * 16.0 + block[s : s + 1, U : 2 * U] for s in range(LEVELS - 1)]


def push_values(factor, y, slots):
    return dot_t(y, factor[PANEL : PANEL + slots * U]).astype(BF)


def solve_back(factor, hots, y, above):
    back = y
    slots = len(above)
    if slots:
        taken = [dot(above[k], hots[k]).astype(BF) for k in range(slots)]
        taken = taken[0] if slots == 1 else jnp.concatenate(taken, axis=1)
        sub = dot(taken, factor[PANEL : PANEL + slots * U])
        back = (y.astype(F32) - sub).astype(BF)
    return dot(back, factor[0:PANEL]).astype(BF)


def pack_factor(place, inv, cpl, sep_idx, up, window, codes, sep_v, sems):
    load = pltpu.make_async_copy(sep_idx.at[0], sep_v, sems.at[0])
    copies = [
        pltpu.make_async_copy(inv.at[r, c], up.at[pr, pc], sems.at[1 + i])
        for i, (r, c, pr, pc) in enumerate(triangle_blocks())
    ]
    copies.append(pltpu.make_async_copy(cpl.at[0 : 3 * U], up.at[CPL0 : packed_rows(3)], sems.at[6]))
    load.start()
    for copy in copies:
        copy.start()
    codes[...] = jnp.zeros_like(codes)
    load.wait()
    value = sep_v[...]
    codes[0 : LEVELS - 1, 0:U] = (value >> 4).astype(F32)
    codes[0 : LEVELS - 1, U : 2 * U] = (value & 15).astype(F32)
    up[IDX] = codes[...].astype(BF)
    for copy in copies:
        copy.wait()
    window[...] = up[pl.ds(pl.multiple_of(place[0] * CUT, 16), WINDOW)]


def load_first(inv, cpl, out, sems):
    copies = [
        pltpu.make_async_copy(inv, out.at[0:PANEL], sems.at[0]),
        pltpu.make_async_copy(cpl, out.at[PANEL : 2 * PANEL], sems.at[1]),
    ]
    for copy in copies:
        copy.start()
    out[2 * PANEL :] = jnp.zeros((128, PANEL), BF)
    for copy in copies:
        copy.wait()


def pick_first(place, own, far, factor, sems):
    even = place[1] % 2 == 0
    copies = [
        pltpu.make_async_copy(source, factor, sems.at[0]) for source in (own, far)
    ]

    @pl.when(even)
    def _():
        copies[0].start()

    @pl.when(jnp.logical_not(even))
    def _():
        copies[1].start()

    copies[0].wait()


def leaf_first(
    place, inv, rhs, cpl, rsep, leaf_idx, sep_idx, yt, rhs_out, one, inv_v, cpl_v,
    rhs_v, rsep_v, leaf_v, sep_v, codes, sems
):
    loads = [
        pltpu.make_async_copy(leaf_idx, leaf_v, sems.at[0]),
        pltpu.make_async_copy(sep_idx.at[0], sep_v, sems.at[1]),
        pltpu.make_async_copy(rhs, rhs_v, sems.at[2]),
    ]
    for i in range(4):
        rows = pl.ds(i * 256, 256)
        loads.append(pltpu.make_async_copy(inv.at[rows], inv_v.at[rows], sems.at[3 + i]))
    loads.append(pltpu.make_async_copy(cpl.at[0], cpl_v, sems.at[7]))
    loads.append(pltpu.make_async_copy(rsep, rsep_v, sems.at[8]))
    for load in loads:
        load.start()
    codes[...] = jnp.zeros_like(codes)
    loads[0].wait()
    for l in range(LEVELS):
        value = leaf_v[l]
        codes[l : l + 1] = (value >> 4).astype(F32)
        codes[16 + l : 17 + l] = (value & 15).astype(F32)
    loads[1].wait()
    value = sep_v[...]
    codes[32 : 32 + LEVELS - 1] = (value >> 4).astype(F32)
    codes[48 : 48 + LEVELS - 1] = (value & 15).astype(F32)
    one[NC:] = codes[...].astype(BF)
    loads[2].wait()
    rhs_t = rhs_v[...].astype(F32).T.astype(BF)
    for i in range(4):
        loads[3 + i].wait()
        span = (i + 1) * 256
        yt[:, i * 256 : span] = dot_t(rhs_t[:, 0:span], inv_v[i * 256 : span, 0:span]).astype(BF)
    loads[7].wait()
    one[0:NC] = dot_t(yt[...], cpl_v[0]).astype(BF)
    loads[8].wait()
    rhs_out[...] = rsep_v[...].astype(F32).T.astype(BF)


def leaf_second(yt, cpl_v, terms):
    for l in range(1, LEVELS):
        terms[:, (l - 1) * U : l * U] = dot_t(yt[...], cpl_v[l]).astype(BF)


def which(place):
    return place[0], place[1], place[2]


def pick_two(core, y, z):
    return y == 1, y == 0, y == 2, y == 3


def pick_top(core, y, z):
    return y == 3, y == 2, y == 0, y == 1


def pick_four(core, y, z):
    after_me = (z == 0) | (z == 4)
    first = core == 0
    return (after_me & first) | (~after_me & ~first), (after_me & ~first) | (~after_me & first)


def pick_five(core, y, z):
    inner = (z == 2) | (z == 4)
    first = core == 0
    low = (z == 2) | (z == 0)
    same = (low & first) | (~low & ~first)
    return inner & same, inner & ~same, ~inner & same, ~inner & ~same


def pick_one(core, y, z):
    even = (y == 0) | (y == 2)
    return even, ~even


def window_sources(core, refs):
    own = refs[0]
    sources = [[(None, own, own, 0)]]
    for i in range(1, len(refs), 2):
        mine, other = refs[i], refs[i + 1]
        sources.append([(core == 0, mine, other, CUT), (core != 0, other, mine, CUT)])
    return sources


def start_one(cases, sources, copies_of):
    for case, versions in zip(cases, sources):
        for on_core, low, high, at in versions:

            @pl.when(case if on_core is None else case & on_core)
            def _(low=low, high=high, at=at):
                for copy in copies_of(low, high, at):
                    copy.start()

    return copies_of(*sources[0][0][1:])


def factor_copies(slots, factor, idx, sems):
    def copies_of(low, high, at):
        copies = [
            pltpu.make_async_copy(low.at[pr, pc], factor.at[r, c], sems.at[i])
            for i, (r, c, pr, pc) in enumerate(triangle_blocks())
        ]
        if slots:
            split = CUT - CPL0
            copies.append(
                pltpu.make_async_copy(low.at[CPL0:CUT], factor.at[PANEL : PANEL + split], sems.at[5])
            )
            copies.append(
                pltpu.make_async_copy(
                    high.at[CUT - at : packed_rows(slots) - at], factor.at[PANEL + split :], sems.at[6]
                )
            )
            copies.append(pltpu.make_async_copy(low.at[IDX], idx, sems.at[7]))
        return copies

    return copies_of


def finish_factor(slots, factor, hots, idx, copies):
    for rows, cols in (
        (slice(0, 128), slice(128, 512)),
        (slice(128, 256), slice(256, 512)),
        (slice(256, 384), slice(384, 512)),
    ):
        factor[rows, cols] = jnp.zeros((rows.stop - rows.start, cols.stop - cols.start), BF)
    if slots:
        copies[-1].wait()
        taken = sep_rows(idx[...])
        for k in range(slots):
            hots[:, k * U : (k + 1) * U] = hot(taken[k])
        copies = copies[:-1]
    else:
        hots[...] = jnp.zeros_like(hots)
    for copy in copies:
        copy.wait()


def stage(slots, pick, count, place, *refs):
    factor, hots, idx, sems = refs[count:]
    sources = [[(None, ref, ref, 0)] for ref in refs[:count]]
    copies = start_one(pick(*which(place)), sources, factor_copies(slots, factor, idx, sems))
    finish_factor(slots, factor, hots, idx, copies)


def stage_two(place, *refs):
    factor, hots, idx, sems = refs[7:]
    sources = window_sources(place[0], refs[:7])
    copies = start_one(pick_two(*which(place)), sources, factor_copies(3, factor, idx, sems))
    finish_factor(3, factor, hots, idx, copies)


def stage_and_pass(place, *refs):
    factor, hots, top, triangle, idx, sems = refs[7:]
    sources = window_sources(place[0], refs[:7])
    cases = pick_top(*which(place))

    def pass_copies(low, high, at):
        return [
            pltpu.make_async_copy(low.at[0:CUT], top.at[0:CUT], sems.at[8]),
            pltpu.make_async_copy(high.at[CUT - at : packed_rows(1) - at], top.at[CUT:], sems.at[9]),
            pltpu.make_async_copy(low.at[0:TRI], triangle, sems.at[10]),
        ]

    passed = start_one(cases, sources, pass_copies)
    copies = start_one(cases, sources, factor_copies(2, factor, idx, sems))
    finish_factor(2, factor, hots, idx, copies)
    for copy in passed:
        copy.wait()


ONE = 2 * U
PAIR_HOTS = 4 * 3 * U


def pair_rows(place, one, other):
    even = place[1] % 2 == 0
    mine, far = one[NC:], other[NC:]

    def rows(block, at, count):
        block = block.astype(F32)
        return [
            block[at + i : at + i + 1] * 16.0 + block[at + 16 + i : at + 17 + i] for i in range(count)
        ]

    left, right = jnp.where(even, mine, far), jnp.where(even, far, mine)
    return rows(left, 0, LEVELS), rows(right, 0, LEVELS), rows(left, 32, LEVELS - 1)


def stage_pair(place, one, other, hots):
    a, b, up = pair_rows(place, one, other)
    for k in range(4):
        at = k * 3 * U
        hots[:, at : at + 3 * U] = hot(jnp.concatenate([a[k + 1], b[k + 1], up[k]], axis=1))


def half_of(place):
    y = place[1]
    return jnp.where((y == 1) | (y == 2), 1, 0)


def level_one(place, one, recv, terms, rhs, factor, hots, y_keep, passed, keep, send, y_all):
    even = place[1] % 2 == 0
    a, b, _ = pair_rows(place, one, recv)
    hots[...] = hot(jnp.concatenate([a[0], b[0]], axis=1))
    total = dot_t(jnp.concatenate([one[0:NC], recv[0:NC]], axis=1), hots[...])
    resid = (rhs[...].astype(F32) - total).astype(BF)
    y = dot_t(resid, factor[0:PANEL]).astype(BF)
    y_all[:, 0:PANEL] = y
    y_all[:, PANEL:] = jnp.where(even, push_values(factor, y, 4), rhs[...])
    side = half_of(place)
    mine = pl.ds(pl.multiple_of(side * 128, 128), 128)
    theirs = pl.ds(pl.multiple_of((1 - side) * 128, 128), 128)
    send[:, 0:PANEL] = terms[theirs]
    send[:, PANEL:] = y_all[theirs, PANEL:]
    keep[:, 0:PANEL] = terms[mine]
    keep[:, PANEL:] = y_all[mine, PANEL:]
    y_keep[...] = y_all[mine, 0:PANEL]
    passed[2 * PANEL :] = y_all[theirs, 0:PANEL]


def join_pair(place, keep, recv, hots, panel_keep, panel_send, panels):
    ring, even = place[1], place[1] % 2 == 0
    a, b = keep[...], recv[...]
    left, right = jnp.where(even, a, b), jnp.where(even, b, a)
    held = right[:, PANEL:].astype(F32)
    level = jnp.where(ring < 2, 2, place[3])
    for k in range(4):
        at = slice(k * U, (k + 1) * U)
        start = k * 3 * U
        parts = [left[:, at], right[:, at], left[:, PANEL + k * U : PANEL + (k + 1) * U]]
        total = dot_t(jnp.concatenate(parts, axis=1), hots[:, start : start + 3 * U])
        total = total - jnp.where(level == k + 2, held, 0.0)
        panels[:, k * PANEL : (k + 1) * PANEL] = total.astype(BF)
    side = ring // 2
    panel_keep[...] = panels[pl.ds(pl.multiple_of(side * 64, 64), 64)]
    panel_send[...] = panels[pl.ds(pl.multiple_of((1 - side) * 64, 64), 64)]


def level_up(level, mine, recv, factor, hots, y_out, panels):
    slots = LEVELS - level
    total = mine[...].astype(F32) + recv[...].astype(F32)
    y = dot_t((-total[:, 0:PANEL]).astype(BF), factor[0:PANEL]).astype(BF)
    y_out[...] = y
    values = push_values(factor, y, slots)
    for k in range(slots):
        at = slice((k + 1) * PANEL, (k + 2) * PANEL)
        term = dot_t(values[:, k * U : (k + 1) * U], hots[:, k * U : (k + 1) * U])
        panels[:, k * PANEL : (k + 1) * PANEL] = (total[:, at] + term).astype(BF)


def turn(mine, recv, f3, f4, f5, h3, h4, y3, y4, x_out):
    total = mine[...].astype(F32) + recv[...].astype(F32)
    y5 = dot_t((-total).astype(BF), f5[0:PANEL]).astype(BF)
    x5 = solve_back(f5, [], y5, [])
    x4 = solve_back(f4, [h4[...]], y4[...], [x5])
    x3 = solve_back(f3, [h3[:, 0:U], h3[:, U : 2 * U]], y3[...], [x4, x5])
    for k, x in enumerate((x3, x4, x5)):
        x_out[:, k * PANEL : (k + 1) * PANEL] = x


def level_two_back(place, mine, recv, f2, h2, y2, x_out):
    x = jnp.where(place[2] % 2 == 0, mine[...], recv[...])
    above = [x[:, k * PANEL : (k + 1) * PANEL] for k in range(3)]
    x_out[:, 0:PANEL] = solve_back(f2, [h2[:, k * U : (k + 1) * U] for k in range(3)], y2[...], above)
    x_out[:, PANEL:] = x


def level_one_back(place, mine, recv, y_mine, factor, first_hots, hots, x1_out, x, rows_send):
    side = place[1] // 2
    even = place[1] % 2 == 0
    x[pl.ds(pl.multiple_of(side * 64, 64), 64)] = mine[...]
    x[pl.ds(pl.multiple_of((1 - side) * 64, 64), 64)] = recv[...]
    above = [x[:, k * PANEL : (k + 1) * PANEL] for k in range(4)]
    ups = [hots[:, k * 3 * U + 2 * U : (k + 1) * 3 * U] for k in range(4)]
    x1 = solve_back(factor, ups, jnp.where(even, y_mine[...], factor[2 * PANEL :]), above)
    x1_out[...] = x1
    for l, value in enumerate([x1] + above):
        pair = first_hots[...] if l == 0 else hots[:, (l - 1) * 3 * U : (l - 1) * 3 * U + 2 * U]
        pair = jnp.where(even, pair[:, U:], pair[:, 0:U])
        rows_send[:, l * U : (l + 1) * U] = dot(value, pair).astype(BF)


def level_one_rest(place, x1_ref, x, first_hots, hots, rows_keep, sep_keep, sep_send, sep_a, sep_b, sems):
    even = place[1] % 2 == 0
    x1 = x1_ref[...]
    above = [x[:, k * PANEL : (k + 1) * PANEL] for k in range(4)]
    level = jnp.where(place[1] < 2, 2, place[3])
    held = jnp.where(level == 0, jnp.zeros_like(x1), above[0])
    for k in (1, 2, 3):
        held = jnp.where(level == k + 2, above[k], held)
    sep_a[...] = jnp.where(even, x1, held)
    sep_b[...] = jnp.where(even, held, x1)
    stores = [
        pltpu.make_async_copy(sep_a, sep_keep, sems.at[0]),
        pltpu.make_async_copy(sep_b, sep_send, sems.at[1]),
    ]
    for store in stores:
        store.start()
    for l, value in enumerate([x1] + above):
        pair = first_hots[...] if l == 0 else hots[:, (l - 1) * 3 * U : (l - 1) * 3 * U + 2 * U]
        pair = jnp.where(even, pair[:, 0:U], pair[:, U:])
        rows_keep[:, l * U : (l + 1) * U] = dot(value, pair).astype(BF)
    for store in stores:
        store.wait()


def leaf_half(rows, inv, cpl, yt, chosen):
    total = yt.astype(F32)
    for l in range(LEVELS):
        total = total - dot(rows[:, l * U : (l + 1) * U], cpl[l])
    back = total.astype(BF)
    parts = []
    for i in range(4):
        start = i * 256
        parts.append(dot(back[:, start:], inv[start:, start : start + 256]).astype(BF))
    xt = jnp.concatenate(parts, axis=1)
    return xt, dot_t(chosen[...], xt).astype(BF)


def leaf_mine(place, keep, inv, cpl, yt, chosen, xt_out, picks_out):
    side = half_of(place)
    xt, picks = leaf_half(keep, inv, cpl, yt[pl.ds(pl.multiple_of(side * 128, 128), 128)], chosen)
    xt_out[...] = xt
    picks_out[...] = picks


def leaf_other(place, recv, inv, cpl, yt, chosen, xt_mine, picks_mine, xt_out, picks_out, xt, picks, sems):
    side = half_of(place)
    mine = pl.ds(pl.multiple_of(side * 128, 128), 128)
    other = pl.ds(pl.multiple_of((1 - side) * 128, 128), 128)
    picks[:, mine] = picks_mine[...]
    xt[mine] = xt_mine[...]
    far, far_picks = leaf_half(recv, inv, cpl, yt[other], chosen)
    picks[:, other] = far_picks
    stores = [pltpu.make_async_copy(picks, picks_out, sems.at[0])]
    stores[0].start()
    xt[other] = far
    stores.append(pltpu.make_async_copy(xt, xt_out, sems.at[1]))
    stores[1].start()
    for store in stores:
        store.wait()


def turn_back(place, keep, recv, xt, x_sep, x_leaf, keep_v, recv_v, xt_v, both, sems):
    loads = [
        pltpu.make_async_copy(keep, keep_v, sems.at[0]),
        pltpu.make_async_copy(recv, recv_v, sems.at[1]),
        pltpu.make_async_copy(xt, xt_v, sems.at[2]),
    ]
    for load in loads:
        load.start()
    loads[2].wait()
    for i in range(4):
        part = slice(i * 256, (i + 1) * 256)
        x_leaf[part] = xt_v[:, part].astype(F32).T.astype(BF)
    for load in loads[:2]:
        load.wait()
    side = half_of(place)
    both[pl.ds(pl.multiple_of(side * 128, 128), 128)] = keep_v[...].astype(F32)
    both[pl.ds(pl.multiple_of((1 - side) * 128, 128), 128)] = recv_v[...].astype(F32)
    x_sep[...] = both[...].T.astype(BF)


def stretch_sum(weight, got, out, weight_v, sems):
    load = pltpu.make_async_copy(weight, weight_v, sems.at[0])
    load.start()
    load.wait()
    out[...] = dot(weight_v[0], got[...]) + dot(weight_v[1], got[...])


def iota(rows, cols, axis):
    return lax.broadcasted_iota(jnp.int32, (rows, cols), axis)


def ones_where(mask):
    return jnp.where(mask, 1.0, 0.0)


def stay_plan(place, dofs, coef, chosen, weight_out, grid, turned, dof_t, coef_t, weight, sems):
    me = place[2] * RING + place[1]
    grid[...] = jnp.full((128, 128), -1, jnp.int32)
    for r in range(16):
        grid[8 * r : 8 * r + 6] = dofs[:, 128 * r : 128 * (r + 1)]
    dof = grid[...]
    match = ones_where((dof >> 10) == me)
    row, col = iota(128, 128, 0), iota(128, 128, 1)
    same = (row >> 3) == (col >> 3)
    earlier = ((row >> 6) == (col >> 6)) & (row < col)
    match_b = match.astype(BF)
    count = dot(ones_where(same).astype(BF), match_b).astype(BF)
    rank = dot(count, ones_where(earlier).astype(BF))
    rank = rank + dot(ones_where(same & (col < row)).astype(BF), match_b)
    high = ((dof >> 5) & 31).astype(F32) + 1.0
    low = (dof & 31).astype(F32)
    rank = jnp.where(match > 0.0, rank, -1.0)
    parts = []
    for value in (high, low):
        for s in range(SLOTS):
            parts.append(jnp.where(rank == float(s), value, 0.0).astype(BF))
    block = ones_where(iota(16, 128, 0) == (iota(16, 128, 1) >> 3)).astype(BF)
    flat = dot(block, jnp.concatenate(parts, axis=1)).astype(BF)
    width = SLOTS * 128
    lane, q = iota(width, 32, 0), iota(width, 32, 1)
    gather = ones_where(q == ((lane >> 6) & 1) * SLOTS + (lane >> 7)).astype(BF)
    table_high = dot(flat[:, 0:width], gather).astype(BF)
    table_low = dot(flat[:, width:], gather).astype(BF)
    spread = ones_where((iota(512, 16, 0) >> 5) == iota(512, 16, 1)).astype(BF)
    here = ones_where((iota(512, 32, 0) & 31) == iota(512, 32, 1))
    sel_high = jnp.sum(dot(spread, table_high) * here, axis=1, keepdims=True)
    sel_low = jnp.sum(dot(spread, table_low) * here, axis=1, keepdims=True)
    sel = (sel_high - 1.0) * 32.0 + sel_low
    for part in range(4):
        at = slice(part * 128, (part + 1) * 128)
        chosen[at] = ones_where(iota(128, LEAF, 1).astype(F32) == sel[at]).astype(BF)

    block_row = pl.multiple_of((me >> 1) * 8, 8)
    block_col = pl.multiple_of((me >> 1) * 128, 128)
    half = pl.ds(pl.multiple_of((me & 1) * 64, 64), 64)
    turned[...] = jnp.zeros_like(turned)
    turned[0:8] = grid[pl.ds(block_row, 8)].astype(F32)
    dof_t[...] = turned[...].T
    turned[0:6] = coef[:, pl.ds(block_col, 128)]
    coef_t[...] = turned[...].T
    my_dof, my_coef = dof_t[half], coef_t[half]
    lanes = iota(64, 32, 1)
    source = [my_dof[:, k : k + 1].astype(jnp.int32) >> 10 for k in range(6)]
    named = [ones_where(source[k] == lanes) for k in range(6)]
    every = named[0]
    for k in range(1, 6):
        every = every + named[k]
    lower = ones_where(iota(64, 64, 1) < iota(64, 64, 0)).astype(BF)
    running = dot(lower, every.astype(BF))
    total = jnp.zeros((64, 512), F32)
    slots = iota(64, 512, 1).astype(F32)
    for k in range(6):
        at = jnp.sum(named[k] * running, axis=1, keepdims=True)
        slot = source[k].astype(F32) * float(SLOTS) + at
        total = total + jnp.where(slots == slot, my_coef[:, k : k + 1], 0.0)
        running = running + named[k]
    first = total.astype(BF)
    weight[0] = first
    weight[1] = (total - first.astype(F32)).astype(BF)
    store = pltpu.make_async_copy(weight, weight_out, sems.at[0])
    store.start()
    store.wait()


def after(value, *others):
    return lax.optimization_barrier((value, *others))[0]


def on_device(
    rhs_leaf, rhs_sep, leaf_inv, leaf_cpl, leaf_idx, sep_inv, sep_cpl, sep_idx, stay_dofs, stay_coef
):
    rows_axis, cols_axis = "rows", "cols"
    columns, rows = lax.axis_size(cols_axis), lax.axis_size(rows_axis)
    me = lax.axis_index(rows_axis)
    core = lax.axis_index(cols_axis) % 2
    y, z = me % RING, me // RING
    top_level = jnp.where(z % 2 == 0, 3, jnp.where(z % 4 == 1, 4, jnp.where(z == 3, 5, 0)))
    place = jnp.stack([core, y, z, top_level]).astype(jnp.int32)

    def route(value, target):
        pairs = []
        for c in range(columns):
            for r in range(rows):
                to = target(c % 2, r % RING, r // RING)
                if to is not None:
                    pairs.append((c * rows + r, (c - c % 2 + to[0]) * rows + to[2] * RING + to[1]))
        return lax.ppermute(value, (cols_axis, rows_axis), pairs)

    def swap_core(value):
        return route(value, lambda c, y, z: (1 - c, y, z))

    def swap(value, flip):
        return route(value, lambda c, y, z: (c, y ^ flip, z))

    def to_odd(value):
        return route(value, lambda c, y, z: (c, y + 1, z) if y % 2 == 0 else None)

    sep_rows_flat = sep_cpl.reshape(4 * U, PANEL)
    own_up, window = call(
        pack_factor,
        [pinned(packed_rows(3), PANEL), pinned(WINDOW, PANEL)],
        [place, sep_inv, sep_rows_flat, sep_idx],
        [SMEM, HBM, HBM, HBM],
        [pltpu.VMEM((16, PANEL), F32), pltpu.VMEM((LEVELS - 1, U), jnp.int32), dma(7)],
    )
    with jax.named_scope("factors_to_pair"):
        pair = route(window, lambda c, y, z: (c, y ^ 1, z) if y % 2 else None)
    with jax.named_scope("factors_to_other"):
        beside = route(window, lambda c, y, z: (c, y ^ 3, z) if y % 2 else None)
    yt, rhs, one, inv_v, cpl_v = call(
        leaf_first,
        [
            pinned(NC, LEAF),
            pinned(NC, PANEL),
            pinned(NC + 4 * 16, U),
            pinned(LEAF, LEAF),
            pinned(LEVELS, U, LEAF),
        ],
        [after(place, own_up), leaf_inv, rhs_leaf, leaf_cpl, rhs_sep, leaf_idx.transpose(1, 0, 2), sep_idx],
        [SMEM] + [HBM] * 6,
        [
            pltpu.VMEM((LEAF, NC), BF),
            pltpu.VMEM((PANEL, NC), BF),
            pltpu.VMEM((LEVELS, 1, U), jnp.int32),
            pltpu.VMEM((LEVELS - 1, U), jnp.int32),
            pltpu.VMEM((64, U), F32),
            dma(9),
        ],
    )
    with jax.named_scope("first_terms"):
        recv = swap(one, 1)
    (terms,) = call(
        leaf_second, [pinned(NC, PANEL)], [yt, cpl_v], [VMEM, VMEM]
    )

    def ready(slots, pick, sources):
        return call(
            functools.partial(stage, slots, pick, len(sources)),
            [pinned(factor_rows(slots), PANEL), pinned(PANEL, max(slots, 1) * U)],
            [place, *sources],
            [SMEM] + [ANY] * len(sources),
            [pltpu.VMEM((16, PANEL), BF), dma(8)],
        )

    def rise(level, panel, recv, factor, hots):
        slots = LEVELS - level
        return call(
            functools.partial(level_up, level),
            [pinned(64, PANEL), pinned(64, slots * PANEL)],
            [panel, recv, factor, hots],
            [VMEM] * 4,
        )

    (f1,) = call(
        load_first,
        [pinned(2 * PANEL + 128, PANEL)],
        [after(sep_inv, one), sep_rows_flat],
        [HBM, HBM],
        [dma(2)],
    )
    pair = after(pair, recv, f1, terms)
    with jax.named_scope("factors_across"):
        far = route(pair, lambda c, y, z: (c, y ^ 3, z) if y % 2 == 0 else None)
    first = after(recv, f1)
    first_hots, y1, passed, keep, send = call(
        level_one,
        [
            pinned(PANEL, ONE),
            pinned(128, PANEL),
            pinned(2 * PANEL + 128, PANEL),
            pinned(128, 2 * PANEL),
            pinned(128, 2 * PANEL),
        ],
        [place, one, first, terms, rhs, f1],
        [SMEM] + [VMEM] * 5,
        [pltpu.VMEM((NC, 2 * PANEL), BF)],
        aliases={5: 2},
    )
    with jax.named_scope("terms_pair"):
        recv = swap(send, 1)
    pair, beside = after((pair, beside), send)
    with jax.named_scope("pair_to_core"):
        pair_o = swap_core(pair)
    with jax.named_scope("beside_to_core"):
        beside_o = swap_core(beside)
    chosen, weight = call(
        stay_plan,
        [pinned(32 * SLOTS, LEAF), stored(2, 64, 512)],
        [place, stay_dofs, after(stay_coef, send)],
        [SMEM, VMEM, VMEM],
        [
            pltpu.VMEM((128, 128), jnp.int32),
            pltpu.VMEM((128, 128), F32),
            pltpu.VMEM((128, 128), F32),
            pltpu.VMEM((128, 128), F32),
            pltpu.VMEM((2, 64, 512), BF),
            dma(1),
        ],
        [VMEM, HBM],
    )
    (h1,) = call(
        stage_pair, [pinned(PANEL, PAIR_HOTS)], [place, one, after(first, send)], [SMEM, VMEM, VMEM]
    )
    recv = after(recv, chosen, h1)
    panel, send = call(
        join_pair,
        [pinned(64, 4 * PANEL), pinned(64, 4 * PANEL)],
        [place, keep, recv, h1],
        [SMEM] + [VMEM] * 3,
        [pltpu.VMEM((128, 4 * PANEL), BF)],
    )
    with jax.named_scope("panels_ring"):
        recv = swap(send, 3)
    far = after(far, send)
    with jax.named_scope("far_to_core"):
        far_o = swap_core(far)
    at = [own_up, pair, pair_o, beside, beside_o, far, far_o]
    f2, h2 = call(
        stage_two,
        [pinned(factor_rows(3), PANEL), pinned(PANEL, 3 * U)],
        [place, *at],
        [SMEM] + [ANY] * 7,
        [pltpu.VMEM((16, PANEL), BF), dma(8)],
    )
    f3, h3, top, triangle = call(
        stage_and_pass,
        [
            pinned(factor_rows(2), PANEL),
            pinned(PANEL, 2 * U),
            pinned(packed_rows(1), PANEL),
            pinned(TRI, PANEL),
        ],
        [place, *at],
        [SMEM] + [ANY] * 7,
        [pltpu.VMEM((16, PANEL), BF), dma(11)],
    )

    def next_up(value, senders):
        return route(value, lambda c, y, z: (c, y, z + (1 if c else -1)) if z in senders else None)

    with jax.named_scope("factors_up"):
        up = next_up(top, (1, 3, 5))
    with jax.named_scope("factor_top"):
        last = route(
            triangle,
            lambda c, y, z: (0, y, 0) if (c, z) == (0, 3) else (1, y, 6) if (c, z) == (1, 3) else None,
        )
    with jax.named_scope("first_factor_to_odd"):
        passed_far = to_odd(after(passed, f2))
    recv = after(recv, f2, h2, f3, h3)
    y2, panel = rise(2, panel, recv, f2, h2)
    with jax.named_scope("panels_z1"):
        recv = route(panel, lambda c, y, z: (c, y, z - 1) if z % 2 else None)
    y3, panel = rise(3, panel, recv, f3, h3)
    with jax.named_scope("panels_z2"):
        recv = route(panel, lambda c, y, z: (c, y, z ^ 2) if z % 2 == 0 else None)
    up, last = after((up, last), panel)
    with jax.named_scope("up_to_core"):
        up_o = swap_core(up)
    with jax.named_scope("last_to_core"):
        last_o = swap_core(last)
    f4, h4 = ready(1, pick_four, [up, up_o])
    f5, _ = ready(0, pick_five, [up, up_o, last, last_o])
    recv = after(recv, f4, h4, f5)
    y4, panel = rise(4, panel, recv, f4, h4)
    with jax.named_scope("panels_z3"):
        recv = route(panel, lambda c, y, z: (c, y, 6 - z) if z % 2 == 0 else None)
    (x,) = call(
        turn,
        [pinned(64, 3 * PANEL)],
        [panel, recv, f3, f4, f5, h3, h4, y3, y4],
        [VMEM] * 9,
    )
    with jax.named_scope("down_z1"):
        recv = route(x, lambda c, y, z: (c, y, z + 1) if z % 2 == 0 else None)
    (x,) = call(
        level_two_back,
        [pinned(64, 4 * PANEL)],
        [place, x, recv, f2, h2, y2],
        [SMEM] + [VMEM] * 5,
    )
    with jax.named_scope("down_ring"):
        recv = swap(x, 3)
    passed_far = after(passed_far, x)
    (f1,) = call(
        pick_first,
        [pinned(2 * PANEL + 128, PANEL)],
        [place, passed, passed_far],
        [SMEM, ANY, ANY],
        [dma(1)],
    )
    recv = after(recv, f1)
    x1, x, rows_send = call(
        level_one_back,
        [pinned(128, PANEL), pinned(128, 4 * PANEL), pinned(128, TERM)],
        [place, x, recv, y1, f1, first_hots, h1],
        [SMEM] + [VMEM] * 6,
    )
    with jax.named_scope("rows_back"):
        recv = swap(rows_send, 1)
    rows_keep, sep_keep, sep_send = call(
        level_one_rest,
        [pinned(128, TERM), stored(128, PANEL), stored(128, PANEL)],
        [place, x1, x, first_hots, h1],
        [SMEM] + [VMEM] * 4,
        [pltpu.VMEM((128, PANEL), BF), pltpu.VMEM((128, PANEL), BF), dma(2)],
        [VMEM, HBM, HBM],
    )
    xt_mine, picks_mine = call(
        leaf_mine,
        [pinned(128, LEAF), pinned(32 * SLOTS, 128)],
        [place, rows_keep, inv_v, cpl_v, yt, chosen],
        [SMEM] + [VMEM] * 5,
    )
    recv = after(recv, xt_mine)
    with jax.named_scope("sep_back"):
        sep_recv = swap(sep_send, 1)
    xt, picks = call(
        leaf_other,
        [stored(NC, LEAF), stored(32 * SLOTS, NC)],
        [place, recv, inv_v, cpl_v, yt, chosen, xt_mine, picks_mine],
        [SMEM] + [VMEM] * 7,
        [pltpu.VMEM((NC, LEAF), BF), pltpu.VMEM((32 * SLOTS, NC), BF), dma(2)],
        [HBM, HBM],
        moved=14 * 10**6,
    )
    picks, sep_recv = lax.optimization_barrier((picks, sep_recv))
    got = lax.all_to_all(
        picks.reshape(32, SLOTS, NC), rows_axis, 0, 0, tiled=True
    ).reshape(32 * SLOTS, NC)
    x_sep, x_leaf = call(
        turn_back,
        [plain(PANEL, NC), plain(LEAF, NC)],
        [place, sep_keep, sep_recv, xt],
        [SMEM, HBM, HBM, HBM],
        [
            pltpu.VMEM((128, PANEL), BF),
            pltpu.VMEM((128, PANEL), BF),
            pltpu.VMEM((NC, LEAF), BF),
            pltpu.VMEM((NC, PANEL), F32),
            dma(3),
        ],
    )
    (stretch,) = call(
        stretch_sum,
        [plain(64, NC, dtype=F32)],
        [weight, got],
        [HBM, VMEM],
        [pltpu.VMEM((2, 64, 512), BF), dma(1)],
    )
    return (x_leaf, x_sep, stretch)


def solution(mesh):
    return jax.shard_map(
        on_device,
        mesh=mesh,
        in_specs=(
            P("rows", "cols"),
            P("rows", "cols"),
            P("rows", None),
            P("rows", None, None, None),
            P("rows", None, None),
            P("rows", None),
            P("rows", None, None, None),
            P("rows", None, None),
            P(),
            P(),
        ),
        out_specs=(P("rows", "cols"), P("rows", "cols"), P("rows", "cols")),
        check_vma=False,
    )
```

```python
import functools

import jax
import jax.numpy as jnp
from jax import lax
from jax.experimental import pallas as pl
from jax.experimental.pallas import tpu as pltpu
from jax.sharding import PartitionSpec as P

BF = jnp.bfloat16
F32 = jnp.float32
LEAF, PANEL, U, NC, LEVELS = 1024, 512, 128, 256, 5
RING, DEPTH = 4, 8
TERM = LEVELS * U
SLOTS = 16
VMEM_LIMIT = 16 * 1024 * 1024

TRI = 320
IDX = slice(TRI, TRI + 16)
CUT, WINDOW = 352, 368
CPL0 = TRI + 16


def packed_rows(slots):
    return CPL0 + slots * U


def factor_rows(slots):
    return PANEL + slots * U


def triangle_blocks():
    return [
        (slice(384, 512), slice(0, 512), slice(0, 128), slice(0, 512)),
        (slice(256, 384), slice(0, 384), slice(128, 256), slice(0, 384)),
        (slice(0, 128), slice(0, 128), slice(128, 256), slice(384, 512)),
        (slice(128, 192), slice(0, 256), slice(256, 320), slice(0, 256)),
        (slice(192, 256), slice(0, 256), slice(256, 320), slice(256, 512)),
    ]


def dot(left, right):
    return jnp.dot(left, right, preferred_element_type=F32)


def dot_t(left, right):
    return lax.dot_general(left, right, (((1,), (1,)), ((), ())), preferred_element_type=F32)


VMEM = pl.BlockSpec(memory_space=pltpu.VMEM)
SMEM = pl.BlockSpec(memory_space=pltpu.SMEM)
HBM = pl.BlockSpec(memory_space=pltpu.HBM)
ANY = pl.BlockSpec(memory_space=pl.ANY)


def call(body, outs, args, specs, scratch=(), out_specs=None, aliases=None, flops=10**8, moved=10**6):
    args = [
        in_vmem(arg) if spec is VMEM else in_hbm(arg) if spec is HBM else arg
        for arg, spec in zip(args, specs)
    ]
    return pl.pallas_call(
        body,
        out_shape=outs,
        in_specs=specs,
        out_specs=out_specs or [VMEM] * len(outs),
        scratch_shapes=list(scratch),
        input_output_aliases=aliases or {},
        compiler_params=pltpu.CompilerParams(vmem_limit_bytes=VMEM_LIMIT),
        cost_estimate=pl.CostEstimate(flops=flops, bytes_accessed=moved, transcendentals=0),
    )(*args)


def dma(n):
    return pltpu.SemaphoreType.DMA((n,))


def pinned(*dims, dtype=BF):
    return pltpu.VMEM(dims, dtype)


def plain(*dims, dtype=BF):
    return jax.ShapeDtypeStruct(dims, dtype)


def stored(*dims, dtype=BF):
    return pltpu.HBM(dims, dtype)


def in_vmem(value):
    return pltpu.with_memory_space_constraint(value, pltpu.VMEM)


def in_hbm(value):
    return pltpu.with_memory_space_constraint(value, pltpu.HBM)


def hot(rows):
    place = lax.broadcasted_iota(jnp.int32, (PANEL, rows.shape[1]), 0).astype(F32)
    return jnp.where(place == rows, 1.0, 0.0).astype(BF)


def sep_rows(block):
    block = block.astype(F32)
    return [block[s : s + 1, 0:U] * 16.0 + block[s : s + 1, U : 2 * U] for s in range(LEVELS - 1)]


def push_values(factor, y, slots):
    return dot_t(y, factor[PANEL : PANEL + slots * U]).astype(BF)


def solve_back(factor, hots, y, above):
    back = y
    slots = len(above)
    if slots:
        taken = [dot(above[k], hots[k]).astype(BF) for k in range(slots)]
        taken = taken[0] if slots == 1 else jnp.concatenate(taken, axis=1)
        sub = dot(taken, factor[PANEL : PANEL + slots * U])
        back = (y.astype(F32) - sub).astype(BF)
    return dot(back, factor[0:PANEL]).astype(BF)


def pack_factor(place, inv, cpl, sep_idx, up, window, codes, sep_v, sems):
    load = pltpu.make_async_copy(sep_idx.at[0], sep_v, sems.at[0])
    copies = [
        pltpu.make_async_copy(inv.at[r, c], up.at[pr, pc], sems.at[1 + i])
        for i, (r, c, pr, pc) in enumerate(triangle_blocks())
    ]
    copies.append(pltpu.make_async_copy(cpl.at[0 : 3 * U], up.at[CPL0 : packed_rows(3)], sems.at[6]))
    load.start()
    for copy in copies:
        copy.start()
    codes[...] = jnp.zeros_like(codes)
    load.wait()
    value = sep_v[...]
    codes[0 : LEVELS - 1, 0:U] = (value >> 4).astype(F32)
    codes[0 : LEVELS - 1, U : 2 * U] = (value & 15).astype(F32)
    up[IDX] = codes[...].astype(BF)
    for copy in copies:
        copy.wait()
    window[...] = up[pl.ds(pl.multiple_of(place[0] * CUT, 16), WINDOW)]


def load_first(inv, cpl, out, sems):
    copies = [
        pltpu.make_async_copy(inv, out.at[0:PANEL], sems.at[0]),
        pltpu.make_async_copy(cpl, out.at[PANEL : 2 * PANEL], sems.at[1]),
    ]
    for copy in copies:
        copy.start()
    out[2 * PANEL :] = jnp.zeros((128, PANEL), BF)
    for copy in copies:
        copy.wait()


def pick_first(place, own, far, factor, sems):
    even = place[1] % 2 == 0
    copies = [
        pltpu.make_async_copy(source, factor, sems.at[0]) for source in (own, far)
    ]

    @pl.when(even)
    def _():
        copies[0].start()

    @pl.when(jnp.logical_not(even))
    def _():
        copies[1].start()

    copies[0].wait()


def leaf_first(
    place, inv, rhs, cpl, rsep, leaf_idx, sep_idx, yt, rhs_out, one, inv_v, cpl_v,
    rhs_v, rsep_v, leaf_v, sep_v, codes, sems
):
    loads = [
        pltpu.make_async_copy(leaf_idx, leaf_v, sems.at[0]),
        pltpu.make_async_copy(sep_idx.at[0], sep_v, sems.at[1]),
        pltpu.make_async_copy(rhs, rhs_v, sems.at[2]),
    ]
    for i in range(4):
        rows = pl.ds(i * 256, 256)
        loads.append(pltpu.make_async_copy(inv.at[rows], inv_v.at[rows], sems.at[3 + i]))
    loads.append(pltpu.make_async_copy(cpl.at[0], cpl_v, sems.at[7]))
    loads.append(pltpu.make_async_copy(rsep, rsep_v, sems.at[8]))
    for load in loads:
        load.start()
    codes[...] = jnp.zeros_like(codes)
    loads[0].wait()
    for l in range(LEVELS):
        value = leaf_v[l]
        codes[l : l + 1] = (value >> 4).astype(F32)
        codes[16 + l : 17 + l] = (value & 15).astype(F32)
    loads[1].wait()
    value = sep_v[...]
    codes[32 : 32 + LEVELS - 1] = (value >> 4).astype(F32)
    codes[48 : 48 + LEVELS - 1] = (value & 15).astype(F32)
    one[NC:] = codes[...].astype(BF)
    loads[2].wait()
    rhs_t = rhs_v[...].astype(F32).T.astype(BF)
    for i in range(4):
        loads[3 + i].wait()
        span = (i + 1) * 256
        yt[:, i * 256 : span] = dot_t(rhs_t[:, 0:span], inv_v[i * 256 : span, 0:span]).astype(BF)
    loads[7].wait()
    one[0:NC] = dot_t(yt[...], cpl_v[0]).astype(BF)
    loads[8].wait()
    rhs_out[...] = rsep_v[...].astype(F32).T.astype(BF)


def leaf_second(yt, cpl_v, terms):
    terms[...] = dot_t(yt[...], cpl_v[1:].reshape(PANEL, LEAF)).astype(BF)


def which(place):
    return place[0], place[1], place[2]


def pick_two(core, y, z):
    return y == 1, y == 0, y == 2, y == 3


def pick_top(core, y, z):
    return y == 3, y == 2, y == 0, y == 1


def pick_four(core, y, z):
    after_me = (z == 0) | (z == 4)
    first = core == 0
    return (after_me & first) | (~after_me & ~first), (after_me & ~first) | (~after_me & first)


def pick_five(core, y, z):
    inner = (z == 2) | (z == 4)
    first = core == 0
    low = (z == 2) | (z == 0)
    same = (low & first) | (~low & ~first)
    return inner & same, inner & ~same, ~inner & ~same, ~inner & same


def pick_one(core, y, z):
    even = (y == 0) | (y == 2)
    return even, ~even


def window_sources(core, refs):
    own = refs[0]
    sources = [[(None, own, own, 0)]]
    for i in range(1, len(refs), 2):
        mine, other = refs[i], refs[i + 1]
        sources.append([(core == 0, mine, other, CUT), (core != 0, other, mine, CUT)])
    return sources


def start_one(cases, sources, copies_of):
    for case, versions in zip(cases, sources):
        for on_core, low, high, at in versions:

            @pl.when(case if on_core is None else case & on_core)
            def _(low=low, high=high, at=at):
                for copy in copies_of(low, high, at):
                    copy.start()

    return copies_of(*sources[0][0][1:])


def factor_copies(slots, factor, idx, sems):
    def copies_of(low, high, at):
        copies = [
            pltpu.make_async_copy(low.at[pr, pc], factor.at[r, c], sems.at[i])
            for i, (r, c, pr, pc) in enumerate(triangle_blocks())
        ]
        if slots:
            split = CUT - CPL0
            copies.append(
                pltpu.make_async_copy(low.at[CPL0:CUT], factor.at[PANEL : PANEL + split], sems.at[5])
            )
            copies.append(
                pltpu.make_async_copy(
                    high.at[CUT - at : packed_rows(slots) - at], factor.at[PANEL + split :], sems.at[6]
                )
            )
            copies.append(pltpu.make_async_copy(low.at[IDX], idx, sems.at[7]))
        return copies

    return copies_of


def finish_factor(slots, factor, hots, idx, copies):
    for rows, cols in (
        (slice(0, 128), slice(128, 512)),
        (slice(128, 256), slice(256, 512)),
        (slice(256, 384), slice(384, 512)),
    ):
        factor[rows, cols] = jnp.zeros((rows.stop - rows.start, cols.stop - cols.start), BF)
    if slots:
        copies[-1].wait()
        taken = sep_rows(idx[...])
        for k in range(slots):
            hots[:, k * U : (k + 1) * U] = hot(taken[k])
        copies = copies[:-1]
    else:
        hots[...] = jnp.zeros_like(hots)
    for copy in copies:
        copy.wait()


def stage(slots, pick, count, place, *refs):
    factor, hots, idx, sems = refs[count:]
    sources = [[(None, ref, ref, 0)] for ref in refs[:count]]
    copies = start_one(pick(*which(place)), sources, factor_copies(slots, factor, idx, sems))
    finish_factor(slots, factor, hots, idx, copies)


def stage_two(place, *refs):
    factor, hots, idx, sems = refs[7:]
    sources = window_sources(place[0], refs[:7])
    copies = start_one(pick_two(*which(place)), sources, factor_copies(3, factor, idx, sems))
    finish_factor(3, factor, hots, idx, copies)


def stage_and_pass(place, *refs):
    factor, hots, top, triangle, idx, sems = refs[7:]
    sources = window_sources(place[0], refs[:7])
    cases = pick_top(*which(place))

    def pass_copies(low, high, at):
        return [
            pltpu.make_async_copy(low.at[0:CUT], top.at[0:CUT], sems.at[8]),
            pltpu.make_async_copy(high.at[CUT - at : packed_rows(1) - at], top.at[CUT:], sems.at[9]),
            pltpu.make_async_copy(low.at[0:TRI], triangle, sems.at[10]),
        ]

    passed = start_one(cases, sources, pass_copies)
    copies = start_one(cases, sources, factor_copies(2, factor, idx, sems))
    finish_factor(2, factor, hots, idx, copies)
    for copy in passed:
        copy.wait()


ONE = 2 * U
PAIR_HOTS = 4 * 3 * U


def pair_rows(place, one, other):
    even = place[1] % 2 == 0
    mine, far = one[NC:], other[NC:]

    def rows(block, at, count):
        block = block.astype(F32)
        return [
            block[at + i : at + i + 1] * 16.0 + block[at + 16 + i : at + 17 + i] for i in range(count)
        ]

    left, right = jnp.where(even, mine, far), jnp.where(even, far, mine)
    return rows(left, 0, LEVELS), rows(right, 0, LEVELS), rows(left, 32, LEVELS - 1)


def stage_pair(place, one, other, hots):
    a, b, up = pair_rows(place, one, other)
    for k in range(4):
        at = k * 3 * U
        hots[:, at : at + 3 * U] = hot(jnp.concatenate([a[k + 1], b[k + 1], up[k]], axis=1))


def half_of(place):
    y = place[1]
    return jnp.where((y == 1) | (y == 2), 1, 0)


def level_one(place, one, recv, terms, rhs, factor, hots, y_keep, passed, keep, send, y_all):
    even = place[1] % 2 == 0
    a, b, _ = pair_rows(place, one, recv)
    hots[...] = hot(jnp.concatenate([a[0], b[0]], axis=1))
    total = dot_t(jnp.concatenate([one[0:NC], recv[0:NC]], axis=1), hots[...])
    resid = (rhs[...].astype(F32) - total).astype(BF)
    y = dot_t(resid, factor[0:PANEL]).astype(BF)
    y_all[:, 0:PANEL] = y
    y_all[:, PANEL:] = jnp.where(even, push_values(factor, y, 4), rhs[...])
    side = half_of(place)
    mine = pl.ds(pl.multiple_of(side * 128, 128), 128)
    theirs = pl.ds(pl.multiple_of((1 - side) * 128, 128), 128)
    send[:, 0:PANEL] = terms[theirs]
    send[:, PANEL:] = y_all[theirs, PANEL:]
    keep[:, 0:PANEL] = terms[mine]
    keep[:, PANEL:] = y_all[mine, PANEL:]
    y_keep[...] = y_all[mine, 0:PANEL]
    passed[2 * PANEL :] = y_all[theirs, 0:PANEL]


def join_pair(place, keep, recv, hots, panel_keep, panel_send, panels):
    ring, even = place[1], place[1] % 2 == 0
    a, b = keep[...], recv[...]
    left, right = jnp.where(even, a, b), jnp.where(even, b, a)
    held = right[:, PANEL:].astype(F32)
    level = jnp.where(ring < 2, 2, place[3])
    for k in range(4):
        at = slice(k * U, (k + 1) * U)
        start = k * 3 * U
        parts = [left[:, at], right[:, at], left[:, PANEL + k * U : PANEL + (k + 1) * U]]
        total = dot_t(jnp.concatenate(parts, axis=1), hots[:, start : start + 3 * U])
        total = total - jnp.where(level == k + 2, held, 0.0)
        panels[:, k * PANEL : (k + 1) * PANEL] = total.astype(BF)
    side = ring // 2
    panel_keep[...] = panels[pl.ds(pl.multiple_of(side * 64, 64), 64)]
    panel_send[...] = panels[pl.ds(pl.multiple_of((1 - side) * 64, 64), 64)]


def level_up(level, mine, recv, factor, hots, y_out, panels):
    slots = LEVELS - level
    total = mine[...].astype(F32) + recv[...].astype(F32)
    y = dot_t((-total[:, 0:PANEL]).astype(BF), factor[0:PANEL]).astype(BF)
    y_out[...] = y
    values = push_values(factor, y, slots)
    for k in range(slots):
        at = slice((k + 1) * PANEL, (k + 2) * PANEL)
        term = dot_t(values[:, k * U : (k + 1) * U], hots[:, k * U : (k + 1) * U])
        panels[:, k * PANEL : (k + 1) * PANEL] = (total[:, at] + term).astype(BF)


def turn(mine, recv, f3, f4, f5, h3, h4, y3, y4, x_out):
    total = mine[...].astype(F32) + recv[...].astype(F32)
    y5 = dot_t((-total).astype(BF), f5[0:PANEL]).astype(BF)
    x5 = solve_back(f5, [], y5, [])
    x4 = solve_back(f4, [h4[...]], y4[...], [x5])
    x3 = solve_back(f3, [h3[:, 0:U], h3[:, U : 2 * U]], y3[...], [x4, x5])
    for k, x in enumerate((x3, x4, x5)):
        x_out[:, k * PANEL : (k + 1) * PANEL] = x


def level_two_back(place, mine, recv, f2, h2, y2, x_out):
    x = jnp.where(place[2] % 2 == 0, mine[...], recv[...])
    above = [x[:, k * PANEL : (k + 1) * PANEL] for k in range(3)]
    x_out[:, 0:PANEL] = solve_back(f2, [h2[:, k * U : (k + 1) * U] for k in range(3)], y2[...], above)
    x_out[:, PANEL:] = x


def level_one_back(place, mine, recv, y_mine, factor, first_hots, hots, x1_out, x, rows_send):
    side = place[1] // 2
    even = place[1] % 2 == 0
    x[pl.ds(pl.multiple_of(side * 64, 64), 64)] = mine[...]
    x[pl.ds(pl.multiple_of((1 - side) * 64, 64), 64)] = recv[...]
    above = [x[:, k * PANEL : (k + 1) * PANEL] for k in range(4)]
    ups = [hots[:, k * 3 * U + 2 * U : (k + 1) * 3 * U] for k in range(4)]
    x1 = solve_back(factor, ups, jnp.where(even, y_mine[...], factor[2 * PANEL :]), above)
    x1_out[...] = x1
    for l, value in enumerate([x1] + above):
        pair = first_hots[...] if l == 0 else hots[:, (l - 1) * 3 * U : (l - 1) * 3 * U + 2 * U]
        pair = jnp.where(even, pair[:, U:], pair[:, 0:U])
        rows_send[:, l * U : (l + 1) * U] = dot(value, pair).astype(BF)


def level_one_rest(place, x1_ref, x, first_hots, hots, rows_keep, sep_keep, sep_send, sep_a, sep_b, sems):
    even = place[1] % 2 == 0
    x1 = x1_ref[...]
    above = [x[:, k * PANEL : (k + 1) * PANEL] for k in range(4)]
    level = jnp.where(place[1] < 2, 2, place[3])
    held = jnp.where(level == 0, jnp.zeros_like(x1), above[0])
    for k in (1, 2, 3):
        held = jnp.where(level == k + 2, above[k], held)
    sep_a[...] = jnp.where(even, x1, held)
    sep_b[...] = jnp.where(even, held, x1)
    stores = [
        pltpu.make_async_copy(sep_a, sep_keep, sems.at[0]),
        pltpu.make_async_copy(sep_b, sep_send, sems.at[1]),
    ]
    for store in stores:
        store.start()
    for l, value in enumerate([x1] + above):
        pair = first_hots[...] if l == 0 else hots[:, (l - 1) * 3 * U : (l - 1) * 3 * U + 2 * U]
        pair = jnp.where(even, pair[:, 0:U], pair[:, U:])
        rows_keep[:, l * U : (l + 1) * U] = dot(value, pair).astype(BF)
    for store in stores:
        store.wait()


def leaf_half(rows, inv, cpl, yt):
    back = (yt.astype(F32) - dot(rows[...], cpl[...].reshape(TERM, LEAF))).astype(BF)
    parts = []
    for i in range(4):
        start = i * 256
        parts.append(dot(back[:, start:], inv[start:, start : start + 256]).astype(BF))
    return jnp.concatenate(parts, axis=1)


def leaf_mine(place, keep, inv, cpl, yt, chosen, xt_out, picks_out):
    side = half_of(place)
    xt = leaf_half(keep, inv, cpl, yt[pl.ds(pl.multiple_of(side * 128, 128), 128)])
    xt_out[...] = xt
    picks_out[...] = dot_t(chosen[...], xt).astype(BF)


def leaf_other(place, recv, inv, cpl, yt, chosen, xt_mine, picks_mine, xt_out, picks_out, xt, picks, sems):
    side = half_of(place)
    mine = pl.ds(pl.multiple_of(side * 128, 128), 128)
    other = pl.ds(pl.multiple_of((1 - side) * 128, 128), 128)
    xt[mine] = xt_mine[...]
    picks[:, mine] = picks_mine[...]
    far = leaf_half(recv, inv, cpl, yt[other])
    xt[other] = far
    stores = [pltpu.make_async_copy(xt, xt_out, sems.at[0])]
    stores[0].start()
    for i in range(2):
        part = slice(i * 16 * SLOTS, (i + 1) * 16 * SLOTS)
        picks[part, other] = dot_t(chosen[part], far).astype(BF)
        stores.append(pltpu.make_async_copy(picks.at[part], picks_out.at[part], sems.at[1 + i]))
        stores[-1].start()
    for store in stores:
        store.wait()


def turn_leaf(xt, x_leaf, xt_v, sems):
    load = pltpu.make_async_copy(xt, xt_v, sems.at[0])
    load.start()
    load.wait()
    for i in range(4):
        part = slice(i * 256, (i + 1) * 256)
        x_leaf[part] = xt_v[:, part].astype(F32).T.astype(BF)


def turn_sep(place, keep, recv, x_sep, keep_v, recv_v, both, sems):
    loads = [
        pltpu.make_async_copy(keep, keep_v, sems.at[0]),
        pltpu.make_async_copy(recv, recv_v, sems.at[1]),
    ]
    for load in loads:
        load.start()
    for load in loads:
        load.wait()
    side = half_of(place)
    both[pl.ds(pl.multiple_of(side * 128, 128), 128)] = keep_v[...].astype(F32)
    both[pl.ds(pl.multiple_of((1 - side) * 128, 128), 128)] = recv_v[...].astype(F32)
    x_sep[...] = both[...].T.astype(BF)


def stretch_sum(weight, got, out, weight_v, sems):
    load = pltpu.make_async_copy(weight, weight_v, sems.at[0])
    load.start()
    load.wait()
    out[...] = dot(weight_v[0], got[...]) + dot(weight_v[1], got[...])


def iota(rows, cols, axis):
    return lax.broadcasted_iota(jnp.int32, (rows, cols), axis)


def ones_where(mask):
    return jnp.where(mask, 1.0, 0.0)


def stay_plan(place, dofs, coef, chosen, weight_out, grid, turned, dof_t, coef_t, weight, sems):
    me = place[2] * RING + place[1]
    grid[...] = jnp.full((128, 128), -1, jnp.int32)
    for r in range(16):
        grid[8 * r : 8 * r + 6] = dofs[:, 128 * r : 128 * (r + 1)]
    dof = grid[...]
    match = ones_where((dof >> 10) == me)
    row, col = iota(128, 128, 0), iota(128, 128, 1)
    same = (row >> 3) == (col >> 3)
    earlier = ((row >> 6) == (col >> 6)) & (row < col)
    match_b = match.astype(BF)
    count = dot(ones_where(same).astype(BF), match_b).astype(BF)
    rank = dot(count, ones_where(earlier).astype(BF))
    rank = rank + dot(ones_where(same & (col < row)).astype(BF), match_b)
    high = ((dof >> 5) & 31).astype(F32) + 1.0
    low = (dof & 31).astype(F32)
    rank = jnp.where(match > 0.0, rank, -1.0)
    parts = []
    for value in (high, low):
        for s in range(SLOTS):
            parts.append(jnp.where(rank == float(s), value, 0.0).astype(BF))
    block = ones_where(iota(16, 128, 0) == (iota(16, 128, 1) >> 3)).astype(BF)
    flat = dot(block, jnp.concatenate(parts, axis=1)).astype(BF)
    width = SLOTS * 128
    lane, q = iota(width, 32, 0), iota(width, 32, 1)
    gather = ones_where(q == ((lane >> 6) & 1) * SLOTS + (lane >> 7)).astype(BF)
    table_high = dot(flat[:, 0:width], gather).astype(BF)
    table_low = dot(flat[:, width:], gather).astype(BF)
    spread = ones_where((iota(512, 16, 0) >> 5) == iota(512, 16, 1)).astype(BF)
    here = ones_where((iota(512, 32, 0) & 31) == iota(512, 32, 1))
    sel_high = jnp.sum(dot(spread, table_high) * here, axis=1, keepdims=True)
    sel_low = jnp.sum(dot(spread, table_low) * here, axis=1, keepdims=True)
    sel = (sel_high - 1.0) * 32.0 + sel_low
    for part in range(4):
        at = slice(part * 128, (part + 1) * 128)
        chosen[at] = ones_where(iota(128, LEAF, 1).astype(F32) == sel[at]).astype(BF)

    block_row = pl.multiple_of((me >> 1) * 8, 8)
    block_col = pl.multiple_of((me >> 1) * 128, 128)
    half = pl.ds(pl.multiple_of((me & 1) * 64, 64), 64)
    turned[...] = jnp.zeros_like(turned)
    turned[0:8] = grid[pl.ds(block_row, 8)].astype(F32)
    dof_t[...] = turned[...].T
    turned[0:6] = coef[:, pl.ds(block_col, 128)]
    coef_t[...] = turned[...].T
    my_dof, my_coef = dof_t[half], coef_t[half]
    lanes = iota(64, 32, 1)
    source = [my_dof[:, k : k + 1].astype(jnp.int32) >> 10 for k in range(6)]
    named = [ones_where(source[k] == lanes) for k in range(6)]
    every = named[0]
    for k in range(1, 6):
        every = every + named[k]
    lower = ones_where(iota(64, 64, 1) < iota(64, 64, 0)).astype(BF)
    running = dot(lower, every.astype(BF))
    total = jnp.zeros((64, 512), F32)
    slots = iota(64, 512, 1).astype(F32)
    for k in range(6):
        at = jnp.sum(named[k] * running, axis=1, keepdims=True)
        slot = source[k].astype(F32) * float(SLOTS) + at
        total = total + jnp.where(slots == slot, my_coef[:, k : k + 1], 0.0)
        running = running + named[k]
    first = total.astype(BF)
    weight[0] = first
    weight[1] = (total - first.astype(F32)).astype(BF)
    store = pltpu.make_async_copy(weight, weight_out, sems.at[0])
    store.start()
    store.wait()


def after(value, *others):
    return lax.optimization_barrier((value, *others))[0]


def on_device(
    rhs_leaf, rhs_sep, leaf_inv, leaf_cpl, leaf_idx, sep_inv, sep_cpl, sep_idx, stay_dofs, stay_coef
):
    rows_axis, cols_axis = "rows", "cols"
    columns, rows = lax.axis_size(cols_axis), lax.axis_size(rows_axis)
    me = lax.axis_index(rows_axis)
    core = lax.axis_index(cols_axis) % 2
    y, z = me % RING, me // RING
    top_level = jnp.where(z % 2 == 0, 3, jnp.where(z % 4 == 1, 4, jnp.where(z == 3, 5, 0)))
    place = jnp.stack([core, y, z, top_level]).astype(jnp.int32)

    def route(value, target):
        pairs = []
        for c in range(columns):
            for r in range(rows):
                to = target(c % 2, r % RING, r // RING)
                if to is not None:
                    pairs.append((c * rows + r, (c - c % 2 + to[0]) * rows + to[2] * RING + to[1]))
        return lax.ppermute(value, (cols_axis, rows_axis), pairs)

    def swap_core(value):
        return route(value, lambda c, y, z: (1 - c, y, z))

    def swap(value, flip):
        return route(value, lambda c, y, z: (c, y ^ flip, z))

    def to_odd(value):
        return route(value, lambda c, y, z: (c, y + 1, z) if y % 2 == 0 else None)

    sep_rows_flat = sep_cpl.reshape(4 * U, PANEL)
    own_up, window = call(
        pack_factor,
        [pinned(packed_rows(3), PANEL), pinned(WINDOW, PANEL)],
        [place, sep_inv, sep_rows_flat, sep_idx],
        [SMEM, HBM, HBM, HBM],
        [pltpu.VMEM((16, PANEL), F32), pltpu.VMEM((LEVELS - 1, U), jnp.int32), dma(7)],
    )
    with jax.named_scope("factors_to_pair"):
        pair = route(window, lambda c, y, z: (c, y ^ 1, z) if y % 2 else None)
    with jax.named_scope("factors_to_other"):
        beside = route(window, lambda c, y, z: (c, y ^ 3, z) if y % 2 else None)
    yt, rhs, one, inv_v, cpl_v = call(
        leaf_first,
        [
            pinned(NC, LEAF),
            pinned(NC, PANEL),
            pinned(NC + 4 * 16, U),
            pinned(LEAF, LEAF),
            pinned(LEVELS, U, LEAF),
        ],
        [after(place, own_up), leaf_inv, rhs_leaf, leaf_cpl, rhs_sep, leaf_idx.transpose(1, 0, 2), sep_idx],
        [SMEM] + [HBM] * 6,
        [
            pltpu.VMEM((LEAF, NC), BF),
            pltpu.VMEM((PANEL, NC), BF),
            pltpu.VMEM((LEVELS, 1, U), jnp.int32),
            pltpu.VMEM((LEVELS - 1, U), jnp.int32),
            pltpu.VMEM((64, U), F32),
            dma(9),
        ],
    )
    with jax.named_scope("first_terms"):
        recv = swap(one, 1)
    (terms,) = call(
        leaf_second, [pinned(NC, PANEL)], [yt, cpl_v], [VMEM, VMEM]
    )

    def ready(slots, pick, sources):
        return call(
            functools.partial(stage, slots, pick, len(sources)),
            [pinned(factor_rows(slots), PANEL), pinned(PANEL, max(slots, 1) * U)],
            [place, *sources],
            [SMEM] + [ANY] * len(sources),
            [pltpu.VMEM((16, PANEL), BF), dma(8)],
        )

    def rise(level, panel, recv, factor, hots):
        slots = LEVELS - level
        return call(
            functools.partial(level_up, level),
            [pinned(64, PANEL), pinned(64, slots * PANEL)],
            [panel, recv, factor, hots],
            [VMEM] * 4,
        )

    (f1,) = call(
        load_first,
        [pinned(2 * PANEL + 128, PANEL)],
        [after(sep_inv, one), sep_rows_flat],
        [HBM, HBM],
        [dma(2)],
    )
    pair = after(pair, recv, f1, terms)
    with jax.named_scope("factors_across"):
        far = route(pair, lambda c, y, z: (c, y ^ 3, z) if y % 2 == 0 else None)
    first = after(recv, f1)
    first_hots, y1, passed, keep, send = call(
        level_one,
        [
            pinned(PANEL, ONE),
            pinned(128, PANEL),
            pinned(2 * PANEL + 128, PANEL),
            pinned(128, 2 * PANEL),
            pinned(128, 2 * PANEL),
        ],
        [place, one, first, terms, rhs, f1],
        [SMEM] + [VMEM] * 5,
        [pltpu.VMEM((NC, 2 * PANEL), BF)],
        aliases={5: 2},
    )
    with jax.named_scope("terms_pair"):
        recv = swap(send, 1)
    pair, beside = after((pair, beside), send)
    with jax.named_scope("pair_to_core"):
        pair_o = swap_core(pair)
    with jax.named_scope("beside_to_core"):
        beside_o = swap_core(beside)
    chosen, weight = call(
        stay_plan,
        [pinned(32 * SLOTS, LEAF), stored(2, 64, 512)],
        [place, stay_dofs, after(stay_coef, send)],
        [SMEM, VMEM, VMEM],
        [
            pltpu.VMEM((128, 128), jnp.int32),
            pltpu.VMEM((128, 128), F32),
            pltpu.VMEM((128, 128), F32),
            pltpu.VMEM((128, 128), F32),
            pltpu.VMEM((2, 64, 512), BF),
            dma(1),
        ],
        [VMEM, HBM],
    )
    (h1,) = call(
        stage_pair, [pinned(PANEL, PAIR_HOTS)], [place, one, after(first, send)], [SMEM, VMEM, VMEM]
    )
    recv = after(recv, chosen, h1)
    panel, send = call(
        join_pair,
        [pinned(64, 4 * PANEL), pinned(64, 4 * PANEL)],
        [place, keep, recv, h1],
        [SMEM] + [VMEM] * 3,
        [pltpu.VMEM((128, 4 * PANEL), BF)],
    )
    with jax.named_scope("panels_ring"):
        recv = swap(send, 3)
    far = after(far, send)
    with jax.named_scope("far_to_core"):
        far_o = swap_core(far)
    at = [own_up, pair, pair_o, beside, beside_o, far, far_o]
    f2, h2 = call(
        stage_two,
        [pinned(factor_rows(3), PANEL), pinned(PANEL, 3 * U)],
        [place, *at],
        [SMEM] + [ANY] * 7,
        [pltpu.VMEM((16, PANEL), BF), dma(8)],
    )
    f3, h3, top, triangle = call(
        stage_and_pass,
        [
            pinned(factor_rows(2), PANEL),
            pinned(PANEL, 2 * U),
            pinned(packed_rows(1), PANEL),
            pinned(TRI, PANEL),
        ],
        [place, *at],
        [SMEM] + [ANY] * 7,
        [pltpu.VMEM((16, PANEL), BF), dma(11)],
    )

    def next_up(value, senders):
        return route(value, lambda c, y, z: (c, y, z + (1 if c else -1)) if z in senders else None)

    with jax.named_scope("factors_up"):
        up = next_up(top, (1, 3, 5))
    with jax.named_scope("factor_top"):
        last = route(
            triangle,
            lambda c, y, z: (c, y, 0 if c else 6) if z == 3 else None,
        )
    with jax.named_scope("first_factor_to_odd"):
        passed_far = to_odd(after(passed, f2))
    recv = after(recv, f2, h2, f3, h3)
    y2, panel = rise(2, panel, recv, f2, h2)
    with jax.named_scope("panels_z1"):
        recv = route(panel, lambda c, y, z: (c, y, z - 1) if z % 2 else None)
    y3, panel = rise(3, panel, recv, f3, h3)
    with jax.named_scope("panels_z2"):
        recv = route(panel, lambda c, y, z: (c, y, z ^ 2) if z % 2 == 0 else None)
    up, last = after((up, last), panel)
    with jax.named_scope("up_to_core"):
        up_o = swap_core(up)
    with jax.named_scope("last_to_core"):
        last_o = swap_core(last)
    f4, h4 = ready(1, pick_four, [up, up_o])
    f5, _ = ready(0, pick_five, [up, up_o, last, last_o])
    recv = after(recv, f4, h4, f5)
    y4, panel = rise(4, panel, recv, f4, h4)
    with jax.named_scope("panels_z3"):
        recv = route(panel, lambda c, y, z: (c, y, 6 - z) if z % 2 == 0 else None)
    (x,) = call(
        turn,
        [pinned(64, 3 * PANEL)],
        [panel, recv, f3, f4, f5, h3, h4, y3, y4],
        [VMEM] * 9,
    )
    with jax.named_scope("down_z1"):
        recv = route(x, lambda c, y, z: (c, y, z + 1) if z % 2 == 0 else None)
    (x,) = call(
        level_two_back,
        [pinned(64, 4 * PANEL)],
        [place, x, recv, f2, h2, y2],
        [SMEM] + [VMEM] * 5,
    )
    with jax.named_scope("down_ring"):
        recv = swap(x, 3)
    passed_far = after(passed_far, x)
    (f1,) = call(
        pick_first,
        [pinned(2 * PANEL + 128, PANEL)],
        [place, passed, passed_far],
        [SMEM, ANY, ANY],
        [dma(1)],
    )
    recv = after(recv, f1)
    x1, x, rows_send = call(
        level_one_back,
        [pinned(128, PANEL), pinned(128, 4 * PANEL), pinned(128, TERM)],
        [place, x, recv, y1, f1, first_hots, h1],
        [SMEM] + [VMEM] * 6,
    )
    with jax.named_scope("rows_back"):
        recv = swap(rows_send, 1)
    rows_keep, sep_keep, sep_send = call(
        level_one_rest,
        [pinned(128, TERM), stored(128, PANEL), stored(128, PANEL)],
        [place, x1, x, first_hots, h1],
        [SMEM] + [VMEM] * 4,
        [pltpu.VMEM((128, PANEL), BF), pltpu.VMEM((128, PANEL), BF), dma(2)],
        [VMEM, HBM, HBM],
    )
    xt_mine, picks_mine = call(
        leaf_mine,
        [pinned(128, LEAF), pinned(32 * SLOTS, 128)],
        [place, rows_keep, inv_v, cpl_v, yt, chosen],
        [SMEM] + [VMEM] * 5,
    )
    recv = after(recv, xt_mine)
    xt, picks = call(
        leaf_other,
        [stored(NC, LEAF), stored(32 * SLOTS, NC)],
        [place, recv, inv_v, cpl_v, yt, chosen, xt_mine, picks_mine],
        [SMEM] + [VMEM] * 7,
        [pltpu.VMEM((NC, LEAF), BF), pltpu.VMEM((32 * SLOTS, NC), BF), dma(3)],
        [HBM, HBM],
        moved=14 * 10**6,
    )
    with jax.named_scope("sep_back"):
        sep_recv = swap(after(sep_send, picks), 1)
    got = lax.all_to_all(
        picks.reshape(32, SLOTS, NC), rows_axis, 0, 0, tiled=True
    ).reshape(32 * SLOTS, NC)
    (x_leaf,) = call(
        turn_leaf, [plain(LEAF, NC)], [xt], [HBM], [pltpu.VMEM((NC, LEAF), BF), dma(1)]
    )
    (x_sep,) = call(
        turn_sep,
        [plain(PANEL, NC)],
        [place, sep_keep, sep_recv],
        [SMEM, HBM, HBM],
        [
            pltpu.VMEM((128, PANEL), BF),
            pltpu.VMEM((128, PANEL), BF),
            pltpu.VMEM((NC, PANEL), F32),
            dma(2),
        ],
    )
    (stretch,) = call(
        stretch_sum,
        [plain(64, NC, dtype=F32)],
        [weight, got],
        [HBM, VMEM],
        [pltpu.VMEM((2, 64, 512), BF), dma(1)],
    )
    return (x_leaf, x_sep, stretch)


def solution(mesh):
    return jax.shard_map(
        on_device,
        mesh=mesh,
        in_specs=(
            P("rows", "cols"),
            P("rows", "cols"),
            P("rows", None),
            P("rows", None, None, None),
            P("rows", None, None),
            P("rows", None),
            P("rows", None, None, None),
            P("rows", None, None),
            P(),
            P(),
        ),
        out_specs=(P("rows", "cols"), P("rows", "cols"), P("rows", "cols")),
        check_vma=False,
    )
```

```python
import functools

import jax
import jax.numpy as jnp
from jax import lax
from jax.experimental import pallas as pl
from jax.experimental.pallas import tpu as pltpu
from jax.sharding import PartitionSpec as P

BF = jnp.bfloat16
F32 = jnp.float32
LEAF, PANEL, U, NC, LEVELS = 1024, 512, 128, 256, 5
RING, DEPTH = 4, 8
TERM = LEVELS * U
SLOTS = 16
VMEM_LIMIT = 16 * 1024 * 1024

TRI = 320
IDX = slice(TRI, TRI + 16)
CUT, WINDOW = 352, 368
CPL0 = TRI + 16


def packed_rows(slots):
    return CPL0 + slots * U


def factor_rows(slots):
    return PANEL + slots * U


def triangle_blocks():
    return [
        (slice(384, 512), slice(0, 512), slice(0, 128), slice(0, 512)),
        (slice(256, 384), slice(0, 384), slice(128, 256), slice(0, 384)),
        (slice(0, 128), slice(0, 128), slice(128, 256), slice(384, 512)),
        (slice(128, 192), slice(0, 256), slice(256, 320), slice(0, 256)),
        (slice(192, 256), slice(0, 256), slice(256, 320), slice(256, 512)),
    ]


def dot(left, right):
    return jnp.dot(left, right, preferred_element_type=F32)


def dot_t(left, right):
    return lax.dot_general(left, right, (((1,), (1,)), ((), ())), preferred_element_type=F32)


VMEM = pl.BlockSpec(memory_space=pltpu.VMEM)
SMEM = pl.BlockSpec(memory_space=pltpu.SMEM)
HBM = pl.BlockSpec(memory_space=pltpu.HBM)
ANY = pl.BlockSpec(memory_space=pl.ANY)


def call(body, outs, args, specs, scratch=(), out_specs=None, aliases=None, flops=10**8, moved=10**6):
    args = [
        in_vmem(arg) if spec is VMEM else in_hbm(arg) if spec is HBM else arg
        for arg, spec in zip(args, specs)
    ]
    return pl.pallas_call(
        body,
        out_shape=outs,
        in_specs=specs,
        out_specs=out_specs or [VMEM] * len(outs),
        scratch_shapes=list(scratch),
        input_output_aliases=aliases or {},
        compiler_params=pltpu.CompilerParams(vmem_limit_bytes=VMEM_LIMIT),
        cost_estimate=pl.CostEstimate(flops=flops, bytes_accessed=moved, transcendentals=0),
    )(*args)


def dma(n):
    return pltpu.SemaphoreType.DMA((n,))


def pinned(*dims, dtype=BF):
    return pltpu.VMEM(dims, dtype)


def plain(*dims, dtype=BF):
    return jax.ShapeDtypeStruct(dims, dtype)


def stored(*dims, dtype=BF):
    return pltpu.HBM(dims, dtype)


def in_vmem(value):
    return pltpu.with_memory_space_constraint(value, pltpu.VMEM)


def in_hbm(value):
    return pltpu.with_memory_space_constraint(value, pltpu.HBM)


def hot(rows):
    place = lax.broadcasted_iota(jnp.int32, (PANEL, rows.shape[1]), 0).astype(F32)
    return jnp.where(place == rows, 1.0, 0.0).astype(BF)


def sep_rows(block):
    block = block.astype(F32)
    return [block[s : s + 1, 0:U] * 16.0 + block[s : s + 1, U : 2 * U] for s in range(LEVELS - 1)]


def push_values(factor, y, slots):
    return dot_t(y, factor[PANEL : PANEL + slots * U]).astype(BF)


def solve_back(factor, hots, y, above):
    back = y
    slots = len(above)
    if slots:
        taken = [dot(above[k], hots[k]).astype(BF) for k in range(slots)]
        taken = taken[0] if slots == 1 else jnp.concatenate(taken, axis=1)
        sub = dot(taken, factor[PANEL : PANEL + slots * U])
        back = (y.astype(F32) - sub).astype(BF)
    return dot(back, factor[0:PANEL]).astype(BF)


def pack_factor(place, inv, cpl, sep_idx, up, window, codes, sep_v, sems):
    load = pltpu.make_async_copy(sep_idx.at[0], sep_v, sems.at[0])
    copies = [
        pltpu.make_async_copy(inv.at[r, c], up.at[pr, pc], sems.at[1 + i])
        for i, (r, c, pr, pc) in enumerate(triangle_blocks())
    ]
    copies.append(pltpu.make_async_copy(cpl.at[0 : 3 * U], up.at[CPL0 : packed_rows(3)], sems.at[6]))
    load.start()
    for copy in copies:
        copy.start()
    codes[...] = jnp.zeros_like(codes)
    load.wait()
    value = sep_v[...]
    codes[0 : LEVELS - 1, 0:U] = (value >> 4).astype(F32)
    codes[0 : LEVELS - 1, U : 2 * U] = (value & 15).astype(F32)
    up[IDX] = codes[...].astype(BF)
    for copy in copies:
        copy.wait()
    window[...] = up[pl.ds(pl.multiple_of(place[0] * CUT, 16), WINDOW)]


def load_first(inv, cpl, out, sems):
    copies = [
        pltpu.make_async_copy(inv, out.at[0:PANEL], sems.at[0]),
        pltpu.make_async_copy(cpl, out.at[PANEL : 2 * PANEL], sems.at[1]),
    ]
    for copy in copies:
        copy.start()
    out[2 * PANEL :] = jnp.zeros((128, PANEL), BF)
    for copy in copies:
        copy.wait()


def pick_first(place, own, far, factor, sems):
    even = place[1] % 2 == 0
    copies = [
        pltpu.make_async_copy(source, factor, sems.at[0]) for source in (own, far)
    ]

    @pl.when(even)
    def _():
        copies[0].start()

    @pl.when(jnp.logical_not(even))
    def _():
        copies[1].start()

    copies[0].wait()


def leaf_first(
    place, inv, rhs, cpl, rsep, leaf_idx, sep_idx, yt, rhs_out, one, inv_v, cpl_v,
    rhs_v, rsep_v, leaf_v, sep_v, codes, sems
):
    loads = [
        pltpu.make_async_copy(leaf_idx, leaf_v, sems.at[0]),
        pltpu.make_async_copy(sep_idx.at[0], sep_v, sems.at[1]),
        pltpu.make_async_copy(rhs, rhs_v, sems.at[2]),
    ]
    for i in range(4):
        rows = pl.ds(i * 256, 256)
        loads.append(pltpu.make_async_copy(inv.at[rows], inv_v.at[rows], sems.at[3 + i]))
    loads.append(pltpu.make_async_copy(cpl.at[0], cpl_v, sems.at[7]))
    loads.append(pltpu.make_async_copy(rsep, rsep_v, sems.at[8]))
    for load in loads:
        load.start()
    codes[...] = jnp.zeros_like(codes)
    loads[0].wait()
    for l in range(LEVELS):
        value = leaf_v[l]
        codes[l : l + 1] = (value >> 4).astype(F32)
        codes[16 + l : 17 + l] = (value & 15).astype(F32)
    loads[1].wait()
    value = sep_v[...]
    codes[32 : 32 + LEVELS - 1] = (value >> 4).astype(F32)
    codes[48 : 48 + LEVELS - 1] = (value & 15).astype(F32)
    one[NC:] = codes[...].astype(BF)
    loads[2].wait()
    rhs_t = rhs_v[...].astype(F32).T.astype(BF)
    for i in range(4):
        loads[3 + i].wait()
        span = (i + 1) * 256
        yt[:, i * 256 : span] = dot_t(rhs_t[:, 0:span], inv_v[i * 256 : span, 0:span]).astype(BF)
    loads[7].wait()
    one[0:NC] = dot_t(yt[...], cpl_v[0]).astype(BF)
    loads[8].wait()
    rhs_out[...] = rsep_v[...].astype(F32).T.astype(BF)


def leaf_second(yt, cpl_v, terms):
    terms[...] = dot_t(yt[...], cpl_v[1:].reshape(PANEL, LEAF)).astype(BF)


def which(place):
    return place[0], place[1], place[2]


def pick_two(core, y, z):
    return y == 1, y == 0, y == 2, y == 3


def pick_top(core, y, z):
    return y == 3, y == 2, y == 0, y == 1


def pick_four(core, y, z):
    after_me = (z == 0) | (z == 4)
    first = core == 0
    return (after_me & first) | (~after_me & ~first), (after_me & ~first) | (~after_me & first)


def pick_five(core, y, z):
    inner = (z == 2) | (z == 4)
    first = core == 0
    low = (z == 2) | (z == 0)
    same = (low & first) | (~low & ~first)
    return inner & same, inner & ~same, ~inner & ~same, ~inner & same


def pick_one(core, y, z):
    even = (y == 0) | (y == 2)
    return even, ~even


def window_sources(core, refs):
    own = refs[0]
    sources = [[(None, own, own, 0)]]
    for i in range(1, len(refs), 2):
        mine, other = refs[i], refs[i + 1]
        sources.append([(core == 0, mine, other, CUT), (core != 0, other, mine, CUT)])
    return sources


def start_one(cases, sources, copies_of):
    for case, versions in zip(cases, sources):
        for on_core, low, high, at in versions:

            @pl.when(case if on_core is None else case & on_core)
            def _(low=low, high=high, at=at):
                for copy in copies_of(low, high, at):
                    copy.start()

    return copies_of(*sources[0][0][1:])


def factor_copies(slots, factor, idx, sems):
    def copies_of(low, high, at):
        copies = [
            pltpu.make_async_copy(low.at[pr, pc], factor.at[r, c], sems.at[i])
            for i, (r, c, pr, pc) in enumerate(triangle_blocks())
        ]
        if slots:
            split = CUT - CPL0
            copies.append(
                pltpu.make_async_copy(low.at[CPL0:CUT], factor.at[PANEL : PANEL + split], sems.at[5])
            )
            copies.append(
                pltpu.make_async_copy(
                    high.at[CUT - at : packed_rows(slots) - at], factor.at[PANEL + split :], sems.at[6]
                )
            )
            copies.append(pltpu.make_async_copy(low.at[IDX], idx, sems.at[7]))
        return copies

    return copies_of


def finish_factor(slots, factor, hots, idx, copies):
    for rows, cols in (
        (slice(0, 128), slice(128, 512)),
        (slice(128, 256), slice(256, 512)),
        (slice(256, 384), slice(384, 512)),
    ):
        factor[rows, cols] = jnp.zeros((rows.stop - rows.start, cols.stop - cols.start), BF)
    if slots:
        copies[-1].wait()
        taken = sep_rows(idx[...])
        for k in range(slots):
            hots[:, k * U : (k + 1) * U] = hot(taken[k])
        copies = copies[:-1]
    else:
        hots[...] = jnp.zeros_like(hots)
    for copy in copies:
        copy.wait()


def stage(slots, pick, count, place, *refs):
    factor, hots, idx, sems = refs[count:]
    sources = [[(None, ref, ref, 0)] for ref in refs[:count]]
    copies = start_one(pick(*which(place)), sources, factor_copies(slots, factor, idx, sems))
    finish_factor(slots, factor, hots, idx, copies)


def stage_two(place, *refs):
    factor, hots, idx, sems = refs[7:]
    sources = window_sources(place[0], refs[:7])
    copies = start_one(pick_two(*which(place)), sources, factor_copies(3, factor, idx, sems))
    finish_factor(3, factor, hots, idx, copies)


def stage_and_pass(place, *refs):
    factor, hots, top, triangle, idx, sems = refs[7:]
    sources = window_sources(place[0], refs[:7])
    cases = pick_top(*which(place))

    def pass_copies(low, high, at):
        return [
            pltpu.make_async_copy(low.at[0:CUT], top.at[0:CUT], sems.at[8]),
            pltpu.make_async_copy(high.at[CUT - at : packed_rows(1) - at], top.at[CUT:], sems.at[9]),
            pltpu.make_async_copy(low.at[0:TRI], triangle, sems.at[10]),
        ]

    passed = start_one(cases, sources, pass_copies)
    copies = start_one(cases, sources, factor_copies(2, factor, idx, sems))
    finish_factor(2, factor, hots, idx, copies)
    for copy in passed:
        copy.wait()


ONE = 2 * U
PAIR_HOTS = 4 * 3 * U


def pair_rows(place, one, other):
    even = place[1] % 2 == 0
    mine, far = one[NC:], other[NC:]

    def rows(block, at, count):
        block = block.astype(F32)
        return [
            block[at + i : at + i + 1] * 16.0 + block[at + 16 + i : at + 17 + i] for i in range(count)
        ]

    left, right = jnp.where(even, mine, far), jnp.where(even, far, mine)
    return rows(left, 0, LEVELS), rows(right, 0, LEVELS), rows(left, 32, LEVELS - 1)


def stage_pair(place, one, other, hots):
    a, b, up = pair_rows(place, one, other)
    for k in range(4):
        at = k * 3 * U
        hots[:, at : at + 3 * U] = hot(jnp.concatenate([a[k + 1], b[k + 1], up[k]], axis=1))


def half_of(place):
    y = place[1]
    return jnp.where((y == 1) | (y == 2), 1, 0)


def level_one(place, one, recv, terms, rhs, factor, hots, y_keep, passed, keep, send, y_all):
    even = place[1] % 2 == 0
    a, b, _ = pair_rows(place, one, recv)
    hots[...] = hot(jnp.concatenate([a[0], b[0]], axis=1))
    total = dot_t(jnp.concatenate([one[0:NC], recv[0:NC]], axis=1), hots[...])
    resid = (rhs[...].astype(F32) - total).astype(BF)
    y = dot_t(resid, factor[0:PANEL]).astype(BF)
    y_all[:, 0:PANEL] = y
    y_all[:, PANEL:] = jnp.where(even, push_values(factor, y, 4), rhs[...])
    side = half_of(place)
    mine = pl.ds(pl.multiple_of(side * 128, 128), 128)
    theirs = pl.ds(pl.multiple_of((1 - side) * 128, 128), 128)
    send[:, 0:PANEL] = terms[theirs]
    send[:, PANEL:] = y_all[theirs, PANEL:]
    keep[:, 0:PANEL] = terms[mine]
    keep[:, PANEL:] = y_all[mine, PANEL:]
    y_keep[...] = y_all[mine, 0:PANEL]
    passed[2 * PANEL :] = y_all[theirs, 0:PANEL]


def join_pair(place, keep, recv, hots, panel_keep, panel_send, panels):
    ring, even = place[1], place[1] % 2 == 0
    a, b = keep[...], recv[...]
    left, right = jnp.where(even, a, b), jnp.where(even, b, a)
    held = right[:, PANEL:].astype(F32)
    level = jnp.where(ring < 2, 2, place[3])
    for k in range(4):
        at = slice(k * U, (k + 1) * U)
        start = k * 3 * U
        parts = [left[:, at], right[:, at], left[:, PANEL + k * U : PANEL + (k + 1) * U]]
        total = dot_t(jnp.concatenate(parts, axis=1), hots[:, start : start + 3 * U])
        total = total - jnp.where(level == k + 2, held, 0.0)
        panels[:, k * PANEL : (k + 1) * PANEL] = total.astype(BF)
    side = ring // 2
    panel_keep[...] = panels[pl.ds(pl.multiple_of(side * 64, 64), 64)]
    panel_send[...] = panels[pl.ds(pl.multiple_of((1 - side) * 64, 64), 64)]


def level_up(level, mine, recv, factor, hots, y_out, panels):
    slots = LEVELS - level
    total = mine[...].astype(F32) + recv[...].astype(F32)
    y = dot_t((-total[:, 0:PANEL]).astype(BF), factor[0:PANEL]).astype(BF)
    y_out[...] = y
    values = push_values(factor, y, slots)
    for k in range(slots):
        at = slice((k + 1) * PANEL, (k + 2) * PANEL)
        term = dot_t(values[:, k * U : (k + 1) * U], hots[:, k * U : (k + 1) * U])
        panels[:, k * PANEL : (k + 1) * PANEL] = (total[:, at] + term).astype(BF)


def turn(mine, recv, f3, f4, f5, h3, h4, y3, y4, x_out):
    total = mine[...].astype(F32) + recv[...].astype(F32)
    y5 = dot_t((-total).astype(BF), f5[0:PANEL]).astype(BF)
    x5 = solve_back(f5, [], y5, [])
    x4 = solve_back(f4, [h4[...]], y4[...], [x5])
    x3 = solve_back(f3, [h3[:, 0:U], h3[:, U : 2 * U]], y3[...], [x4, x5])
    for k, x in enumerate((x3, x4, x5)):
        x_out[:, k * PANEL : (k + 1) * PANEL] = x


def level_two_back(place, mine, recv, f2, h2, y2, x_out):
    x = jnp.where(place[2] % 2 == 0, mine[...], recv[...])
    above = [x[:, k * PANEL : (k + 1) * PANEL] for k in range(3)]
    x_out[:, 0:PANEL] = solve_back(f2, [h2[:, k * U : (k + 1) * U] for k in range(3)], y2[...], above)
    x_out[:, PANEL:] = x


def level_one_back(place, mine, recv, y_mine, factor, first_hots, hots, x1_out, x, rows_send):
    side = place[1] // 2
    even = place[1] % 2 == 0
    x[pl.ds(pl.multiple_of(side * 64, 64), 64)] = mine[...]
    x[pl.ds(pl.multiple_of((1 - side) * 64, 64), 64)] = recv[...]
    above = [x[:, k * PANEL : (k + 1) * PANEL] for k in range(4)]
    ups = [hots[:, k * 3 * U + 2 * U : (k + 1) * 3 * U] for k in range(4)]
    x1 = solve_back(factor, ups, jnp.where(even, y_mine[...], factor[2 * PANEL :]), above)
    x1_out[...] = x1
    for l, value in enumerate([x1] + above):
        pair = first_hots[...] if l == 0 else hots[:, (l - 1) * 3 * U : (l - 1) * 3 * U + 2 * U]
        pair = jnp.where(even, pair[:, U:], pair[:, 0:U])
        rows_send[:, l * U : (l + 1) * U] = dot(value, pair).astype(BF)


def level_one_rest(place, x1_ref, x, first_hots, hots, rows_keep, sep_keep, sep_send, sep_a, sep_b, sems):
    even = place[1] % 2 == 0
    x1 = x1_ref[...]
    above = [x[:, k * PANEL : (k + 1) * PANEL] for k in range(4)]
    level = jnp.where(place[1] < 2, 2, place[3])
    held = jnp.where(level == 0, jnp.zeros_like(x1), above[0])
    for k in (1, 2, 3):
        held = jnp.where(level == k + 2, above[k], held)
    sep_a[...] = jnp.where(even, x1, held)
    sep_b[...] = jnp.where(even, held, x1)
    stores = [
        pltpu.make_async_copy(sep_a, sep_keep, sems.at[0]),
        pltpu.make_async_copy(sep_b, sep_send, sems.at[1]),
    ]
    for store in stores:
        store.start()
    for l, value in enumerate([x1] + above):
        pair = first_hots[...] if l == 0 else hots[:, (l - 1) * 3 * U : (l - 1) * 3 * U + 2 * U]
        pair = jnp.where(even, pair[:, 0:U], pair[:, U:])
        rows_keep[:, l * U : (l + 1) * U] = dot(value, pair).astype(BF)
    for store in stores:
        store.wait()


def leaf_half(rows, inv, cpl, yt):
    back = (yt.astype(F32) - dot(rows[...], cpl[...].reshape(TERM, LEAF))).astype(BF)
    parts = []
    for i in range(4):
        start = i * 256
        parts.append(dot(back[:, start:], inv[start:, start : start + 256]).astype(BF))
    return jnp.concatenate(parts, axis=1)


def leaf_mine(place, keep, inv, cpl, yt, chosen, xt_out, picks_out):
    side = half_of(place)
    xt = leaf_half(keep, inv, cpl, yt[pl.ds(pl.multiple_of(side * 128, 128), 128)])
    xt_out[...] = xt
    picks_out[...] = dot_t(chosen[...], xt).astype(BF)


def leaf_other(place, recv, inv, cpl, yt, chosen, xt_mine, picks_mine, xt_out, picks_out, xt, picks, sems):
    side = half_of(place)
    mine = pl.ds(pl.multiple_of(side * 128, 128), 128)
    other = pl.ds(pl.multiple_of((1 - side) * 128, 128), 128)
    xt[mine] = xt_mine[...]
    picks[:, mine] = picks_mine[...]
    far = leaf_half(recv, inv, cpl, yt[other])
    xt[other] = far
    stores = [pltpu.make_async_copy(xt, xt_out, sems.at[0])]
    stores[0].start()
    for i in range(2):
        part = slice(i * 16 * SLOTS, (i + 1) * 16 * SLOTS)
        picks[part, other] = dot_t(chosen[part], far).astype(BF)
        stores.append(pltpu.make_async_copy(picks.at[part], picks_out.at[part], sems.at[1 + i]))
        stores[-1].start()
    for store in stores:
        store.wait()


def turn_leaf(xt, x_leaf, xt_v, sems):
    load = pltpu.make_async_copy(xt, xt_v, sems.at[0])
    load.start()
    load.wait()
    for i in range(4):
        part = slice(i * 256, (i + 1) * 256)
        x_leaf[part] = xt_v[:, part].astype(F32).T.astype(BF)


def turn_sep(place, keep, recv, x_sep, keep_v, recv_v, both, sems):
    loads = [
        pltpu.make_async_copy(keep, keep_v, sems.at[0]),
        pltpu.make_async_copy(recv, recv_v, sems.at[1]),
    ]
    for load in loads:
        load.start()
    for load in loads:
        load.wait()
    side = half_of(place)
    both[pl.ds(pl.multiple_of(side * 128, 128), 128)] = keep_v[...].astype(F32)
    both[pl.ds(pl.multiple_of((1 - side) * 128, 128), 128)] = recv_v[...].astype(F32)
    x_sep[...] = both[...].T.astype(BF)


def stretch_sum(weight, got, out, weight_v, sems):
    load = pltpu.make_async_copy(weight, weight_v, sems.at[0])
    load.start()
    load.wait()
    out[...] = dot(weight_v[0], got[...]) + dot(weight_v[1], got[...])


def iota(rows, cols, axis):
    return lax.broadcasted_iota(jnp.int32, (rows, cols), axis)


def ones_where(mask):
    return jnp.where(mask, 1.0, 0.0)


def stay_plan(place, dofs, coef, chosen, weight_out, grid, turned, dof_t, coef_t, weight, sems):
    me = place[2] * RING + place[1]
    grid[...] = jnp.full((128, 128), -1, jnp.int32)
    for r in range(16):
        grid[8 * r : 8 * r + 6] = dofs[:, 128 * r : 128 * (r + 1)]
    dof = grid[...]
    match = ones_where((dof >> 10) == me)
    row, col = iota(128, 128, 0), iota(128, 128, 1)
    same = (row >> 3) == (col >> 3)
    earlier = ((row >> 6) == (col >> 6)) & (row < col)
    match_b = match.astype(BF)
    count = dot(ones_where(same).astype(BF), match_b).astype(BF)
    rank = dot(count, ones_where(earlier).astype(BF))
    rank = rank + dot(ones_where(same & (col < row)).astype(BF), match_b)
    high = ((dof >> 5) & 31).astype(F32) + 1.0
    low = (dof & 31).astype(F32)
    rank = jnp.where(match > 0.0, rank, -1.0)
    parts = []
    for value in (high, low):
        for s in range(SLOTS):
            parts.append(jnp.where(rank == float(s), value, 0.0).astype(BF))
    block = ones_where(iota(16, 128, 0) == (iota(16, 128, 1) >> 3)).astype(BF)
    flat = dot(block, jnp.concatenate(parts, axis=1)).astype(BF)
    width = SLOTS * 128
    lane, q = iota(width, 32, 0), iota(width, 32, 1)
    gather = ones_where(q == ((lane >> 6) & 1) * SLOTS + (lane >> 7)).astype(BF)
    table_high = dot(flat[:, 0:width], gather).astype(BF)
    table_low = dot(flat[:, width:], gather).astype(BF)
    spread = ones_where((iota(512, 16, 0) >> 5) == iota(512, 16, 1)).astype(BF)
    here = ones_where((iota(512, 32, 0) & 31) == iota(512, 32, 1))
    sel_high = jnp.sum(dot(spread, table_high) * here, axis=1, keepdims=True)
    sel_low = jnp.sum(dot(spread, table_low) * here, axis=1, keepdims=True)
    sel = (sel_high - 1.0) * 32.0 + sel_low
    for part in range(4):
        at = slice(part * 128, (part + 1) * 128)
        chosen[at] = ones_where(iota(128, LEAF, 1).astype(F32) == sel[at]).astype(BF)

    block_row = pl.multiple_of((me >> 1) * 8, 8)
    block_col = pl.multiple_of((me >> 1) * 128, 128)
    half = pl.ds(pl.multiple_of((me & 1) * 64, 64), 64)
    turned[...] = jnp.zeros_like(turned)
    turned[0:8] = grid[pl.ds(block_row, 8)].astype(F32)
    dof_t[...] = turned[...].T
    turned[0:6] = coef[:, pl.ds(block_col, 128)]
    coef_t[...] = turned[...].T
    my_dof, my_coef = dof_t[half], coef_t[half]
    lanes = iota(64, 32, 1)
    source = [my_dof[:, k : k + 1].astype(jnp.int32) >> 10 for k in range(6)]
    named = [ones_where(source[k] == lanes) for k in range(6)]
    every = named[0]
    for k in range(1, 6):
        every = every + named[k]
    lower = ones_where(iota(64, 64, 1) < iota(64, 64, 0)).astype(BF)
    running = dot(lower, every.astype(BF))
    total = jnp.zeros((64, 512), F32)
    slots = iota(64, 512, 1).astype(F32)
    for k in range(6):
        at = jnp.sum(named[k] * running, axis=1, keepdims=True)
        slot = source[k].astype(F32) * float(SLOTS) + at
        total = total + jnp.where(slots == slot, my_coef[:, k : k + 1], 0.0)
        running = running + named[k]
    first = total.astype(BF)
    weight[0] = first
    weight[1] = (total - first.astype(F32)).astype(BF)
    store = pltpu.make_async_copy(weight, weight_out, sems.at[0])
    store.start()
    store.wait()


def after(value, *others):
    return lax.optimization_barrier((value, *others))[0]


def on_device(
    rhs_leaf, rhs_sep, leaf_inv, leaf_cpl, leaf_idx, sep_inv, sep_cpl, sep_idx, stay_dofs, stay_coef
):
    rows_axis, cols_axis = "rows", "cols"
    columns, rows = lax.axis_size(cols_axis), lax.axis_size(rows_axis)
    me = lax.axis_index(rows_axis)
    core = lax.axis_index(cols_axis) % 2
    y, z = me % RING, me // RING
    top_level = jnp.where(z % 2 == 0, 3, jnp.where(z % 4 == 1, 4, jnp.where(z == 3, 5, 0)))
    place = jnp.stack([core, y, z, top_level]).astype(jnp.int32)

    def route(value, target):
        pairs = []
        for c in range(columns):
            for r in range(rows):
                to = target(c % 2, r % RING, r // RING)
                if to is not None:
                    pairs.append((c * rows + r, (c - c % 2 + to[0]) * rows + to[2] * RING + to[1]))
        return lax.ppermute(value, (cols_axis, rows_axis), pairs)

    def swap_core(value):
        return route(value, lambda c, y, z: (1 - c, y, z))

    def swap(value, flip):
        return route(value, lambda c, y, z: (c, y ^ flip, z))

    def to_odd(value):
        return route(value, lambda c, y, z: (c, y + 1, z) if y % 2 == 0 else None)

    sep_rows_flat = sep_cpl.reshape(4 * U, PANEL)
    own_up, window = call(
        pack_factor,
        [pinned(packed_rows(3), PANEL), pinned(WINDOW, PANEL)],
        [place, sep_inv, sep_rows_flat, sep_idx],
        [SMEM, HBM, HBM, HBM],
        [pltpu.VMEM((16, PANEL), F32), pltpu.VMEM((LEVELS - 1, U), jnp.int32), dma(7)],
    )
    with jax.named_scope("factors_to_pair"):
        pair = route(window, lambda c, y, z: (c, y ^ 1, z) if y % 2 else None)
    with jax.named_scope("factors_to_other"):
        beside = route(window, lambda c, y, z: (c, y ^ 3, z) if y % 2 else None)
    yt, rhs, one, inv_v, cpl_v = call(
        leaf_first,
        [
            pinned(NC, LEAF),
            pinned(NC, PANEL),
            pinned(NC + 4 * 16, U),
            pinned(LEAF, LEAF),
            pinned(LEVELS, U, LEAF),
        ],
        [after(place, own_up), leaf_inv, rhs_leaf, leaf_cpl, rhs_sep, leaf_idx.transpose(1, 0, 2), sep_idx],
        [SMEM] + [HBM] * 6,
        [
            pltpu.VMEM((LEAF, NC), BF),
            pltpu.VMEM((PANEL, NC), BF),
            pltpu.VMEM((LEVELS, 1, U), jnp.int32),
            pltpu.VMEM((LEVELS - 1, U), jnp.int32),
            pltpu.VMEM((64, U), F32),
            dma(9),
        ],
    )
    with jax.named_scope("first_terms"):
        recv = swap(one, 1)
    (terms,) = call(
        leaf_second, [pinned(NC, PANEL)], [yt, cpl_v], [VMEM, VMEM]
    )

    def ready(slots, pick, sources):
        return call(
            functools.partial(stage, slots, pick, len(sources)),
            [pinned(factor_rows(slots), PANEL), pinned(PANEL, max(slots, 1) * U)],
            [place, *sources],
            [SMEM] + [ANY] * len(sources),
            [pltpu.VMEM((16, PANEL), BF), dma(8)],
        )

    def rise(level, panel, recv, factor, hots):
        slots = LEVELS - level
        return call(
            functools.partial(level_up, level),
            [pinned(64, PANEL), pinned(64, slots * PANEL)],
            [panel, recv, factor, hots],
            [VMEM] * 4,
        )

    (f1,) = call(
        load_first,
        [pinned(2 * PANEL + 128, PANEL)],
        [after(sep_inv, one), sep_rows_flat],
        [HBM, HBM],
        [dma(2)],
    )
    pair = after(pair, recv, f1, terms)
    with jax.named_scope("factors_across"):
        far = route(pair, lambda c, y, z: (c, y ^ 3, z) if y % 2 == 0 else None)
    first = after(recv, f1)
    first_hots, y1, passed, keep, send = call(
        level_one,
        [
            pinned(PANEL, ONE),
            pinned(128, PANEL),
            pinned(2 * PANEL + 128, PANEL),
            pinned(128, 2 * PANEL),
            pinned(128, 2 * PANEL),
        ],
        [place, one, first, terms, rhs, f1],
        [SMEM] + [VMEM] * 5,
        [pltpu.VMEM((NC, 2 * PANEL), BF)],
        aliases={5: 2},
    )
    with jax.named_scope("terms_pair"):
        recv = swap(send, 1)
    pair, beside = after((pair, beside), send)
    with jax.named_scope("pair_to_core"):
        pair_o = swap_core(pair)
    with jax.named_scope("beside_to_core"):
        beside_o = swap_core(beside)
    chosen, weight = call(
        stay_plan,
        [pinned(32 * SLOTS, LEAF), stored(2, 64, 512)],
        [place, stay_dofs, after(stay_coef, send)],
        [SMEM, VMEM, VMEM],
        [
            pltpu.VMEM((128, 128), jnp.int32),
            pltpu.VMEM((128, 128), F32),
            pltpu.VMEM((128, 128), F32),
            pltpu.VMEM((128, 128), F32),
            pltpu.VMEM((2, 64, 512), BF),
            dma(1),
        ],
        [VMEM, HBM],
    )
    (h1,) = call(
        stage_pair, [pinned(PANEL, PAIR_HOTS)], [place, one, after(first, send)], [SMEM, VMEM, VMEM]
    )
    recv = after(recv, chosen, h1)
    panel, send = call(
        join_pair,
        [pinned(64, 4 * PANEL), pinned(64, 4 * PANEL)],
        [place, keep, recv, h1],
        [SMEM] + [VMEM] * 3,
        [pltpu.VMEM((128, 4 * PANEL), BF)],
    )
    with jax.named_scope("panels_ring"):
        recv = swap(send, 3)
    far = after(far, send)
    with jax.named_scope("far_to_core"):
        far_o = swap_core(far)
    at = [own_up, pair, pair_o, beside, beside_o, far, far_o]
    f2, h2 = call(
        stage_two,
        [pinned(factor_rows(3), PANEL), pinned(PANEL, 3 * U)],
        [place, *at],
        [SMEM] + [ANY] * 7,
        [pltpu.VMEM((16, PANEL), BF), dma(8)],
    )
    f3, h3, top, triangle = call(
        stage_and_pass,
        [
            pinned(factor_rows(2), PANEL),
            pinned(PANEL, 2 * U),
            pinned(packed_rows(1), PANEL),
            pinned(TRI, PANEL),
        ],
        [place, *at],
        [SMEM] + [ANY] * 7,
        [pltpu.VMEM((16, PANEL), BF), dma(11)],
    )

    def next_up(value, senders):
        return route(value, lambda c, y, z: (c, y, z + (1 if c else -1)) if z in senders else None)

    with jax.named_scope("factors_up"):
        up = next_up(top, (1, 3, 5))
    with jax.named_scope("factor_top"):
        last = route(
            triangle,
            lambda c, y, z: (c, y, 0 if c else 6) if z == 3 else None,
        )
    with jax.named_scope("first_factor_to_odd"):
        passed_far = to_odd(after(passed, f2))
    recv = after(recv, f2, h2, f3, h3)
    y2, panel = rise(2, panel, recv, f2, h2)
    with jax.named_scope("panels_z1"):
        recv = route(panel, lambda c, y, z: (c, y, z - 1) if z % 2 else None)
    y3, panel = rise(3, panel, recv, f3, h3)
    with jax.named_scope("panels_z2"):
        recv = route(panel, lambda c, y, z: (c, y, z ^ 2))
    up, last = after((up, last), panel)
    with jax.named_scope("up_to_core"):
        up_o = swap_core(up)
    with jax.named_scope("last_to_core"):
        last_o = swap_core(last)
    f4, h4 = ready(1, pick_four, [up, up_o])
    f5, _ = ready(0, pick_five, [up, up_o, last, last_o])
    recv = after(recv, f4, h4, f5)
    y4, panel = rise(4, panel, recv, f4, h4)
    with jax.named_scope("panels_z3"):
        recv = route(panel, lambda c, y, z: (c, y, 8 - z if z % 2 else 6 - z))
    (x,) = call(
        turn,
        [pinned(64, 3 * PANEL)],
        [panel, recv, f3, f4, f5, h3, h4, y3, y4],
        [VMEM] * 9,
    )
    with jax.named_scope("down_z1"):
        recv = route(x, lambda c, y, z: (c, y, z ^ 1))
    (x,) = call(
        level_two_back,
        [pinned(64, 4 * PANEL)],
        [place, x, recv, f2, h2, y2],
        [SMEM] + [VMEM] * 5,
    )
    with jax.named_scope("down_ring"):
        recv = swap(x, 3)
    passed_far = after(passed_far, x)
    (f1,) = call(
        pick_first,
        [pinned(2 * PANEL + 128, PANEL)],
        [place, passed, passed_far],
        [SMEM, ANY, ANY],
        [dma(1)],
    )
    recv = after(recv, f1)
    x1, x, rows_send = call(
        level_one_back,
        [pinned(128, PANEL), pinned(128, 4 * PANEL), pinned(128, TERM)],
        [place, x, recv, y1, f1, first_hots, h1],
        [SMEM] + [VMEM] * 6,
    )
    with jax.named_scope("rows_back"):
        recv = swap(rows_send, 1)
    rows_keep, sep_keep, sep_send = call(
        level_one_rest,
        [pinned(128, TERM), stored(128, PANEL), stored(128, PANEL)],
        [place, x1, x, first_hots, h1],
        [SMEM] + [VMEM] * 4,
        [pltpu.VMEM((128, PANEL), BF), pltpu.VMEM((128, PANEL), BF), dma(2)],
        [VMEM, HBM, HBM],
    )
    xt_mine, picks_mine = call(
        leaf_mine,
        [pinned(128, LEAF), pinned(32 * SLOTS, 128)],
        [place, rows_keep, inv_v, cpl_v, yt, chosen],
        [SMEM] + [VMEM] * 5,
    )
    recv = after(recv, xt_mine)
    xt, picks = call(
        leaf_other,
        [stored(NC, LEAF), stored(32 * SLOTS, NC)],
        [place, recv, inv_v, cpl_v, yt, chosen, xt_mine, picks_mine],
        [SMEM] + [VMEM] * 7,
        [pltpu.VMEM((NC, LEAF), BF), pltpu.VMEM((32 * SLOTS, NC), BF), dma(3)],
        [HBM, HBM],
        moved=14 * 10**6,
    )
    with jax.named_scope("sep_back"):
        sep_recv = swap(after(sep_send, picks), 1)
    got = lax.all_to_all(
        picks.reshape(32, SLOTS, NC), rows_axis, 0, 0, tiled=True
    ).reshape(32 * SLOTS, NC)
    (x_leaf,) = call(
        turn_leaf, [plain(LEAF, NC)], [xt], [HBM], [pltpu.VMEM((NC, LEAF), BF), dma(1)]
    )
    (x_sep,) = call(
        turn_sep,
        [plain(PANEL, NC)],
        [place, sep_keep, sep_recv],
        [SMEM, HBM, HBM],
        [
            pltpu.VMEM((128, PANEL), BF),
            pltpu.VMEM((128, PANEL), BF),
            pltpu.VMEM((NC, PANEL), F32),
            dma(2),
        ],
    )
    (stretch,) = call(
        stretch_sum,
        [plain(64, NC, dtype=F32)],
        [weight, got],
        [HBM, VMEM],
        [pltpu.VMEM((2, 64, 512), BF), dma(1)],
    )
    return (x_leaf, x_sep, stretch)


def solution(mesh):
    return jax.shard_map(
        on_device,
        mesh=mesh,
        in_specs=(
            P("rows", "cols"),
            P("rows", "cols"),
            P("rows", None),
            P("rows", None, None, None),
            P("rows", None, None),
            P("rows", None),
            P("rows", None, None, None),
            P("rows", None, None),
            P(),
            P(),
        ),
        out_specs=(P("rows", "cols"), P("rows", "cols"), P("rows", "cols")),
        check_vma=False,
    )
```

```python
import functools

import jax
import jax.numpy as jnp
from jax import lax
from jax.experimental import pallas as pl
from jax.experimental.pallas import tpu as pltpu
from jax.sharding import PartitionSpec as P

BF = jnp.bfloat16
F32 = jnp.float32
LEAF, PANEL, U, NC, LEVELS = 1024, 512, 128, 256, 5
RING, DEPTH = 4, 8
TERM = LEVELS * U
SLOTS = 16
VMEM_LIMIT = 16 * 1024 * 1024

TRI = 320
IDX = slice(TRI, TRI + 16)
CUT, WINDOW = 352, 368
CPL0 = TRI + 16


def packed_rows(slots):
    return CPL0 + slots * U


def factor_rows(slots):
    return PANEL + slots * U


def triangle_blocks():
    return [
        (slice(384, 512), slice(0, 512), slice(0, 128), slice(0, 512)),
        (slice(256, 384), slice(0, 384), slice(128, 256), slice(0, 384)),
        (slice(0, 128), slice(0, 128), slice(128, 256), slice(384, 512)),
        (slice(128, 192), slice(0, 256), slice(256, 320), slice(0, 256)),
        (slice(192, 256), slice(0, 256), slice(256, 320), slice(256, 512)),
    ]


def dot(left, right):
    return jnp.dot(left, right, preferred_element_type=F32)


def dot_t(left, right):
    return lax.dot_general(left, right, (((1,), (1,)), ((), ())), preferred_element_type=F32)


VMEM = pl.BlockSpec(memory_space=pltpu.VMEM)
SMEM = pl.BlockSpec(memory_space=pltpu.SMEM)
HBM = pl.BlockSpec(memory_space=pltpu.HBM)
ANY = pl.BlockSpec(memory_space=pl.ANY)


def call(body, outs, args, specs, scratch=(), out_specs=None, aliases=None, flops=10**8, moved=10**6):
    args = [
        in_vmem(arg) if spec is VMEM else in_hbm(arg) if spec is HBM else arg
        for arg, spec in zip(args, specs)
    ]
    return pl.pallas_call(
        body,
        out_shape=outs,
        in_specs=specs,
        out_specs=out_specs or [VMEM] * len(outs),
        scratch_shapes=list(scratch),
        input_output_aliases=aliases or {},
        compiler_params=pltpu.CompilerParams(vmem_limit_bytes=VMEM_LIMIT),
        cost_estimate=pl.CostEstimate(flops=flops, bytes_accessed=moved, transcendentals=0),
    )(*args)


def dma(n):
    return pltpu.SemaphoreType.DMA((n,))


def pinned(*dims, dtype=BF):
    return pltpu.VMEM(dims, dtype)


def plain(*dims, dtype=BF):
    return jax.ShapeDtypeStruct(dims, dtype)


def stored(*dims, dtype=BF):
    return pltpu.HBM(dims, dtype)


def in_vmem(value):
    return pltpu.with_memory_space_constraint(value, pltpu.VMEM)


def in_hbm(value):
    return pltpu.with_memory_space_constraint(value, pltpu.HBM)


def hot(rows):
    place = lax.broadcasted_iota(jnp.int32, (PANEL, rows.shape[1]), 0).astype(F32)
    return jnp.where(place == rows, 1.0, 0.0).astype(BF)


def sep_rows(block):
    block = block.astype(F32)
    return [block[s : s + 1, 0:U] * 16.0 + block[s : s + 1, U : 2 * U] for s in range(LEVELS - 1)]


def push_values(factor, y, slots):
    return dot_t(y, factor[PANEL : PANEL + slots * U]).astype(BF)


def solve_back(factor, hots, y, above):
    back = y
    slots = len(above)
    if slots:
        taken = [dot(above[k], hots[k]).astype(BF) for k in range(slots)]
        taken = taken[0] if slots == 1 else jnp.concatenate(taken, axis=1)
        sub = dot(taken, factor[PANEL : PANEL + slots * U])
        back = (y.astype(F32) - sub).astype(BF)
    return dot(back, factor[0:PANEL]).astype(BF)


def pack_factor(place, inv, cpl, sep_idx, up, window, codes, sep_v, sems):
    load = pltpu.make_async_copy(sep_idx.at[0], sep_v, sems.at[0])
    copies = [
        pltpu.make_async_copy(inv.at[r, c], up.at[pr, pc], sems.at[1 + i])
        for i, (r, c, pr, pc) in enumerate(triangle_blocks())
    ]
    copies.append(pltpu.make_async_copy(cpl.at[0 : 3 * U], up.at[CPL0 : packed_rows(3)], sems.at[6]))
    load.start()
    for copy in copies:
        copy.start()
    codes[...] = jnp.zeros_like(codes)
    load.wait()
    value = sep_v[...]
    codes[0 : LEVELS - 1, 0:U] = (value >> 4).astype(F32)
    codes[0 : LEVELS - 1, U : 2 * U] = (value & 15).astype(F32)
    up[IDX] = codes[...].astype(BF)
    for copy in copies:
        copy.wait()
    window[...] = up[pl.ds(pl.multiple_of(place[0] * CUT, 16), WINDOW)]


def load_first(inv, cpl, out, sems):
    copies = [
        pltpu.make_async_copy(inv, out.at[0:PANEL], sems.at[0]),
        pltpu.make_async_copy(cpl, out.at[PANEL : 2 * PANEL], sems.at[1]),
    ]
    for copy in copies:
        copy.start()
    out[2 * PANEL :] = jnp.zeros((128, PANEL), BF)
    for copy in copies:
        copy.wait()


def pick_first(place, own, far, factor, sems):
    even = place[1] % 2 == 0
    copies = [
        pltpu.make_async_copy(source, factor, sems.at[0]) for source in (own, far)
    ]

    @pl.when(even)
    def _():
        copies[0].start()

    @pl.when(jnp.logical_not(even))
    def _():
        copies[1].start()

    copies[0].wait()


def leaf_first(
    place, inv, rhs, cpl, rsep, leaf_idx, sep_idx, yt, rhs_out, one, inv_v, cpl_v,
    rhs_v, rsep_v, leaf_v, sep_v, codes, sems
):
    loads = [
        pltpu.make_async_copy(leaf_idx, leaf_v, sems.at[0]),
        pltpu.make_async_copy(sep_idx.at[0], sep_v, sems.at[1]),
        pltpu.make_async_copy(rhs, rhs_v, sems.at[2]),
    ]
    for i in range(4):
        rows = pl.ds(i * 256, 256)
        loads.append(pltpu.make_async_copy(inv.at[rows], inv_v.at[rows], sems.at[3 + i]))
    loads.append(pltpu.make_async_copy(cpl.at[0], cpl_v, sems.at[7]))
    loads.append(pltpu.make_async_copy(rsep, rsep_v, sems.at[8]))
    for load in loads:
        load.start()
    codes[...] = jnp.zeros_like(codes)
    loads[0].wait()
    for l in range(LEVELS):
        value = leaf_v[l]
        codes[l : l + 1] = (value >> 4).astype(F32)
        codes[16 + l : 17 + l] = (value & 15).astype(F32)
    loads[1].wait()
    value = sep_v[...]
    codes[32 : 32 + LEVELS - 1] = (value >> 4).astype(F32)
    codes[48 : 48 + LEVELS - 1] = (value & 15).astype(F32)
    one[NC:] = codes[...].astype(BF)
    loads[2].wait()
    rhs_t = rhs_v[...].astype(F32).T.astype(BF)
    for i in range(4):
        loads[3 + i].wait()
        span = (i + 1) * 256
        yt[:, i * 256 : span] = dot_t(rhs_t[:, 0:span], inv_v[i * 256 : span, 0:span]).astype(BF)
    loads[7].wait()
    one[0:NC] = dot_t(yt[...], cpl_v[0]).astype(BF)
    loads[8].wait()
    rhs_out[...] = rsep_v[...].astype(F32).T.astype(BF)


def leaf_second(yt, cpl_v, terms):
    terms[...] = dot_t(yt[...], cpl_v[1:].reshape(PANEL, LEAF)).astype(BF)


def which(place):
    return place[0], place[1], place[2]


def pick_two(core, y, z):
    return y == 1, y == 0, y == 2, y == 3


def pick_top(core, y, z):
    return y == 3, y == 2, y == 0, y == 1


def pick_four(core, y, z):
    after_me = (z == 0) | (z == 4)
    first = core == 0
    return (after_me & first) | (~after_me & ~first), (after_me & ~first) | (~after_me & first)


def pick_five(core, y, z):
    inner = (z == 2) | (z == 4)
    first = core == 0
    low = (z == 2) | (z == 0)
    same = (low & first) | (~low & ~first)
    return inner & same, inner & ~same, ~inner & ~same, ~inner & same


def pick_one(core, y, z):
    even = (y == 0) | (y == 2)
    return even, ~even


def window_sources(core, refs):
    own = refs[0]
    sources = [[(None, own, own, 0)]]
    for i in range(1, len(refs), 2):
        mine, other = refs[i], refs[i + 1]
        sources.append([(core == 0, mine, other, CUT), (core != 0, other, mine, CUT)])
    return sources


def start_one(cases, sources, copies_of):
    for case, versions in zip(cases, sources):
        for on_core, low, high, at in versions:

            @pl.when(case if on_core is None else case & on_core)
            def _(low=low, high=high, at=at):
                for copy in copies_of(low, high, at):
                    copy.start()

    return copies_of(*sources[0][0][1:])


def factor_copies(slots, factor, idx, sems):
    def copies_of(low, high, at):
        copies = [
            pltpu.make_async_copy(low.at[pr, pc], factor.at[r, c], sems.at[i])
            for i, (r, c, pr, pc) in enumerate(triangle_blocks())
        ]
        if slots:
            split = CUT - CPL0
            copies.append(
                pltpu.make_async_copy(low.at[CPL0:CUT], factor.at[PANEL : PANEL + split], sems.at[5])
            )
            copies.append(
                pltpu.make_async_copy(
                    high.at[CUT - at : packed_rows(slots) - at], factor.at[PANEL + split :], sems.at[6]
                )
            )
            copies.append(pltpu.make_async_copy(low.at[IDX], idx, sems.at[7]))
        return copies

    return copies_of


def finish_factor(slots, factor, hots, idx, copies):
    for rows, cols in (
        (slice(0, 128), slice(128, 512)),
        (slice(128, 256), slice(256, 512)),
        (slice(256, 384), slice(384, 512)),
    ):
        factor[rows, cols] = jnp.zeros((rows.stop - rows.start, cols.stop - cols.start), BF)
    if slots:
        copies[-1].wait()
        taken = sep_rows(idx[...])
        for k in range(slots):
            hots[:, k * U : (k + 1) * U] = hot(taken[k])
        copies = copies[:-1]
    else:
        hots[...] = jnp.zeros_like(hots)
    for copy in copies:
        copy.wait()


def stage(slots, pick, count, place, *refs):
    factor, hots, idx, sems = refs[count:]
    sources = [[(None, ref, ref, 0)] for ref in refs[:count]]
    copies = start_one(pick(*which(place)), sources, factor_copies(slots, factor, idx, sems))
    finish_factor(slots, factor, hots, idx, copies)


def stage_two(place, *refs):
    factor, hots, idx, sems = refs[7:]
    sources = window_sources(place[0], refs[:7])
    copies = start_one(pick_two(*which(place)), sources, factor_copies(3, factor, idx, sems))
    finish_factor(3, factor, hots, idx, copies)


def stage_and_pass(place, *refs):
    factor, hots, top, triangle, idx, sems = refs[7:]
    sources = window_sources(place[0], refs[:7])
    cases = pick_top(*which(place))

    def pass_copies(low, high, at):
        return [
            pltpu.make_async_copy(low.at[0:CUT], top.at[0:CUT], sems.at[8]),
            pltpu.make_async_copy(high.at[CUT - at : packed_rows(1) - at], top.at[CUT:], sems.at[9]),
            pltpu.make_async_copy(low.at[0:TRI], triangle, sems.at[10]),
        ]

    passed = start_one(cases, sources, pass_copies)
    copies = start_one(cases, sources, factor_copies(2, factor, idx, sems))
    finish_factor(2, factor, hots, idx, copies)
    for copy in passed:
        copy.wait()


ONE = 2 * U
PAIR_HOTS = 4 * 3 * U


def pair_rows(place, one, other):
    even = place[1] % 2 == 0
    mine, far = one[NC:], other[NC:]

    def rows(block, at, count):
        block = block.astype(F32)
        return [
            block[at + i : at + i + 1] * 16.0 + block[at + 16 + i : at + 17 + i] for i in range(count)
        ]

    left, right = jnp.where(even, mine, far), jnp.where(even, far, mine)
    return rows(left, 0, LEVELS), rows(right, 0, LEVELS), rows(left, 32, LEVELS - 1)


def stage_pair(place, one, other, hots):
    a, b, up = pair_rows(place, one, other)
    for k in range(4):
        at = k * 3 * U
        hots[:, at : at + 3 * U] = hot(jnp.concatenate([a[k + 1], b[k + 1], up[k]], axis=1))


def half_of(place):
    y = place[1]
    return jnp.where((y == 1) | (y == 2), 1, 0)


def level_one(place, one, recv, terms, rhs, factor, hots, y_keep, passed, keep, send, y_all):
    even = place[1] % 2 == 0
    a, b, _ = pair_rows(place, one, recv)
    hots[...] = hot(jnp.concatenate([a[0], b[0]], axis=1))
    total = dot_t(jnp.concatenate([one[0:NC], recv[0:NC]], axis=1), hots[...])
    resid = (rhs[...].astype(F32) - total).astype(BF)
    y = dot_t(resid, factor[0:PANEL]).astype(BF)
    y_all[:, 0:PANEL] = y
    y_all[:, PANEL:] = jnp.where(even, push_values(factor, y, 4), rhs[...])
    side = half_of(place)
    mine = pl.ds(pl.multiple_of(side * 128, 128), 128)
    theirs = pl.ds(pl.multiple_of((1 - side) * 128, 128), 128)
    send[:, 0:PANEL] = terms[theirs]
    send[:, PANEL:] = y_all[theirs, PANEL:]
    keep[:, 0:PANEL] = terms[mine]
    keep[:, PANEL:] = y_all[mine, PANEL:]
    y_keep[...] = y_all[mine, 0:PANEL]
    passed[2 * PANEL :] = y_all[theirs, 0:PANEL]


def join_pair(place, keep, recv, hots, panel_keep, panel_send, panels):
    ring, even = place[1], place[1] % 2 == 0
    a, b = keep[...], recv[...]
    left, right = jnp.where(even, a, b), jnp.where(even, b, a)
    held = right[:, PANEL:].astype(F32)
    level = jnp.where(ring < 2, 2, place[3])
    for k in range(4):
        at = slice(k * U, (k + 1) * U)
        start = k * 3 * U
        parts = [left[:, at], right[:, at], left[:, PANEL + k * U : PANEL + (k + 1) * U]]
        total = dot_t(jnp.concatenate(parts, axis=1), hots[:, start : start + 3 * U])
        total = total - jnp.where(level == k + 2, held, 0.0)
        panels[:, k * PANEL : (k + 1) * PANEL] = total.astype(BF)
    side = ring // 2
    panel_keep[...] = panels[pl.ds(pl.multiple_of(side * 64, 64), 64)]
    panel_send[...] = panels[pl.ds(pl.multiple_of((1 - side) * 64, 64), 64)]


def level_up(level, mine, recv, factor, hots, y_out, panels):
    slots = LEVELS - level
    total = mine[...].astype(F32) + recv[...].astype(F32)
    y = dot_t((-total[:, 0:PANEL]).astype(BF), factor[0:PANEL]).astype(BF)
    y_out[...] = y
    values = push_values(factor, y, slots)
    for k in range(slots):
        at = slice((k + 1) * PANEL, (k + 2) * PANEL)
        term = dot_t(values[:, k * U : (k + 1) * U], hots[:, k * U : (k + 1) * U])
        panels[:, k * PANEL : (k + 1) * PANEL] = (total[:, at] + term).astype(BF)


def turn(mine, recv, f3, f4, f5, h3, h4, y3, y4, x_out):
    total = mine[...].astype(F32) + recv[...].astype(F32)
    y5 = dot_t((-total).astype(BF), f5[0:PANEL]).astype(BF)
    x5 = solve_back(f5, [], y5, [])
    x4 = solve_back(f4, [h4[...]], y4[...], [x5])
    x3 = solve_back(f3, [h3[:, 0:U], h3[:, U : 2 * U]], y3[...], [x4, x5])
    for k, x in enumerate((x3, x4, x5)):
        x_out[:, k * PANEL : (k + 1) * PANEL] = x


def level_two_back(place, mine, recv, f2, h2, y2, x_out):
    x = jnp.where(place[2] % 2 == 0, mine[...], recv[...])
    above = [x[:, k * PANEL : (k + 1) * PANEL] for k in range(3)]
    x_out[:, 0:PANEL] = solve_back(f2, [h2[:, k * U : (k + 1) * U] for k in range(3)], y2[...], above)
    x_out[:, PANEL:] = x


def level_one_back(place, mine, recv, y_mine, factor, first_hots, hots, x1_out, x, rows_send):
    side = place[1] // 2
    even = place[1] % 2 == 0
    x[pl.ds(pl.multiple_of(side * 64, 64), 64)] = mine[...]
    x[pl.ds(pl.multiple_of((1 - side) * 64, 64), 64)] = recv[...]
    above = [x[:, k * PANEL : (k + 1) * PANEL] for k in range(4)]
    ups = [hots[:, k * 3 * U + 2 * U : (k + 1) * 3 * U] for k in range(4)]
    x1 = solve_back(factor, ups, jnp.where(even, y_mine[...], factor[2 * PANEL :]), above)
    x1_out[...] = x1
    for l, value in enumerate([x1] + above):
        pair = first_hots[...] if l == 0 else hots[:, (l - 1) * 3 * U : (l - 1) * 3 * U + 2 * U]
        pair = jnp.where(even, pair[:, U:], pair[:, 0:U])
        rows_send[:, l * U : (l + 1) * U] = dot(value, pair).astype(BF)


def level_one_rest(place, x1_ref, x, first_hots, hots, rows_keep, sep_keep, sep_send, sep_a, sep_b, sems):
    even = place[1] % 2 == 0
    x1 = x1_ref[...]
    above = [x[:, k * PANEL : (k + 1) * PANEL] for k in range(4)]
    level = jnp.where(place[1] < 2, 2, place[3])
    held = jnp.where(level == 0, jnp.zeros_like(x1), above[0])
    for k in (1, 2, 3):
        held = jnp.where(level == k + 2, above[k], held)
    sep_a[...] = jnp.where(even, x1, held)
    sep_b[...] = jnp.where(even, held, x1)
    stores = [
        pltpu.make_async_copy(sep_a, sep_keep, sems.at[0]),
        pltpu.make_async_copy(sep_b, sep_send, sems.at[1]),
    ]
    for store in stores:
        store.start()
    for l, value in enumerate([x1] + above):
        pair = first_hots[...] if l == 0 else hots[:, (l - 1) * 3 * U : (l - 1) * 3 * U + 2 * U]
        pair = jnp.where(even, pair[:, 0:U], pair[:, U:])
        rows_keep[:, l * U : (l + 1) * U] = dot(value, pair).astype(BF)
    for store in stores:
        store.wait()


def leaf_half(rows, inv, cpl, yt):
    back = (yt.astype(F32) - dot(rows[...], cpl[...].reshape(TERM, LEAF))).astype(BF)
    parts = []
    for i in range(4):
        start = i * 256
        parts.append(dot(back[:, start:], inv[start:, start : start + 256]).astype(BF))
    return jnp.concatenate(parts, axis=1)


def leaf_mine(place, keep, inv, cpl, yt, chosen, xt_out, picks_out):
    side = half_of(place)
    xt = leaf_half(keep, inv, cpl, yt[pl.ds(pl.multiple_of(side * 128, 128), 128)])
    xt_out[...] = xt
    picks_out[...] = dot_t(chosen[...], xt).astype(BF)


def leaf_other(place, recv, inv, cpl, yt, chosen, xt_mine, picks_mine, xt_out, picks_out, xt, picks, sems):
    side = half_of(place)
    mine = pl.ds(pl.multiple_of(side * 128, 128), 128)
    other = pl.ds(pl.multiple_of((1 - side) * 128, 128), 128)
    xt[mine] = xt_mine[...]
    picks[:, mine] = picks_mine[...]
    far = leaf_half(recv, inv, cpl, yt[other])
    xt[other] = far
    stores = [pltpu.make_async_copy(xt, xt_out, sems.at[0])]
    stores[0].start()
    for i in range(2):
        part = slice(i * 16 * SLOTS, (i + 1) * 16 * SLOTS)
        picks[part, other] = dot_t(chosen[part], far).astype(BF)
        stores.append(pltpu.make_async_copy(picks.at[part], picks_out.at[part], sems.at[1 + i]))
        stores[-1].start()
    for store in stores:
        store.wait()


def turn_leaf(xt, x_leaf, xt_v, sems):
    load = pltpu.make_async_copy(xt, xt_v, sems.at[0])
    load.start()
    load.wait()
    for i in range(4):
        part = slice(i * 256, (i + 1) * 256)
        x_leaf[part] = xt_v[:, part].astype(F32).T.astype(BF)


def turn_sep(place, keep, recv, x_sep, keep_v, recv_v, both, sems):
    loads = [
        pltpu.make_async_copy(keep, keep_v, sems.at[0]),
        pltpu.make_async_copy(recv, recv_v, sems.at[1]),
    ]
    for load in loads:
        load.start()
    for load in loads:
        load.wait()
    side = half_of(place)
    both[pl.ds(pl.multiple_of(side * 128, 128), 128)] = keep_v[...].astype(F32)
    both[pl.ds(pl.multiple_of((1 - side) * 128, 128), 128)] = recv_v[...].astype(F32)
    x_sep[...] = both[...].T.astype(BF)


def stretch_sum(weight, got, out, weight_v, sems):
    load = pltpu.make_async_copy(weight, weight_v, sems.at[0])
    load.start()
    load.wait()
    out[...] = dot(weight_v[0], got[...]) + dot(weight_v[1], got[...])


def iota(rows, cols, axis):
    return lax.broadcasted_iota(jnp.int32, (rows, cols), axis)


def ones_where(mask):
    return jnp.where(mask, 1.0, 0.0)


def stay_plan(place, dofs, coef, chosen, weight_out, grid, turned, dof_t, coef_t, weight, sems):
    me = place[2] * RING + place[1]
    grid[...] = jnp.full((128, 128), -1, jnp.int32)
    for r in range(16):
        grid[8 * r : 8 * r + 6] = dofs[:, 128 * r : 128 * (r + 1)]
    dof = grid[...]
    match = ones_where((dof >> 10) == me)
    row, col = iota(128, 128, 0), iota(128, 128, 1)
    same = (row >> 3) == (col >> 3)
    earlier = ((row >> 6) == (col >> 6)) & (row < col)
    match_b = match.astype(BF)
    count = dot(ones_where(same).astype(BF), match_b).astype(BF)
    rank = dot(count, ones_where(earlier).astype(BF))
    rank = rank + dot(ones_where(same & (col < row)).astype(BF), match_b)
    high = ((dof >> 5) & 31).astype(F32) + 1.0
    low = (dof & 31).astype(F32)
    rank = jnp.where(match > 0.0, rank, -1.0)
    parts = []
    for value in (high, low):
        for s in range(SLOTS):
            parts.append(jnp.where(rank == float(s), value, 0.0).astype(BF))
    block = ones_where(iota(16, 128, 0) == (iota(16, 128, 1) >> 3)).astype(BF)
    flat = dot(block, jnp.concatenate(parts, axis=1)).astype(BF)
    width = SLOTS * 128
    lane, q = iota(width, 32, 0), iota(width, 32, 1)
    gather = ones_where(q == ((lane >> 6) & 1) * SLOTS + (lane >> 7)).astype(BF)
    table_high = dot(flat[:, 0:width], gather).astype(BF)
    table_low = dot(flat[:, width:], gather).astype(BF)
    spread = ones_where((iota(512, 16, 0) >> 5) == iota(512, 16, 1)).astype(BF)
    here = ones_where((iota(512, 32, 0) & 31) == iota(512, 32, 1))
    sel_high = jnp.sum(dot(spread, table_high) * here, axis=1, keepdims=True)
    sel_low = jnp.sum(dot(spread, table_low) * here, axis=1, keepdims=True)
    sel = (sel_high - 1.0) * 32.0 + sel_low
    for part in range(4):
        at = slice(part * 128, (part + 1) * 128)
        chosen[at] = ones_where(iota(128, LEAF, 1).astype(F32) == sel[at]).astype(BF)

    block_row = pl.multiple_of((me >> 1) * 8, 8)
    block_col = pl.multiple_of((me >> 1) * 128, 128)
    half = pl.ds(pl.multiple_of((me & 1) * 64, 64), 64)
    turned[...] = jnp.zeros_like(turned)
    turned[0:8] = grid[pl.ds(block_row, 8)].astype(F32)
    dof_t[...] = turned[...].T
    turned[0:6] = coef[:, pl.ds(block_col, 128)]
    coef_t[...] = turned[...].T
    my_dof, my_coef = dof_t[half], coef_t[half]
    lanes = iota(64, 32, 1)
    source = [my_dof[:, k : k + 1].astype(jnp.int32) >> 10 for k in range(6)]
    named = [ones_where(source[k] == lanes) for k in range(6)]
    every = named[0]
    for k in range(1, 6):
        every = every + named[k]
    lower = ones_where(iota(64, 64, 1) < iota(64, 64, 0)).astype(BF)
    running = dot(lower, every.astype(BF))
    total = jnp.zeros((64, 512), F32)
    slots = iota(64, 512, 1).astype(F32)
    for k in range(6):
        at = jnp.sum(named[k] * running, axis=1, keepdims=True)
        slot = source[k].astype(F32) * float(SLOTS) + at
        total = total + jnp.where(slots == slot, my_coef[:, k : k + 1], 0.0)
        running = running + named[k]
    first = total.astype(BF)
    weight[0] = first
    weight[1] = (total - first.astype(F32)).astype(BF)
    store = pltpu.make_async_copy(weight, weight_out, sems.at[0])
    store.start()
    store.wait()


def after(value, *others):
    return lax.optimization_barrier((value, *others))[0]


def on_device(
    rhs_leaf, rhs_sep, leaf_inv, leaf_cpl, leaf_idx, sep_inv, sep_cpl, sep_idx, stay_dofs, stay_coef
):
    rows_axis, cols_axis = "rows", "cols"
    columns, rows = lax.axis_size(cols_axis), lax.axis_size(rows_axis)
    me = lax.axis_index(rows_axis)
    core = lax.axis_index(cols_axis) % 2
    y, z = me % RING, me // RING
    top_level = jnp.where(z % 2 == 0, 3, jnp.where(z % 4 == 1, 4, jnp.where(z == 3, 5, 0)))
    place = jnp.stack([core, y, z, top_level]).astype(jnp.int32)

    def route(value, target):
        pairs = []
        for c in range(columns):
            for r in range(rows):
                to = target(c % 2, r % RING, r // RING)
                if to is not None:
                    pairs.append((c * rows + r, (c - c % 2 + to[0]) * rows + to[2] * RING + to[1]))
        return lax.ppermute(value, (cols_axis, rows_axis), pairs)

    def swap_core(value):
        return route(value, lambda c, y, z: (1 - c, y, z))

    def swap(value, flip):
        return route(value, lambda c, y, z: (c, y ^ flip, z))

    def to_odd(value):
        return route(value, lambda c, y, z: (c, y + 1, z) if y % 2 == 0 else None)

    sep_rows_flat = sep_cpl.reshape(4 * U, PANEL)
    own_up, window = call(
        pack_factor,
        [pinned(packed_rows(3), PANEL), pinned(WINDOW, PANEL)],
        [place, sep_inv, sep_rows_flat, sep_idx],
        [SMEM, HBM, HBM, HBM],
        [pltpu.VMEM((16, PANEL), F32), pltpu.VMEM((LEVELS - 1, U), jnp.int32), dma(7)],
    )
    with jax.named_scope("factors_to_pair"):
        pair = route(window, lambda c, y, z: (c, y ^ 1, z) if y % 2 else None)
    with jax.named_scope("factors_to_other"):
        beside = route(window, lambda c, y, z: (c, y ^ 3, z) if y % 2 else None)
    yt, rhs, one, inv_v, cpl_v = call(
        leaf_first,
        [
            pinned(NC, LEAF),
            pinned(NC, PANEL),
            pinned(NC + 4 * 16, U),
            pinned(LEAF, LEAF),
            pinned(LEVELS, U, LEAF),
        ],
        [after(place, own_up), leaf_inv, rhs_leaf, leaf_cpl, rhs_sep, leaf_idx.transpose(1, 0, 2), sep_idx],
        [SMEM] + [HBM] * 6,
        [
            pltpu.VMEM((LEAF, NC), BF),
            pltpu.VMEM((PANEL, NC), BF),
            pltpu.VMEM((LEVELS, 1, U), jnp.int32),
            pltpu.VMEM((LEVELS - 1, U), jnp.int32),
            pltpu.VMEM((64, U), F32),
            dma(9),
        ],
    )
    with jax.named_scope("first_terms"):
        recv = swap(one, 1)
    (terms,) = call(
        leaf_second, [pinned(NC, PANEL)], [yt, cpl_v], [VMEM, VMEM]
    )

    def ready(slots, pick, sources):
        return call(
            functools.partial(stage, slots, pick, len(sources)),
            [pinned(factor_rows(slots), PANEL), pinned(PANEL, max(slots, 1) * U)],
            [place, *sources],
            [SMEM] + [ANY] * len(sources),
            [pltpu.VMEM((16, PANEL), BF), dma(8)],
        )

    def rise(level, panel, recv, factor, hots):
        slots = LEVELS - level
        return call(
            functools.partial(level_up, level),
            [pinned(64, PANEL), pinned(64, slots * PANEL)],
            [panel, recv, factor, hots],
            [VMEM] * 4,
        )

    (f1,) = call(
        load_first,
        [pinned(2 * PANEL + 128, PANEL)],
        [after(sep_inv, one), sep_rows_flat],
        [HBM, HBM],
        [dma(2)],
    )
    pair = after(pair, recv, f1, terms)
    with jax.named_scope("factors_across"):
        far = route(pair, lambda c, y, z: (c, y ^ 3, z) if y % 2 == 0 else None)
    first = after(recv, f1)
    first_hots, y1, passed, keep, send = call(
        level_one,
        [
            pinned(PANEL, ONE),
            pinned(128, PANEL),
            pinned(2 * PANEL + 128, PANEL),
            pinned(128, 2 * PANEL),
            pinned(128, 2 * PANEL),
        ],
        [place, one, first, terms, rhs, f1],
        [SMEM] + [VMEM] * 5,
        [pltpu.VMEM((NC, 2 * PANEL), BF)],
        aliases={5: 2},
    )
    with jax.named_scope("terms_pair"):
        recv = swap(send, 1)
    pair, beside = after((pair, beside), send)
    with jax.named_scope("pair_to_core"):
        pair_o = swap_core(pair)
    with jax.named_scope("beside_to_core"):
        beside_o = swap_core(beside)
    chosen, weight = call(
        stay_plan,
        [pinned(32 * SLOTS, LEAF), stored(2, 64, 512)],
        [place, stay_dofs, after(stay_coef, send)],
        [SMEM, VMEM, VMEM],
        [
            pltpu.VMEM((128, 128), jnp.int32),
            pltpu.VMEM((128, 128), F32),
            pltpu.VMEM((128, 128), F32),
            pltpu.VMEM((128, 128), F32),
            pltpu.VMEM((2, 64, 512), BF),
            dma(1),
        ],
        [VMEM, HBM],
    )
    (h1,) = call(
        stage_pair, [pinned(PANEL, PAIR_HOTS)], [place, one, after(first, send)], [SMEM, VMEM, VMEM]
    )
    recv = after(recv, chosen, h1)
    panel, send = call(
        join_pair,
        [pinned(64, 4 * PANEL), pinned(64, 4 * PANEL)],
        [place, keep, recv, h1],
        [SMEM] + [VMEM] * 3,
        [pltpu.VMEM((128, 4 * PANEL), BF)],
    )
    with jax.named_scope("panels_ring"):
        recv = swap(send, 3)
    far = after(far, send)
    with jax.named_scope("far_to_core"):
        far_o = swap_core(far)
    at = [own_up, pair, pair_o, beside, beside_o, far, far_o]
    f2, h2 = call(
        stage_two,
        [pinned(factor_rows(3), PANEL), pinned(PANEL, 3 * U)],
        [place, *at],
        [SMEM] + [ANY] * 7,
        [pltpu.VMEM((16, PANEL), BF), dma(8)],
    )
    f3, h3, top, triangle = call(
        stage_and_pass,
        [
            pinned(factor_rows(2), PANEL),
            pinned(PANEL, 2 * U),
            pinned(packed_rows(1), PANEL),
            pinned(TRI, PANEL),
        ],
        [place, *at],
        [SMEM] + [ANY] * 7,
        [pltpu.VMEM((16, PANEL), BF), dma(11)],
    )

    def next_up(value):
        return route(value, lambda c, y, z: (c, y, (z + (1 if c == z % 2 else -1)) % DEPTH))

    with jax.named_scope("factors_up"):
        up = next_up(top)
    with jax.named_scope("factor_top"):
        last = route(
            triangle,
            lambda c, y, z: (c, y, 0 if c else 6) if z == 3 else None,
        )
    with jax.named_scope("first_factor_to_odd"):
        passed_far = to_odd(after(passed, f2))
    recv = after(recv, f2, h2, f3, h3)
    y2, panel = rise(2, panel, recv, f2, h2)
    with jax.named_scope("panels_z1"):
        recv = route(panel, lambda c, y, z: (c, y, z - 1) if z % 2 else None)
    y3, panel = rise(3, panel, recv, f3, h3)
    with jax.named_scope("panels_z2"):
        recv = route(panel, lambda c, y, z: (c, y, z ^ 2))
    up, last = after((up, last), panel)
    with jax.named_scope("up_to_core"):
        up_o = swap_core(up)
    with jax.named_scope("last_to_core"):
        last_o = swap_core(last)
    f4, h4 = ready(1, pick_four, [up, up_o])
    f5, _ = ready(0, pick_five, [up, up_o, last, last_o])
    recv = after(recv, f4, h4, f5)
    y4, panel = rise(4, panel, recv, f4, h4)
    with jax.named_scope("panels_z3"):
        recv = route(panel, lambda c, y, z: (c, y, 8 - z if z % 2 else 6 - z))
    (x,) = call(
        turn,
        [pinned(64, 3 * PANEL)],
        [panel, recv, f3, f4, f5, h3, h4, y3, y4],
        [VMEM] * 9,
    )
    with jax.named_scope("down_z1"):
        recv = route(x, lambda c, y, z: (c, y, z ^ 1))
    (x,) = call(
        level_two_back,
        [pinned(64, 4 * PANEL)],
        [place, x, recv, f2, h2, y2],
        [SMEM] + [VMEM] * 5,
    )
    with jax.named_scope("down_ring"):
        recv = swap(x, 3)
    passed_far = after(passed_far, x)
    (f1,) = call(
        pick_first,
        [pinned(2 * PANEL + 128, PANEL)],
        [place, passed, passed_far],
        [SMEM, ANY, ANY],
        [dma(1)],
    )
    recv = after(recv, f1)
    x1, x, rows_send = call(
        level_one_back,
        [pinned(128, PANEL), pinned(128, 4 * PANEL), pinned(128, TERM)],
        [place, x, recv, y1, f1, first_hots, h1],
        [SMEM] + [VMEM] * 6,
    )
    with jax.named_scope("rows_back"):
        recv = swap(rows_send, 1)
    rows_keep, sep_keep, sep_send = call(
        level_one_rest,
        [pinned(128, TERM), stored(128, PANEL), stored(128, PANEL)],
        [place, x1, x, first_hots, h1],
        [SMEM] + [VMEM] * 4,
        [pltpu.VMEM((128, PANEL), BF), pltpu.VMEM((128, PANEL), BF), dma(2)],
        [VMEM, HBM, HBM],
    )
    xt_mine, picks_mine = call(
        leaf_mine,
        [pinned(128, LEAF), pinned(32 * SLOTS, 128)],
        [place, rows_keep, inv_v, cpl_v, yt, chosen],
        [SMEM] + [VMEM] * 5,
    )
    recv = after(recv, xt_mine)
    xt, picks = call(
        leaf_other,
        [stored(NC, LEAF), stored(32 * SLOTS, NC)],
        [place, recv, inv_v, cpl_v, yt, chosen, xt_mine, picks_mine],
        [SMEM] + [VMEM] * 7,
        [pltpu.VMEM((NC, LEAF), BF), pltpu.VMEM((32 * SLOTS, NC), BF), dma(3)],
        [HBM, HBM],
        moved=14 * 10**6,
    )
    with jax.named_scope("sep_back"):
        sep_recv = swap(after(sep_send, picks), 1)
    got = lax.all_to_all(
        picks.reshape(32, SLOTS, NC), rows_axis, 0, 0, tiled=True
    ).reshape(32 * SLOTS, NC)
    (x_leaf,) = call(
        turn_leaf, [plain(LEAF, NC)], [xt], [HBM], [pltpu.VMEM((NC, LEAF), BF), dma(1)]
    )
    (x_sep,) = call(
        turn_sep,
        [plain(PANEL, NC)],
        [place, sep_keep, sep_recv],
        [SMEM, HBM, HBM],
        [
            pltpu.VMEM((128, PANEL), BF),
            pltpu.VMEM((128, PANEL), BF),
            pltpu.VMEM((NC, PANEL), F32),
            dma(2),
        ],
    )
    (stretch,) = call(
        stretch_sum,
        [plain(64, NC, dtype=F32)],
        [weight, got],
        [HBM, VMEM],
        [pltpu.VMEM((2, 64, 512), BF), dma(1)],
    )
    return (x_leaf, x_sep, stretch)


def solution(mesh):
    return jax.shard_map(
        on_device,
        mesh=mesh,
        in_specs=(
            P("rows", "cols"),
            P("rows", "cols"),
            P("rows", None),
            P("rows", None, None, None),
            P("rows", None, None),
            P("rows", None),
            P("rows", None, None, None),
            P("rows", None, None),
            P(),
            P(),
        ),
        out_specs=(P("rows", "cols"), P("rows", "cols"), P("rows", "cols")),
        check_vma=False,
    )
```
